128 devices in a mesh: dp: 4 (over z_lo, core), ctx: 32 (over y, z_hi, x).
Axes of the slice: x: 4, y: 4, z: 4 (z_hi: 2, z_lo: 2; z = z_hi * 2 + z_lo), core: 2. Of those that a mesh axis runs over, the one named last changes fastest.
Arguments:
- tokens: bfloat16 [4, 2048, 2, 1536], P('dp', 'ctx'), may hold values from -6 to 6
- cotangent: bfloat16 [4, 2048, 2, 1536], P('dp', 'ctx'), may hold values from -6 to 6
- w_qkv: bfloat16 [1536, 2048], P(('dp', 'ctx')), may hold values from -0.15625 to 0.15625
- b_qkv: bfloat16 [2048], replicated, may hold values from -3 to 3
- w_out: bfloat16 [1536, 1536], P(('dp', 'ctx')), may hold values from -0.625 to 0.625
- w_gu: bfloat16 [1536, 2, 8960], P(('dp', 'ctx')), may hold values from -0.15625 to 0.15625
- w_down: bfloat16 [8960, 1536], P(('dp', 'ctx')), may hold values from -0.0625 to 0.0625
- gain_attn: bfloat16 [1536], replicated, may hold values from 0.099609375 to 1.8984375
- gain_mlp: bfloat16 [1536], replicated, may hold values from 0.099609375 to 1.8984375
- adapt_in: bfloat16 [8, 6, 16, 1536], replicated, may hold values from -0.15625 to 0.15625
- adapt_in_ff: bfloat16 [8, 16, 8960], replicated, may hold values from -0.0625 to 0.0625
- adapt_out_qkv: bfloat16 [8, 16, 2048], replicated, may hold values from -0.75 to 0.75
- adapt_out_res: bfloat16 [8, 2, 16, 1536], replicated, may hold values from -0.75 to 0.75
- adapt_out_ff: bfloat16 [8, 2, 16, 8960], replicated, may hold values from -0.75 to 0.75
- doc_lengths: int32 [4, 8], P('dp'), may hold values from 1 to 2048, 4096 in all within a row
- adapter_index: int32 [4], P('dp'), may hold values from 0 to 7
- window: int32 [4], P('dp'), may hold values from 512 to 1024, as said below
Outputs:
- layer_out: bfloat16 [4, 2048, 2, 1536], P('dp', 'ctx')
- grad_tokens: bfloat16 [4, 2048, 2, 1536], P('dp', 'ctx')
- grad_adapt_in: float32 [8, 6, 16, 1536], replicated
- grad_adapt_in_ff: float32 [8, 16, 8960], replicated
- grad_adapt_out_qkv: float32 [8, 16, 2048], replicated
- grad_adapt_out_res: float32 [8, 2, 16, 1536], replicated
- grad_adapt_out_ff: float32 [8, 2, 16, 8960], replicated
The draws below stay inside these ranges and needn't reach their ends.
Inputs may be any that keep to these rules, and one draw needn't show every extreme that they name: `doc_lengths`: a sequence's document lengths sum to 4096, and one document of every sequence has exactly 2048 tokens. Some sequence has a window of exactly 1024.
All inputs are finite; a program needn't handle non-finite values.
Results may differ from the reference program's by a relative error of at most 0.029.
Values may be sent and summed in bfloat16 or wider, within the bound.
A program may use at most 448 MiB of HBM per device.

```python
import math
import jax
import jax.numpy as jnp
import numpy as np
from jax import lax

D = 1536
QUERY_HEADS = 12
VALUE_HEADS = 2
HEAD_SIZE = 128
FF = 8960
RANK = 16
ADAPT = 8
WINDOW_LIMIT = 1024
DOCS = 8
BLK = 64
HALF = 2048
SEQUENCE_TOKENS = 4096
SEQS = 4
QUERY_FEATURES = 1536
KEY_FEATURES = 256
QKVW = 2048
N_CTX = 32


def draw_window(key, part):
    key = jax.random.fold_in(key, 11)
    first_key, second_key = jax.random.split(key)
    values = jax.random.randint(first_key, (SEQS,), WINDOW_LIMIT // 2, WINDOW_LIMIT + 1)
    chosen = jax.random.randint(second_key, (), 0, SEQS)
    return jnp.where(jnp.arange(SEQS) == chosen, WINDOW_LIMIT, values).astype(jnp.int32)


def touch_ends(array, own_key, low, high):
    shape = array.shape
    place = [jax.random.randint(jax.random.fold_in(own_key, axis), (), 0, shape[axis]) for axis in range(len(shape))]
    array = array.at[tuple(place)].set(low)
    longest = shape.index(max(shape))
    place[longest] = (place[longest] + 1) % shape[longest]
    return array.at[tuple(place)].set(high)


def level_of(stream_key, extent, cuts, low, largest):
    factor_of, own = 1.0, jax.random.fold_in(stream_key, 6)
    for dim, parts in cuts:
        draws = jnp.exp(jax.random.uniform(jax.random.fold_in(own, dim), (parts,), jnp.float32, low / len(cuts), largest / len(cuts)))
        factor_of = factor_of * jnp.repeat(draws, extent[dim] // parts).reshape([-1 if axis == dim else 1 for axis in range(len(extent))])
    return factor_of


def length_profile(number_of, total, limit, skew):
    portions = [(1 << 20) // math.isqrt(grade ** skew) + 1 for grade in range(2, number_of + 1)]
    spare, given = total - limit - (number_of - 1), [1] * (number_of - 1)
    while spare > 0:
        movable = [i for i in range(number_of - 1) if given[i] < limit]
        mass, left = sum([portions[i] for i in movable]), spare
        for i in movable:
            extra = min(limit - given[i], max(1, left * portions[i] // mass), spare)
            given[i] = given[i] + extra
            spare = spare - extra
    return np.array([limit] + given)


def ragged_sizes(rng, amount, total, limit, slope):
    if amount == 2:
        one = jax.random.randint(rng, (), max(1, total - limit), min(limit, total - 1) + 1)
        return jnp.stack([one, total - one])
    tallies = jnp.asarray(length_profile(amount, total, limit, slope), jnp.int32)
    pairs = (amount - 1) // 2
    source_of, receiver = tallies[1:1 + 2 * pairs:2], tallies[2:2 + 2 * pairs:2]
    margin = jnp.minimum(source_of - 1, limit - receiver)
    shifted = jax.random.randint(jax.random.fold_in(rng, 1), (pairs,), 0, 1 << 20) % (margin + 1)
    tallies = tallies.at[1:1 + 2 * pairs:2].set(source_of - shifted).at[2:2 + 2 * pairs:2].set(receiver + shifted)
    return tallies[jax.random.permutation(jax.random.fold_in(rng, 2), amount)]


def centred(key, extent, spread, limit, cuts=(), kind=jnp.bfloat16):
    gain = level_of(key, extent, cuts, -0.22, 0.18) if cuts else 1.0
    values = jax.random.normal(key, extent, jnp.float32) * spread * gain
    return jnp.minimum(jnp.maximum(values, -limit), limit).astype(kind)


def setup_inputs(seed: int = 0) -> dict:
    key_of = jax.random.split(jax.random.key(seed), 18)
    tokens = centred(key_of[0], (SEQS, HALF, 2, D), 1.0, 6.0, ((0, 4), (1, 32)))
    cotangent = centred(key_of[1], (SEQS, HALF, 2, D), 1.0, 6.0, ((0, 4), (1, 32)))
    w_qkv = centred(key_of[2], (D, QKVW), D ** -0.5, 0.15625, ((0, 128),))
    b_qkv = centred(key_of[3], (QKVW,), 0.5, 3.0)
    w_out = centred(key_of[4], (QUERY_FEATURES, D), (D // 16) ** -0.5, 0.625, ((0, 128),))
    w_gu = centred(key_of[5], (D, 2, FF), D ** -0.5, 0.15625, ((0, 128),))
    w_down = centred(key_of[6], (FF, D), FF ** -0.5, 0.0625, ((0, 128),))
    gain_attn = jnp.clip(1.0 + 0.18 * jax.random.normal(key_of[7], (D,), jnp.float32), 0.099609375, 1.8984375).astype(jnp.bfloat16)
    gain_mlp = jnp.clip(1.0 + 0.18 * jax.random.normal(key_of[8], (D,), jnp.float32), 0.099609375, 1.8984375).astype(jnp.bfloat16)
    adapt_in = centred(key_of[9], (ADAPT, 6, RANK, D), D ** -0.5, 0.15625)
    adapt_in_ff = centred(key_of[10], (ADAPT, RANK, FF), FF ** -0.5, 0.0625)
    adapt_out_qkv = centred(key_of[11], (ADAPT, RANK, QKVW), (4 * RANK) ** -0.5, 0.75)
    adapt_out_res = centred(key_of[12], (ADAPT, 2, RANK, D), (4 * RANK) ** -0.5, 0.75)
    adapt_out_ff = centred(key_of[13], (ADAPT, 2, RANK, FF), (4 * RANK) ** -0.5, 0.75)
    doc_lengths = jax.vmap(lambda own: ragged_sizes(own, DOCS, SEQUENCE_TOKENS, SEQUENCE_TOKENS // 2, 2))(jax.random.split(key_of[14], SEQS)).reshape((SEQS, DOCS)).astype(jnp.int32)
    adapter_index = touch_ends(jax.random.randint(key_of[15], (SEQS,), 0, ADAPT), jax.random.fold_in(key_of[15], 1), 0, ADAPT - 1).astype(jnp.int32)
    window = draw_window(jax.random.fold_in(key_of[17], 71), 0)
    return dict(tokens=tokens, cotangent=cotangent, w_qkv=w_qkv, b_qkv=b_qkv, w_out=w_out, w_gu=w_gu, w_down=w_down, gain_attn=gain_attn, gain_mlp=gain_mlp, adapt_in=adapt_in, adapt_in_ff=adapt_in_ff, adapt_out_qkv=adapt_out_qkv, adapt_out_res=adapt_out_res, adapt_out_ff=adapt_out_ff, doc_lengths=doc_lengths, adapter_index=adapter_index, window=window)


rope_base = 1000000.0
norm_eps = 1e-06

@jax.custom_vjp
def adapter_lowered(v):
    return lax.optimization_barrier(v.astype(jnp.bfloat16)).astype(jnp.float32)

@jax.custom_vjp
def low_back(v):
    return v

def low_keep(v):
    return (adapter_lowered(v), None)

def low_pass(kept, grad):
    return (grad,)

def back_keep(v):
    return (v, None)

def back_low(kept, grad):
    return (adapter_lowered(grad),)
adapter_lowered.defvjp(low_keep, low_pass)
low_back.defvjp(back_keep, back_low)

def highest(left_side, right_side):
    return jnp.dot(left_side, right_side, precision=lax.Precision.HIGHEST)

def un_deal(dealt_rows):
    first_half = dealt_rows[:, 0]
    second = dealt_rows[:, 1].reshape((N_CTX, BLK) + dealt_rows.shape[2:])[::-1].reshape(first_half.shape)
    return jnp.concatenate([first_half, second], 0)

def deal(natural):
    first_half = natural[:HALF]
    second = natural[HALF:].reshape((N_CTX, BLK) + natural.shape[1:])[::-1].reshape(first_half.shape)
    return jnp.stack([first_half, second], 1)

def rms_norm(values, scaling):
    return values * lax.rsqrt(lax.optimization_barrier(jnp.mean(values * values, -1, keepdims=True)) + norm_eps) * scaling

def rotary_embedding(values, token_position):
    frequency = rope_base ** (-(2.0 * jnp.arange(HEAD_SIZE // 2, dtype=jnp.float32)) / HEAD_SIZE)
    angles = token_position.astype(jnp.float32)[:, None] * frequency[None, :]
    cosine = jnp.concatenate([jnp.cos(angles), jnp.cos(angles)], -1)[:, None, :]
    sine_part = jnp.concatenate([jnp.sin(angles), jnp.sin(angles)], -1)[:, None, :]
    halfway = HEAD_SIZE // 2
    turned = jnp.concatenate([-values[..., halfway:], values[..., :halfway]], -1)
    return values * cosine + turned * sine_part

def attention(query_rows, rows_of_keys, rows_of_values, doc_ids, window_len):
    rows_per_block = min(512, SEQUENCE_TOKENS)
    query_group_width = QUERY_HEADS // VALUE_HEADS
    score_scale = HEAD_SIZE ** (-0.5)
    padded_keys = jnp.concatenate([jnp.zeros((WINDOW_LIMIT, VALUE_HEADS, HEAD_SIZE), jnp.float32), rows_of_keys], 0)
    padded_values = jnp.concatenate([jnp.zeros((WINDOW_LIMIT, VALUE_HEADS, HEAD_SIZE), jnp.float32), rows_of_values], 0)
    doc_pad = jnp.concatenate([jnp.full((WINDOW_LIMIT,), -1, jnp.int32), doc_ids], 0)

    def one_block(start_offset):
        query_row_count = lax.dynamic_slice_in_dim(query_rows, start_offset, rows_per_block, 0).reshape(rows_per_block, VALUE_HEADS, query_group_width, HEAD_SIZE)
        near_keys = lax.dynamic_slice_in_dim(padded_keys, start_offset, WINDOW_LIMIT + rows_per_block, 0)
        near_values = lax.dynamic_slice_in_dim(padded_values, start_offset, WINDOW_LIMIT + rows_per_block, 0)
        near_docs = lax.dynamic_slice_in_dim(doc_pad, start_offset, WINDOW_LIMIT + rows_per_block, 0)
        query_docs = lax.dynamic_slice_in_dim(doc_ids, start_offset, rows_per_block, 0)
        query_pos = start_offset + jnp.arange(rows_per_block, dtype=jnp.int32)
        key_pos = start_offset - WINDOW_LIMIT + jnp.arange(WINDOW_LIMIT + rows_per_block, dtype=jnp.int32)
        distance = query_pos[:, None] - key_pos[None, :]
        allowed = (distance >= 0) & (distance < window_len) & (query_docs[:, None] == near_docs[None, :])
        scores = jnp.einsum('qagd,kad->agqk', query_row_count, near_keys, precision=lax.Precision.HIGHEST) * score_scale
        scores = low_back(scores)
        scores = jnp.where(allowed[None, None], scores, -1e+30)
        weights = jax.nn.softmax(scores, axis=-1)
        mixed_heads = jnp.einsum('agqk,kad->qagd', adapter_lowered(weights), near_values, precision=lax.Precision.HIGHEST)
        return mixed_heads.reshape(rows_per_block, QUERY_HEADS, HEAD_SIZE)
    starts = jnp.arange(SEQUENCE_TOKENS // rows_per_block, dtype=jnp.int32) * rows_per_block
    return lax.map(jax.checkpoint(one_block), starts).reshape(SEQUENCE_TOKENS, QUERY_HEADS, HEAD_SIZE)

def layer(tokens_f, adapt_in_f, adapt_in_ff_f, adapt_out_qkv_f, adapt_out_res_f, adapt_out_ff_f, frozen, chosen, window_len, doc_ids):
    w_qkv, b_qkv, w_out, w_gu, w_down, gain_attn, gain_mlp = frozen
    adapter_in = adapt_in_f[chosen]
    adapter_ff = adapt_in_ff_f[chosen]
    out_qkv = adapt_out_qkv_f[chosen]
    out_res = adapt_out_res_f[chosen]
    out_ff = adapt_out_ff_f[chosen]
    token_position = jnp.arange(SEQUENCE_TOKENS, dtype=jnp.int32)
    normed = adapter_lowered(rms_norm(tokens_f, gain_attn))
    low_rank = jnp.einsum('td,krd->tkr', normed, adapter_in[:3], precision=lax.Precision.HIGHEST)
    adapter_terms = jnp.concatenate([highest(low_rank[:, 0], out_qkv[:, :QUERY_FEATURES]), highest(low_rank[:, 1], out_qkv[:, QUERY_FEATURES:QUERY_FEATURES + KEY_FEATURES]), highest(low_rank[:, 2], out_qkv[:, QUERY_FEATURES + KEY_FEATURES:])], 1)
    joined_heads = low_back(highest(normed, w_qkv) + b_qkv + adapter_terms)
    query_rows = adapter_lowered(rotary_embedding(joined_heads[:, :QUERY_FEATURES].reshape(SEQUENCE_TOKENS, QUERY_HEADS, HEAD_SIZE), token_position))
    rows_of_keys = adapter_lowered(rotary_embedding(joined_heads[:, QUERY_FEATURES:QUERY_FEATURES + KEY_FEATURES].reshape(SEQUENCE_TOKENS, VALUE_HEADS, HEAD_SIZE), token_position))
    rows_of_values = adapter_lowered(joined_heads[:, QUERY_FEATURES + KEY_FEATURES:].reshape(SEQUENCE_TOKENS, VALUE_HEADS, HEAD_SIZE))
    attended = attention(query_rows, rows_of_keys, rows_of_values, doc_ids, window_len).reshape(SEQUENCE_TOKENS, QUERY_FEATURES)
    mixed_heads = adapter_lowered(low_back(attended))
    out_rank = highest(mixed_heads, adapter_in[3].T)
    branch = low_back(highest(mixed_heads, w_out) + highest(out_rank, out_res[0]))
    hidden = tokens_f + branch
    normed_mlp = adapter_lowered(rms_norm(hidden, gain_mlp))
    mlp_rank = jnp.einsum('td,krd->tkr', normed_mlp, adapter_in[4:], precision=lax.Precision.HIGHEST)
    gate_up = low_back(jnp.einsum('td,dsf->tsf', normed_mlp, w_gu, precision=lax.Precision.HIGHEST) + jnp.einsum('tkr,krf->tkf', mlp_rank, out_ff, precision=lax.Precision.HIGHEST))
    active = adapter_lowered(jax.nn.silu(gate_up[:, 0]) * gate_up[:, 1])
    down_rank = highest(active, adapter_ff.T)
    result = low_back(highest(active, w_down) + highest(down_rank, out_res[1]))
    return hidden + result

def reference(tokens, cotangent, w_qkv, b_qkv, w_out, w_gu, w_down, gain_attn, gain_mlp, adapt_in, adapt_in_ff, adapt_out_qkv, adapt_out_res, adapt_out_ff, doc_lengths, adapter_index, window):
    frozen = tuple((source.astype(jnp.float32) for source in (w_qkv, b_qkv, w_out, w_gu, w_down, gain_attn, gain_mlp)))
    adapters = tuple((source.astype(jnp.float32) for source in (adapt_in, adapt_in_ff, adapt_out_qkv, adapt_out_res, adapt_out_ff)))

    def one_sequence(totals, inputs):
        seq_tokens, seq_cot, lengths, chosen, window_len = inputs
        doc_ends = jnp.cumsum(lengths)
        places = jnp.arange(SEQUENCE_TOKENS, dtype=jnp.int32)
        doc_ids = lax.optimization_barrier(jnp.sum((places[:, None] >= doc_ends[None, :]).astype(jnp.int32), 1)).astype(jnp.int32)

        def forward(tokens_f, first_in, second_in, first_out, second_out, third_out):
            return layer(tokens_f, first_in, second_in, first_out, second_out, third_out, frozen, chosen, window_len, doc_ids)
        output, pullback = jax.vjp(forward, un_deal(seq_tokens.astype(jnp.float32)), *adapters)
        grads = pullback(un_deal(seq_cot.astype(jnp.float32)))
        totals = tuple((running + update for running, update in zip(totals, grads[1:])))
        return (totals, (deal(output).astype(jnp.bfloat16), deal(grads[0]).astype(jnp.bfloat16)))
    starting = tuple((jnp.zeros(source.shape, jnp.float32) for source in adapters))
    totals, (layer_out, grad_tokens) = lax.scan(one_sequence, starting, (tokens, cotangent, doc_lengths, adapter_index, window))
    return (layer_out, grad_tokens, totals[0], totals[1], totals[2], totals[3], totals[4])
```

```python
import functools

import jax
import jax.numpy as jnp
from jax import lax
from jax.experimental import pallas as pl
from jax.experimental.pallas import tpu as pltpu
from jax.sharding import PartitionSpec as P

D = 1536
HEADS = 12
KV_HEADS = 2
HS = 128
GROUP = HEADS // KV_HEADS
FF = 8960
R = 16
ADAPT = 8
BLK = 64
ROWS = 2 * BLK
N_CTX = 32
NBLK = 2 * N_CTX
WIN = 1024
NWB = WIN // BLK + 1
KEYS = NWB * BLK
EXT = 128
DX = D + EXT
FW = 1280
FV = FF // 8
QW = HEADS * HS
KW = KV_HEADS * HS
SCALE = HS**-0.5
EPS = 1e-6

MESH = pl.DeviceIdType.MESH
BF = jnp.bfloat16
F32 = jnp.float32
ANY = pl.BlockSpec(memory_space=pl.ANY)
VM = pl.BlockSpec(memory_space=pltpu.VMEM)
SM = pl.BlockSpec(memory_space=pltpu.SMEM)
DMA = pltpu.SemaphoreType.DMA
VMEM_LIMIT = 60 * 2**20


def sds(shape, dtype):
    return jax.ShapeDtypeStruct(shape, dtype)


def nt(a, b):
    return lax.dot_general(a, b, (((1,), (1,)), ((), ())), preferred_element_type=F32)


def tn(a, b):
    return lax.dot_general(a, b, (((0,), (0,)), ((), ())), preferred_element_type=F32)


def mm(a, b):
    return jnp.dot(a, b, preferred_element_type=F32)


def iota(shape, dim):
    return lax.broadcasted_iota(jnp.int32, shape, dim)


class Place:
    def __init__(self):
        dp, ctx = lax.axis_index("dp"), lax.axis_index("ctx")
        self.dp, self.ctx = dp, ctx
        self.zlo, self.core = lax.div(dp, 2), lax.rem(dp, 2)
        self.y, self.zhi, self.x = lax.div(ctx, 8), lax.rem(lax.div(ctx, 4), 2), lax.rem(ctx, 4)
        self.z = self.zhi * 2 + self.zlo
        self.slice = 2 * dp + self.zhi

    def at(self, x=None, y=None, z=None, core=None):
        x = self.x if x is None else x
        y = self.y if y is None else y
        z = self.z if z is None else z
        core = self.core if core is None else core
        return (lax.rem(z, 2) * 2 + core, y * 8 + lax.div(z, 2) * 4 + x)

    def step(self, axis, by):
        return lax.rem(getattr(self, axis) + by, 4)

    def ring(self, axis):
        return [self.at(**{axis: self.step(axis, k)}) for k in (1, 2, 3)]

    def sibling(self):
        return self.at(core=1 - self.core)


def window_tile(piece):
    return jnp.minimum(lax.div(35 * piece, 4), 60)


def remote(src, dst, send, recv, device):
    return pltpu.make_async_remote_copy(
        src_ref=src, dst_ref=dst, send_sem=send, recv_sem=recv, device_id=device, device_id_type=MESH
    )


def greet(peers):
    sem = pltpu.get_barrier_semaphore()
    for device in peers:
        pl.semaphore_signal(sem, inc=1, device_id=device, device_id_type=MESH)
    pl.semaphore_wait(sem, len(peers))


class Ring:
    def __init__(self, me, axis, own, view, send, recv):
        self.i = getattr(me, axis)
        self.r, self.o, self.l = (me.step(axis, k) for k in (1, 2, 3))
        self.right, self.left = me.at(**{axis: self.r}), me.at(**{axis: self.l})
        self.own, self.view, self.send, self.recv = own, view, send, recv

    def copy(self, k, src, dst, device):
        return remote(src, dst, self.send.at[k], self.recv.at[k], device)

    def first(self):
        place = self.view(self.i, None)
        self.out = [self.copy(0, self.own, place, self.right), self.copy(1, self.own, place, self.left)]
        for c in self.out:
            c.start()

    def second(self):
        v = self.view
        self.copy(0, v(self.l, None), v(self.l, None), self.right).wait_recv()
        c = self.copy(2, v(self.l, 0), v(self.l, 0), self.right)
        c.start()
        self.out.append(c)
        self.copy(1, v(self.r, None), v(self.r, None), self.left).wait_recv()
        c = self.copy(3, v(self.r, 1), v(self.r, 1), self.left)
        c.start()
        self.out.append(c)

    def last(self):
        v = self.view
        self.copy(2, v(self.o, 0), v(self.o, 0), self.right).wait_recv()
        self.copy(3, v(self.o, 1), v(self.o, 1), self.left).wait_recv()

    def sent(self):
        for c in self.out:
            c.wait_send()


class ZGather:
    def __init__(self, me, own, buf, send, recv, core_send, core_recv, half):
        self.me, self.own, self.buf = me, own, buf
        self.cs, self.cr = core_send, core_recv

        def view(j, h, core=me.core):
            ref = buf.at[lax.rem(j, 2), core, lax.div(j, 2)]
            return ref if h is None else ref.at[pl.ds(h * half, half)]

        self.view = view
        self.ring = Ring(me, "z", own, view, send, recv)
        self.out = []

    def swap(self, src, j):
        c = remote(src, self.view(j, None), self.cs.at[len(self.out)], self.cr.at[len(self.out)], self.me.sibling())
        c.start()
        self.out.append((c, j))

    def first(self):
        self.ring.first()
        self.swap(self.own, self.me.z)

    def second(self):
        self.ring.second()
        self.swap(self.view(self.ring.l, None), self.ring.l)
        self.swap(self.view(self.ring.r, None), self.ring.r)

    def last(self):
        self.ring.last()
        self.swap(self.view(self.ring.o, None), self.ring.o)

    def finish(self):
        self.ring.sent()
        for k, (c, j) in enumerate(self.out):
            c.wait_send()
            place = self.view(j, None, 1 - self.me.core)
            remote(place, place, self.cs.at[k], self.cr.at[k], self.me.sibling()).wait_recv()


def rms(z):
    return lax.rsqrt(jnp.mean(z * z, -1, keepdims=True) + EPS)


def prepare_kernel(idx, tok, cot, a_in, b_qkv_ad, b_res, gain, bias, x_o, n1_o, e_o, ub_o, a45_o, bd_o):
    s = lax.axis_index("dp")
    x = tok[...].astype(F32)
    x_o[...] = tok[...]
    n1 = (x * rms(x) * gain[...].astype(F32)).astype(BF)
    n1_o[...] = n1
    for m, (lo, hi) in enumerate(((0, QW), (QW, QW + KW), (QW + KW, QW + 2 * KW))):
        u = nt(n1, a_in[0, m]).astype(BF)
        ub_o[:, lo:hi] = mm(u, b_qkv_ad[0, :, lo:hi]) + bias[:, lo:hi].astype(F32)
    at = pl.multiple_of(s * R, R)
    a45_o[...] = jnp.zeros_like(a45_o)
    a45_o[pl.ds(at, R), :] = a_in[0, 4]
    a45_o[pl.ds(at + 64, R), :] = a_in[0, 5]
    bd_o[...] = jnp.zeros_like(bd_o)
    bd_o[pl.ds(at, R), :] = b_res[0, 1]
    e_o[:, :D] = cot[...]
    e_o[:, D:] = nt(cot[...], bd_o[...]).astype(BF)


def pick(shape):
    return pl.BlockSpec((1,) + shape[1:], lambda i, idx: (idx[0],) + (0,) * (len(shape) - 1))


def whole(shape):
    return pl.BlockSpec(shape, lambda i, idx: (0,) * len(shape))


def prepare(idx, tok, cot, a_in, b_qkv_ad, b_res, gain, bias):
    outs = (
        sds((ROWS, D), BF),
        sds((ROWS, D), BF),
        sds((ROWS, DX), BF),
        sds((ROWS, 2048), F32),
        sds((EXT, D), BF),
        sds((EXT, D), BF),
    )
    return pl.pallas_call(
        prepare_kernel,
        out_shape=outs,
        grid_spec=pltpu.PrefetchScalarGridSpec(
            num_scalar_prefetch=1,
            grid=(1,),
            in_specs=[
                whole((ROWS, D)),
                whole((ROWS, D)),
                pick(a_in.shape),
                pick(b_qkv_ad.shape),
                pick(b_res.shape),
                whole((1, D)),
                whole((1, 2048)),
            ],
            out_specs=[whole(o.shape) for o in outs],
        ),
        compiler_params=pltpu.CompilerParams(vmem_limit_bytes=VMEM_LIMIT),
    )(idx, tok, cot, a_in, b_qkv_ad, b_res, gain, bias)


def weights_kernel(
    idx, wq, wo, wg, wd, eext,
    oq, oo, og, od, oe, oi,
    rq, ro, rg, cq, co, cg,
    ss, rs, ls, s1, r1, s2, r2, sc, rc_, sd, rd, se, re_, ce, cre, si, ri,
):
    me = Place()
    sib = me.sibling()
    zpeers = [
        me.at(z=me.step("z", dz), core=lax.rem(me.core + dc, 2)) for dz in range(4) for dc in range(2) if dz or dc
    ]
    m = me.ctx
    bar = pltpu.get_barrier_semaphore()

    def hello(t, carry):
        @pl.when(t != m)
        def _():
            pl.semaphore_signal(bar, inc=1, device_id=(me.dp, t), device_id_type=MESH)

        return carry

    lax.fori_loop(0, N_CTX, hello, 0)
    others = [
        me.at(z=me.step("z", dz), core=lax.rem(me.core + dc, 2)) for dz in range(4) for dc in range(2) if dz % 2 or dc
    ]
    for d in others:
        pl.semaphore_signal(bar, inc=1, device_id=d, device_id_type=MESH)
    pl.semaphore_wait(bar, N_CTX - 1 + len(others))

    first = []
    for k in (1, 2, 3):
        t = me.step("x", k)
        d = me.at(x=t)
        for n, (src, dst) in enumerate(((wq, rq.at[me.x]), (wo, ro.at[me.x]))):
            first.append(remote(src, dst, s1.at[k - 1, n], r1.at[k - 1, n], d))
        for g in range(8):
            tile = 60 if g == 7 else 35 * g // 4
            col = pl.multiple_of(tile * 128 + lax.rem(t, 2) * 640, 128)
            src = wg.at[lax.div(t, 2), :, pl.ds(col, 640)]
            first.append(remote(src, rg.at[me.x, g], s1.at[k - 1, 2 + g], r1.at[k - 1, 2 + g], d))
    for c in first:
        c.start()
    mine = [
        pltpu.make_async_copy(wq, rq.at[me.x], ls.at[0]),
        pltpu.make_async_copy(wo, ro.at[me.x], ls.at[1]),
    ]
    for g in range(8):
        tile = 60 if g == 7 else 35 * g // 4
        col = pl.multiple_of(tile * 128 + lax.rem(me.x, 2) * 640, 128)
        mine.append(
            pltpu.make_async_copy(wg.at[lax.div(me.x, 2), :, pl.ds(col, 640)], rg.at[me.x, g], ls.at[2 + g])
        )
    for c in mine:
        c.start()
    ez = ZGather(me, eext, oe, se, re_, ce, cre, BLK)
    ez.first()
    own_e = pltpu.make_async_copy(eext, oe.at[me.zlo, me.core, me.zhi], ls.at[10])
    own_e.start()
    own_i = pltpu.make_async_copy(idx, oi.at[me.dp, me.zhi], ls.at[11])
    own_i.start()
    ic = []
    for n, d in enumerate(zpeers):
        c = remote(idx, oi.at[me.dp, me.zhi], si.at[n], ri.at[n], d)
        c.start()
        ic.append(c)

    for c in mine:
        c.wait()
    for k in (1, 2, 3):
        f = me.step("x", 4 - k)
        d = me.at(x=f)
        for n, ref in enumerate((rq.at[f], ro.at[f])):
            remote(ref, ref, s1.at[k - 1, n], r1.at[k - 1, n], d).wait_recv()
        for g in range(8):
            ref = rg.at[f, g]
            remote(ref, ref, s1.at[k - 1, 2 + g], r1.at[k - 1, 2 + g], d).wait_recv()
    row, col = iota((48, 64), 0), iota((48, 64), 1)
    put = jnp.where(
        (lax.rem(col, 16) < 12) & (lax.div(col, 16) * 12 + lax.rem(col, 16) == row), 1.0, 0.0
    ).astype(BF)
    cq[...] = mm(put, rq[...].reshape(64, 2048)).astype(BF)
    co[...] = mm(put, ro[...].reshape(64, D)).astype(BF)

    def vy0(j, h):
        ref = oq.at[me.zlo, me.core, j, me.zhi]
        return ref if h is None else ref.at[:, pl.ds(1024 * h, 1024)]

    def vz0(j, h, core=me.core):
        zl, zh = lax.rem(j, 2), lax.div(j, 2)
        return oq.at[zl, core, :, zh] if h is None else oq.at[zl, core, pl.ds(2 * h, 2), zh]

    def vz1(j, h):
        ref = oo.at[lax.rem(j, 2), me.core, me.y, lax.div(j, 2)]
        return ref if h is None else ref.at[:, pl.ds(768 * h, 768)]

    def vy1(j, h, core=me.core):
        return oo.at[:, core, j] if h is None else oo.at[h, core, j]

    ra = Ring(me, "y", cq, vy0, ss.at[0], rs.at[0])
    rb = Ring(me, "z", co, vz1, ss.at[1], rs.at[1])
    ra.first()
    rb.first()
    own = [
        pltpu.make_async_copy(cq, oq.at[me.zlo, me.core, me.y, me.zhi], ls.at[12]),
        pltpu.make_async_copy(co, oo.at[me.zlo, me.core, me.y, me.zhi], ls.at[13]),
    ]
    for c in own:
        c.start()
    for g in range(8):
        cg[g] = mm(put, rg[:, g].reshape(64, 640)).astype(BF)
    own_g = pltpu.make_async_copy(
        cg.at[me.slice], og.at[me.x, me.zlo, me.core, me.y, me.zhi], ls.at[14]
    )
    own_g.start()
    zc = []
    zk = [(dz, dc) for dz in range(4) for dc in range(2) if dz or dc]
    for n, (dz, dc) in enumerate(zk):
        z, core = me.step("z", dz), lax.rem(me.core + dc, 2)
        piece = 2 * (2 * lax.rem(z, 2) + core) + lax.div(z, 2)
        c = remote(
            cg.at[piece], og.at[me.x, me.zlo, me.core, me.y, me.zhi], s2.at[n], r2.at[n], me.at(z=z, core=core)
        )
        c.start()
        zc.append(c)
    zr = lax.div(me.y, 2)
    slot = lax.rem(me.y, 2) * 8 + me.zhi * 4 + me.x

    def down(k, wait):
        t = lax.rem(m + k, N_CTX)

        @pl.when(lax.rem(lax.div(t, 4), 2) == zr)
        def _():
            c = remote(wd, od.at[slot], sd.at[k], rd.at[slot], (me.dp, t))
            if wait:
                c.wait_send()
            else:
                c.start()

    def down_send(k, carry):
        down(k, False)
        return carry

    def down_sent(k, carry):
        down(k, True)
        return carry

    lax.fori_loop(1, N_CTX, down_send, 0)

    @pl.when(me.zhi == zr)
    def _():
        c = pltpu.make_async_copy(wd, od.at[slot], ls.at[15])
        c.start()
        c.wait()

    ra.second()
    rb.second()
    ez.second()
    ra.last()
    rb.last()
    for c in own:
        c.wait()
    ra2 = Ring(me, "z", vz0(me.z, None), vz0, ss.at[2], rs.at[2])
    rb2 = Ring(me, "y", vy1(me.y, None), vy1, ss.at[3], rs.at[3])
    ra2.first()
    rb2.first()
    swaps = []

    def swap(view, j):
        n = len(swaps)
        c = remote(view(j, None), view(j, None), sc.at[n], rc_.at[n], sib)
        c.start()
        swaps.append((c, view, j))

    swap(vz0, me.z)
    swap(vy1, me.y)

    own_g.wait()
    for n, (dz, dc) in enumerate(zk):
        z, core = me.step("z", 4 - dz if dz else 0), lax.rem(me.core + dc, 2)
        ref = og.at[me.x, lax.rem(z, 2), core, me.y, lax.div(z, 2)]
        remote(ref, ref, s2.at[n], r2.at[n], me.at(z=z, core=core)).wait_recv()

    def g0a(j, h):
        return og.at[me.x, 0, :, j] if h is None else og.at[me.x, 0, h, j]

    def g0b(j, h):
        return og.at[j, 0] if h is None else og.at[j, 0, h]

    def g1a(j, h):
        return og.at[j, 1, :, me.y] if h is None else og.at[j, 1, h, me.y]

    def g1b(j, h):
        return og.at[:, 1, :, j] if h is None else og.at[:, 1, h, j]

    ga = Ring(me, "y", g0a(me.y, None), g0a, ss.at[4], rs.at[4])
    gb = Ring(me, "x", g1a(me.x, None), g1a, ss.at[5], rs.at[5])
    ga.first()
    gb.first()
    ra2.second()
    rb2.second()
    swap(vz0, ra2.l)
    swap(vy1, rb2.l)
    swap(vz0, ra2.r)
    swap(vy1, rb2.r)
    ga.second()
    gb.second()
    ga.last()
    gb.last()
    ga2 = Ring(me, "x", g0b(me.x, None), g0b, ss.at[6], rs.at[6])
    gb2 = Ring(me, "y", g1b(me.y, None), g1b, ss.at[7], rs.at[7])
    ga2.first()
    gb2.first()
    ra2.last()
    rb2.last()
    swap(vz0, ra2.o)
    swap(vy1, rb2.o)
    ez.last()
    ga2.second()
    gb2.second()
    ga2.last()
    gb2.last()

    for r in (ra, rb, ra2, rb2, ga, gb, ga2, gb2):
        r.sent()
    for c in first:
        c.wait_send()
    for c in zc:
        c.wait_send()
    for n, (c, view, j) in enumerate(swaps):
        c.wait_send()
        ref = view(j, None, 1 - me.core)
        remote(ref, ref, sc.at[n], rc_.at[n], sib).wait_recv()
    ez.finish()
    own_e.wait()
    own_i.wait()
    for n, (dz, dc) in enumerate(zk):
        z, core = me.step("z", 4 - dz if dz else 0), lax.rem(me.core + dc, 2)
        ic[n].wait_send()
        ref = oi.at[2 * lax.rem(z, 2) + core, lax.div(z, 2)]
        remote(ref, ref, si.at[n], ri.at[n], me.at(z=z, core=core)).wait_recv()
    lax.fori_loop(1, N_CTX, down_sent, 0)

    def down_got(n, carry):
        src = (2 * me.zhi + lax.div(n, 8)) * 8 + lax.rem(n, 8)

        @pl.when(src != m)
        def _():
            remote(wd, od.at[n], sd.at[0], rd.at[n], (me.dp, src)).wait_recv()

        return carry

    lax.fori_loop(0, 16, down_got, 0)


def weights(idx, wq, wo, wg, wd, eext):
    outs = (
        sds((2, 2, 4, 2, 48, 2048), BF),
        sds((2, 2, 4, 2, 48, D), BF),
        sds((4, 2, 2, 4, 2, 48, 640), BF),
        sds((16, 80, D), BF),
        sds((2, 2, 2, ROWS, DX), BF),
        sds((4, 2, 8, 128), jnp.int32),
    )
    scratch = [
        pltpu.VMEM((4, 16, 2048), BF),
        pltpu.VMEM((4, 16, D), BF),
        pltpu.VMEM((4, 8, 16, 640), BF),
        pltpu.VMEM((48, 2048), BF),
        pltpu.VMEM((48, D), BF),
        pltpu.VMEM((8, 48, 640), BF),
        DMA((8, 4)),
        DMA((8, 4)),
        DMA((16,)),
        DMA((3, 10)),
        DMA((3, 10)),
        DMA((7,)),
        DMA((7,)),
        DMA((8,)),
        DMA((8,)),
        DMA((N_CTX,)),
        DMA((16,)),
        DMA((4,)),
        DMA((4,)),
        DMA((4,)),
        DMA((4,)),
        DMA((7,)),
        DMA((7,)),
    ]
    return pl.pallas_call(
        weights_kernel,
        out_shape=outs,
        in_specs=[ANY] * 6,
        out_specs=[ANY] * 6,
        scratch_shapes=scratch,
        compiler_params=pltpu.CompilerParams(collective_id=1, has_side_effects=True, vmem_limit_bytes=VMEM_LIMIT),
    )(idx, wq, wo, wg, wd, eext)


def turn(v, cos, sin):
    return v * cos + pltpu.roll(v, 64, 1) * sin


def turn_back(v, cos, sin):
    return v * cos - pltpu.roll(v, 64, 1) * sin


def qkv_kernel(n1, w, ub, cos, sin, q_o, kv_o):
    c, s = cos[...], sin[...]
    for h in range(HEADS + 2 * KV_HEADS):
        cols = slice(h * HS, (h + 1) * HS)
        if h % 2 == 0:
            pair = slice(h * HS, (h + 2) * HS)
            j = mm(n1[...], w[:, pair]) + ub[:, pair]
        v = j[:, (h % 2) * HS : (h % 2 + 1) * HS]
        if h < HEADS + KV_HEADS:
            v = turn(v, c, s)
        v = v.astype(BF)
        if h < HEADS:
            q_o[:, cols] = v
        else:
            at = slice((h - HEADS) * HS, (h - HEADS + 1) * HS)
            kv_o[0, :, at] = v[:BLK]
            kv_o[1, :, at] = v[BLK:]


def qkv(n1, w, ub, cos, sin):
    return pl.pallas_call(
        qkv_kernel,
        out_shape=(sds((ROWS, D), BF), sds((2, BLK, 2 * KW), BF)),
        in_specs=[VM] * 5,
        out_specs=[VM] * 2,
        compiler_params=pltpu.CompilerParams(vmem_limit_bytes=VMEM_LIMIT),
    )(n1, w, ub, cos, sin)


def reads(t, block):
    a, b = t - block, NBLK - 1 - t - block
    return ((a >= 0) & (a < NWB)) | ((b >= 0) & (b < NWB))


def halo_kernel(own, out, zero, ss, rs, ls):
    me = Place()
    m = me.ctx
    bar = pltpu.get_barrier_semaphore()

    def hello(t, carry):
        @pl.when(t != m)
        def _():
            pl.semaphore_signal(bar, inc=1, device_id=(me.dp, t), device_id_type=MESH)

        return carry

    lax.fori_loop(0, N_CTX, hello, 0)
    zero[...] = jnp.zeros_like(zero)
    local = [
        pltpu.make_async_copy(own.at[0], out.at[16 + m], ls.at[0]),
        pltpu.make_async_copy(own.at[1], out.at[16 + NBLK - 1 - m], ls.at[1]),
        pltpu.make_async_copy(zero, out.at[pl.ds(0, 16)], ls.at[2]),
    ]
    for c in local:
        c.start()
    pl.semaphore_wait(bar, N_CTX - 1)

    def send(k, carry):
        t = lax.rem(m + k, N_CTX)
        for h in range(2):
            block = m if h == 0 else NBLK - 1 - m

            @pl.when(reads(t, block))
            def _():
                remote(own.at[h], out.at[16 + block], ss.at[h, k], rs.at[block], (me.dp, t)).start()

        return carry

    lax.fori_loop(1, N_CTX, send, 0)

    def wait(k, carry):
        t = lax.rem(m + k, N_CTX)
        for h in range(2):
            block = m if h == 0 else NBLK - 1 - m

            @pl.when(reads(t, block))
            def _():
                remote(own.at[h], out.at[16 + block], ss.at[h, k], rs.at[block], (me.dp, t)).wait_send()

            theirs = t if h == 0 else NBLK - 1 - t

            @pl.when(reads(m, theirs))
            def _():
                remote(own.at[h], out.at[16 + theirs], ss.at[h, k], rs.at[theirs], (me.dp, t)).wait_recv()

        return carry

    lax.fori_loop(1, N_CTX, wait, 0)
    for c in local:
        c.wait()


def halo(kv):
    return pl.pallas_call(
        halo_kernel,
        out_shape=sds((16 + NBLK, BLK, 2 * KW), BF),
        in_specs=[ANY],
        out_specs=ANY,
        scratch_shapes=[pltpu.VMEM((16, BLK, 2 * KW), BF), DMA((2, N_CTX)), DMA((NBLK,)), DMA((3,))],
        compiler_params=pltpu.CompilerParams(collective_id=2, has_side_effects=True, vmem_limit_bytes=VMEM_LIMIT),
    )(kv)


def load_windows(kv, win, sem):
    m = lax.axis_index("ctx")
    copies = [
        pltpu.make_async_copy(kv.at[pl.ds(m, NWB)], win.at[0], sem.at[0]),
        pltpu.make_async_copy(kv.at[pl.ds(NBLK - 1 - m, NWB)], win.at[1], sem.at[1]),
    ]
    for c in copies:
        c.start()
    return copies


def stack_heads(ref, h, a):
    rows = slice(h * BLK, (h + 1) * BLK)
    return jnp.concatenate(
        [ref[rows, (a * GROUP + g) * HS : (a * GROUP + g + 1) * HS] for g in range(GROUP)], 0
    )


def attend_kernel(idx, low, q, kv, x, w_out, a_in, b_res, gain, a45, p_o, o_o, h_o, n2_o, win, sem):
    m = lax.axis_index("ctx")
    copies = load_windows(kv, win, sem)
    for h in range(2):
        copies[h].wait()
        base = (m if h == 0 else NBLK - 1 - m) * BLK
        kpos = base - WIN + iota((BLK, KEYS), 1)
        qpos = base + iota((BLK, KEYS), 0)
        keep = (kpos <= qpos) & (kpos >= low[h * BLK : (h + 1) * BLK, :1])
        for a in range(KV_HEADS):
            qs = stack_heads(q, h, a)
            k = win[h, :, :, a * HS : (a + 1) * HS].reshape(KEYS, HS)
            v = win[h, :, :, KW + a * HS : KW + (a + 1) * HS].reshape(KEYS, HS)
            sc = nt(qs, k) * SCALE
            sc = jnp.where(keep[None], sc.reshape(GROUP, BLK, KEYS), -1e30)
            e = jnp.exp(sc - jnp.max(sc, -1, keepdims=True))
            p = (e / jnp.sum(e, -1, keepdims=True)).astype(BF).reshape(GROUP * BLK, KEYS)
            p_o[2 * h + a] = p
            o = mm(p, v).astype(BF)
            for g in range(GROUP):
                o_o[h * BLK : (h + 1) * BLK, (a * GROUP + g) * HS : (a * GROUP + g + 1) * HS] = o[
                    g * BLK : (g + 1) * BLK
                ]
    o = o_o[...]
    u3 = nt(o, a_in[0, 3]).astype(BF)
    hid = x[...].astype(F32) + mm(o, w_out[...]) + mm(u3, b_res[0, 0])
    h_o[...] = hid
    n2 = (hid * rms(hid) * gain[...].astype(F32)).astype(BF)
    n2_o[:, :D] = n2
    n2_o[:, D:] = nt(n2, a45[...]).astype(BF)


def attend(idx, low, q, kv, x, w_out, a_in, b_res, gain, a45):
    outs = (
        sds((4, GROUP * BLK, KEYS), BF),
        sds((ROWS, D), BF),
        sds((ROWS, D), F32),
        sds((ROWS, DX), BF),
    )
    return pl.pallas_call(
        attend_kernel,
        out_shape=outs,
        grid_spec=pltpu.PrefetchScalarGridSpec(
            num_scalar_prefetch=1,
            grid=(1,),
            in_specs=[
                whole(low.shape),
                whole(q.shape),
                ANY,
                whole(x.shape),
                whole(w_out.shape),
                pick(a_in.shape),
                pick(b_res.shape),
                whole((1, D)),
                whole(a45.shape),
            ],
            out_specs=[whole(o.shape) for o in outs],
            scratch_shapes=[pltpu.VMEM((2, NWB, BLK, 2 * KW), BF), DMA((2,))],
        ),
        compiler_params=pltpu.CompilerParams(vmem_limit_bytes=VMEM_LIMIT),
    )(idx, low, q, kv, x, w_out, a_in, b_res, gain, a45)


def gather_kernel(own, out, ss, rs, cs, cr, ls):
    me = Place()
    greet(me.ring("z") + [me.sibling()])
    c = pltpu.make_async_copy(own, out.at[me.zlo, me.core, me.zhi], ls.at[0])
    c.start()
    z = ZGather(me, own, out, ss, rs, cs, cr, BLK)
    z.first()
    z.second()
    z.last()
    z.finish()
    c.wait()


def gather(own):
    return pl.pallas_call(
        gather_kernel,
        out_shape=sds((2, 2, 2, ROWS, DX), BF),
        in_specs=[ANY],
        out_specs=ANY,
        scratch_shapes=[DMA((4,))] * 4 + [DMA((1,))],
        compiler_params=pltpu.CompilerParams(collective_id=3, has_side_effects=True, vmem_limit_bytes=VMEM_LIMIT),
    )(own)


def compact_kernel(wd, out):
    piece = 2 * lax.axis_index("dp") + lax.rem(lax.div(lax.axis_index("ctx"), 4), 2)
    o = FV * piece - 128 * window_tile(piece)
    for r in range(5):
        row = iota((256, 1280), 0) + 256 * r - o
        col = iota((256, 1280), 1)
        i, k = lax.div(col, 80), lax.rem(col, 80)
        put = jnp.where((k < 70) & (i * 70 + k == row), 1.0, 0.0).astype(BF)
        out[256 * r : 256 * (r + 1)] = mm(put, wd[...].reshape(1280, D)).astype(BF)


def compact(wd):
    return pl.pallas_call(
        compact_kernel,
        out_shape=sds((FW, D), BF),
        in_specs=[VM],
        out_specs=VM,
        compiler_params=pltpu.CompilerParams(vmem_limit_bytes=VMEM_LIMIT),
    )(wd)


FSTEPS = 4
FROWS = 8 * ROWS // FSTEPS


def feed_kernel(idx, x, e, og, wd, ad_all, b_all, y_o, g_o, tiles_o, wg, wu, ad, bg, bu, acc, sem):
    piece = 2 * lax.axis_index("dp") + lax.rem(lax.div(lax.axis_index("ctx"), 4), 2)
    tile = window_tile(piece)
    o = FV * piece - 128 * tile
    step = pl.program_id(0)

    @pl.when(step == 0)
    def _():
        cols = pl.ds(pl.multiple_of(tile * 128, 128), FW)
        copies = []
        for q in range(4):
            w = wg if q < 2 else wu
            copies.append(pltpu.make_async_copy(og.at[q], w.at[:, pl.ds(640 * (q % 2), 640)], sem.at[q]))
        for s in range(4):
            rows, rows2 = pl.ds(R * s, R), pl.ds(64 + R * s, R)
            copies.append(pltpu.make_async_copy(ad_all.at[idx[s], :, cols], ad.at[rows], sem.at[4 + s]))
            copies.append(pltpu.make_async_copy(b_all.at[idx[s], 0, :, cols], bg.at[rows], sem.at[8 + s]))
            copies.append(pltpu.make_async_copy(b_all.at[idx[s], 1, :, cols], bu.at[rows2], sem.at[12 + s]))
        for c in copies:
            c.start()
        ad[64:] = jnp.zeros((64, FW), BF)
        bg[64:] = jnp.zeros((64, FW), BF)
        bu[:64] = jnp.zeros((64, FW), BF)
        acc[...] = jnp.zeros_like(acc)
        for c in copies:
            c.wait()
        col = iota((64, FW), 1)
        ad[:64] = jnp.where((col >= o) & (col < o + FV), ad[:64], jnp.zeros((), BF))

    n2, u = x[:, :D], x[:, D:]
    eo, gud = e[:, :D], e[:, D:]
    gate = mm(n2, wg[...]) + mm(u, bg[...])
    up = mm(n2, wu[...]) + mm(u, bu[...])
    gm = nt(eo, wd[...]) + mm(gud, ad[...])
    sig = 1.0 / (1.0 + jnp.exp(-gate))
    sl = gate * sig
    act = (sl * up).astype(BF)
    gg = (gm * up * (sig * (1.0 + gate * (1.0 - sig)))).astype(BF)
    gu = (gm * sl).astype(BF)
    y_o[:, :D] = mm(act, wd[...]).astype(BF)
    y_o[:, D:] = nt(act, ad[...]).astype(BF)
    g_o[:, :D] = (nt(gg, wg[...]) + nt(gu, wu[...])).astype(BF)
    g_o[:, D:] = (nt(gg, bg[...]) + nt(gu, bu[...])).astype(BF)
    acc[0] += tn(gud, act)[:64]
    acc[1] += tn(u, gg)[:64]
    acc[2] += tn(u, gu)[64:]

    @pl.when(step == FSTEPS - 1)
    def _():
        col = iota((64, FW), 1)
        valid = (col >= o) & (col < o + FV)
        for k in range(3):
            v = jnp.where(valid, acc[k], 0.0).astype(BF)
            for s in range(4):
                for t in range(10):
                    tiles_o[s * 30 + k * 10 + t] = v[R * s : R * (s + 1), 128 * t : 128 * (t + 1)]
        for t in range(120, 128):
            tiles_o[t] = jnp.zeros((R, 128), BF)


def feed(idx, x, e, og, wd, ad_all, b_all):
    outs = (sds((8 * ROWS, DX), BF), sds((8 * ROWS, DX), BF), sds((128, R, 128), BF))
    rows = pl.BlockSpec((FROWS, DX), lambda i, idx: (i, 0))
    return pl.pallas_call(
        feed_kernel,
        out_shape=outs,
        grid_spec=pltpu.PrefetchScalarGridSpec(
            num_scalar_prefetch=1,
            grid=(FSTEPS,),
            in_specs=[rows, rows, ANY, whole((FW, D)), ANY, ANY],
            out_specs=[rows, rows, whole((128, R, 128))],
            scratch_shapes=[
                pltpu.VMEM((D, FW), BF),
                pltpu.VMEM((D, FW), BF),
                pltpu.VMEM((EXT, FW), BF),
                pltpu.VMEM((EXT, FW), BF),
                pltpu.VMEM((EXT, FW), BF),
                pltpu.VMEM((3, 64, FW), F32),
                DMA((16,)),
            ],
        ),
        compiler_params=pltpu.CompilerParams(vmem_limit_bytes=VMEM_LIMIT),
    )(idx, x, e, og, wd, ad_all, b_all)


def scatter_kernel(part, out, own, got, got2, red, ls, cs, cr, ss, rs):
    me = Place()
    sib = me.sibling()
    greet(me.ring("z") + [sib])
    sends, mine = [], []
    for j in range(4):
        z = me.step("z", j)
        zl, zh = lax.rem(z, 2), lax.div(z, 2)
        c = remote(part.at[zl, 1 - me.core, zh], got.at[j], cs.at[j], cr.at[j], sib)
        c.start()
        sends.append(c)
        c = pltpu.make_async_copy(part.at[zl, me.core, zh], own.at[j], ls.at[j])
        c.start()
        mine.append(c)
    outs = []
    for j in (2, 1, 3, 0):
        sends[j].wait_recv()
        mine[j].wait()
        total = own[j].astype(F32) + got[j].astype(F32)
        if j == 0:
            out[...] = total
        else:
            red[j - 1] = total.astype(BF)
            c = remote(red.at[j - 1], got2.at[j - 1], ss.at[j - 1], rs.at[j - 1], me.at(z=me.step("z", j)))
            c.start()
            outs.append(c)
    for c in sends:
        c.wait_send()
    for j in (1, 3, 2):
        f = me.at(z=me.step("z", 4 - j))
        remote(red.at[j - 1], got2.at[j - 1], ss.at[j - 1], rs.at[j - 1], f).wait_recv()
        out[...] += got2[j - 1].astype(F32)
    for c in outs:
        c.wait_send()


def scatter(part, cid):
    return pl.pallas_call(
        scatter_kernel,
        out_shape=sds((ROWS, DX), F32),
        in_specs=[ANY],
        out_specs=VM,
        scratch_shapes=[
            pltpu.VMEM((4, ROWS, DX), BF),
            pltpu.VMEM((4, ROWS, DX), BF),
            pltpu.VMEM((3, ROWS, DX), BF),
            pltpu.VMEM((3, ROWS, DX), BF),
            DMA((4,)),
            DMA((4,)),
            DMA((4,)),
            DMA((3,)),
            DMA((3,)),
        ],
        compiler_params=pltpu.CompilerParams(collective_id=cid, has_side_effects=True, vmem_limit_bytes=VMEM_LIMIT),
    )(part)


def norm_back(z, gain, grad):
    r = rms(z)
    t = gain * grad
    return r * t - z * (r * r * r) * jnp.mean(t * z, -1, keepdims=True)


def back_kernel(
    idx, gn2, e, hid, n2, q, o, p, kv, w_out, a_in, b_res, gain, a45,
    gh_o, gq_o, win_o, g45_o, gbo_o, ga3_o, go, win, sem,
):
    copies = load_windows(kv, win, sem)
    s = lax.axis_index("dp")
    gue = gn2[:, D:].astype(BF)
    gn = gn2[:, :D] + mm(gue, a45[...])
    gh = e[:, :D].astype(F32) + norm_back(hid[...], gain[...].astype(F32), gn)
    gh_o[...] = gh
    ghb = gh.astype(BF)
    ob = o[...]
    gu3 = nt(ghb, b_res[0, 0]).astype(BF)
    go[...] = (nt(ghb, w_out[...]) + mm(gu3, a_in[0, 3])).astype(BF)
    u3 = nt(ob, a_in[0, 3]).astype(BF)
    gbo_o[...] = tn(u3, ghb)
    ga3_o[...] = tn(gu3, ob)
    g45_o[...] = tn(gue, n2[:, :D])
    for h in range(2):
        copies[h].wait()
        for a in range(KV_HEADS):
            qs, gs, os = stack_heads(q, h, a), stack_heads(go, h, a), stack_heads(o, h, a)
            k = win[h, :, :, a * HS : (a + 1) * HS].reshape(KEYS, HS)
            v = win[h, :, :, KW + a * HS : KW + (a + 1) * HS].reshape(KEYS, HS)
            pr = p[2 * h + a]
            delta = jnp.sum(gs.astype(F32) * os.astype(F32), -1, keepdims=True)
            ds = (pr.astype(F32) * (nt(gs, v) - delta)).astype(BF)
            gq = mm(ds, k) * SCALE
            for g in range(GROUP):
                gq_o[h * BLK : (h + 1) * BLK, (a * GROUP + g) * HS : (a * GROUP + g + 1) * HS] = gq[
                    g * BLK : (g + 1) * BLK
                ]
            win_o[h, :, :, a * HS : (a + 1) * HS] = (tn(ds, qs) * SCALE).astype(BF).reshape(NWB, BLK, HS)
            win_o[h, :, :, KW + a * HS : KW + (a + 1) * HS] = tn(pr, gs).astype(BF).reshape(NWB, BLK, HS)


def back(idx, gn2, e, hid, n2, q, o, p, kv, w_out, a_in, b_res, gain, a45):
    outs = (
        sds((ROWS, D), F32),
        sds((ROWS, D), F32),
        sds((2, NWB, BLK, 2 * KW), BF),
        sds((EXT, D), F32),
        sds((R, D), F32),
        sds((R, D), F32),
    )
    return pl.pallas_call(
        back_kernel,
        out_shape=outs,
        grid_spec=pltpu.PrefetchScalarGridSpec(
            num_scalar_prefetch=1,
            grid=(1,),
            in_specs=[
                whole(gn2.shape),
                whole(e.shape),
                whole(hid.shape),
                whole(n2.shape),
                whole(q.shape),
                whole(o.shape),
                whole(p.shape),
                ANY,
                whole(w_out.shape),
                pick(a_in.shape),
                pick(b_res.shape),
                whole((1, D)),
                whole(a45.shape),
            ],
            out_specs=[whole(x.shape) for x in outs],
            scratch_shapes=[
                pltpu.VMEM((ROWS, D), BF),
                pltpu.VMEM((2, NWB, BLK, 2 * KW), BF),
                DMA((2,)),
            ],
        ),
        compiler_params=pltpu.CompilerParams(vmem_limit_bytes=VMEM_LIMIT),
    )(idx, gn2, e, hid, n2, q, o, p, kv, w_out, a_in, b_res, gain, a45)


def return_kernel(win, out, got, ss, rs, ls):
    me = Place()
    m = me.ctx
    bar = pltpu.get_barrier_semaphore()

    def hello(t, carry):
        @pl.when(t != m)
        def _():
            pl.semaphore_signal(bar, inc=1, device_id=(me.dp, t), device_id_type=MESH)

        return carry

    lax.fori_loop(0, N_CTX, hello, 0)
    pl.semaphore_wait(bar, N_CTX - 1)

    def covers(t, w, owner, h):
        block = owner if h == 0 else NBLK - 1 - owner
        j = block - ((t if w == 0 else NBLK - 1 - t) - (NWB - 1))
        return j, (j >= 0) & (j < NWB)

    def send(k, carry):
        t = lax.rem(m + k, N_CTX)
        for w in range(2):
            for h in range(2):
                j, ok = covers(m, w, t, h)

                @pl.when(ok)
                def _():
                    remote(win.at[w, j], got.at[h, w, m], ss.at[h, w, t], rs.at[h, w, m], (me.dp, t)).start()

        return carry

    lax.fori_loop(1, N_CTX, send, 0)
    for w in range(2):
        for h in range(2):
            j, ok = covers(m, w, m, h)

            @pl.when(ok)
            def _():
                c = pltpu.make_async_copy(win.at[w, j], got.at[h, w, m], ls.at[h, w])
                c.start()
                c.wait()

    out[...] = jnp.zeros_like(out)

    def take(k, carry):
        t = lax.rem(m + N_CTX - k, N_CTX)
        for w in range(2):
            for h in range(2):
                _, ok = covers(t, w, m, h)

                @pl.when(ok & (k > 0))
                def _():
                    remote(got.at[h, w, t], got.at[h, w, t], ss.at[h, w, t], rs.at[h, w, t], (me.dp, t)).wait_recv()

                @pl.when(ok)
                def _():
                    out[h] += got[h, w, t].astype(F32)

        return carry

    lax.fori_loop(0, N_CTX, take, 0)

    def sent(k, carry):
        t = lax.rem(m + k, N_CTX)
        for w in range(2):
            for h in range(2):
                j, ok = covers(m, w, t, h)

                @pl.when(ok)
                def _():
                    remote(win.at[w, j], got.at[h, w, m], ss.at[h, w, t], rs.at[h, w, m], (me.dp, t)).wait_send()

        return carry

    lax.fori_loop(1, N_CTX, sent, 0)


def give_back(win):
    return pl.pallas_call(
        return_kernel,
        out_shape=sds((2, BLK, 2 * KW), F32),
        in_specs=[ANY],
        out_specs=VM,
        scratch_shapes=[
            pltpu.VMEM((2, 2, N_CTX, BLK, 2 * KW), BF),
            DMA((2, 2, N_CTX)),
            DMA((2, 2, N_CTX)),
            DMA((2, 2)),
        ],
        compiler_params=pltpu.CompilerParams(collective_id=5, has_side_effects=True, vmem_limit_bytes=VMEM_LIMIT),
    )(win)


def final_kernel(
    idx, gkv, gq, x, n1, gh, hid, y, e, w_qkv, a_in, b_qkv_ad, bd, gain, cos, sin, g45, gbo, ga3,
    out_o, gt_o, tiles_o, gj,
):
    s = lax.axis_index("dp")
    c, sn = cos[...], sin[...]
    for h in range(HEADS):
        cols = slice(h * HS, (h + 1) * HS)
        gj[:, cols] = turn_back(gq[:, cols], c, sn).astype(BF)
    for a in range(KV_HEADS):
        v = jnp.concatenate([gkv[0, :, a * HS : (a + 1) * HS], gkv[1, :, a * HS : (a + 1) * HS]], 0)
        gj[:, QW + a * HS : QW + (a + 1) * HS] = turn_back(v, c, sn).astype(BF)
    gj[:, QW + KW :] = jnp.concatenate([gkv[0, :, KW:], gkv[1, :, KW:]], 0).astype(BF)
    n1b = n1[...]
    gn = nt(gj[...], w_qkv[...])

    def put(at, v):
        for t in range(v.shape[1] // 128):
            tiles_o[at + t] = v[:, 128 * t : 128 * (t + 1)].astype(BF)

    at_qkv = 8 * 12
    for m, (lo, hi) in enumerate(((0, QW), (QW, QW + KW), (QW + KW, QW + 2 * KW))):
        am = a_in[0, m]
        u = nt(n1b, am).astype(BF)
        gjm = gj[:, lo:hi]
        gum = nt(gjm, b_qkv_ad[0, :, lo:hi]).astype(BF)
        gn += mm(gum, am)
        put(at_qkv + lo // 128, tn(u, gjm))
        put(12 * m, tn(gum, n1b))
    put(12 * 3, ga3[...])
    own = pl.multiple_of(s * R, R)
    put(12 * 4, g45[pl.ds(own, R), :])
    put(12 * 5, g45[pl.ds(own + 64, R), :])
    put(12 * 6, gbo[...])
    ud = y[:, D:].astype(BF)
    gbd = tn(ud, e[:, :D])
    own_bd = jnp.where((iota((R, EXT), 1) == iota((R, EXT), 0) + s * R), 1.0, 0.0)
    put(12 * 7, jnp.dot(own_bd, gbd, preferred_element_type=F32))
    for t in range(112, 128):
        tiles_o[t] = jnp.zeros((R, 128), BF)
    gt_o[...] = (gh[...] + norm_back(x[...].astype(F32), gain[...].astype(F32), gn)).astype(BF)
    out_o[...] = (hid[...] + y[:, :D] + mm(ud, bd[...])).astype(BF)


def final(idx, gkv, gq, x, n1, gh, hid, y, e, w_qkv, a_in, b_qkv_ad, bd, gain, cos, sin, g45, gbo, ga3):
    outs = (sds((ROWS, D), BF), sds((ROWS, D), BF), sds((128, R, 128), BF))
    args = (gkv, gq, x, n1, gh, hid, y, e, w_qkv, a_in, b_qkv_ad, bd, gain, cos, sin, g45, gbo, ga3)
    return pl.pallas_call(
        final_kernel,
        out_shape=outs,
        grid_spec=pltpu.PrefetchScalarGridSpec(
            num_scalar_prefetch=1,
            grid=(1,),
            in_specs=[pick(v.shape) if i in (9, 10) else whole(v.shape) for i, v in enumerate(args)],
            out_specs=[whole(x.shape) for x in outs],
            scratch_shapes=[pltpu.VMEM((ROWS, 2048), BF)],
        ),
        compiler_params=pltpu.CompilerParams(vmem_limit_bytes=VMEM_LIMIT),
    )(idx, *args)


def total_kernel(lt, ft, out, gl, gf, red, ls, s1, r1, s2, r2, ss, rs, cs, cr, s3, r3):
    me = Place()
    sib = me.sibling()
    m = me.ctx
    bar = pltpu.get_barrier_semaphore()

    def hello(t, carry):
        @pl.when(t != m)
        def _():
            pl.semaphore_signal(bar, inc=1, device_id=(me.dp, t), device_id_type=MESH)

        return carry

    lax.fori_loop(0, N_CTX, hello, 0)
    others = [me.at(z=me.step("z", 1)), me.at(z=me.step("z", 3)), sib]
    for d in others:
        pl.semaphore_signal(bar, inc=1, device_id=d, device_id_type=MESH)
    pl.semaphore_wait(bar, N_CTX - 1 + len(others))

    xy = me.y * 4 + me.x

    def plane(k):
        return me.at(x=lax.rem(k, 4), y=lax.div(k, 4))

    def send_l(k, carry):
        t = lax.rem(m + k, N_CTX)
        remote(lt.at[pl.ds(4 * t, 4)], gl.at[m], s1.at[t], r1.at[m], (me.dp, t)).start()
        return carry

    def send_f(k, carry):
        t = lax.rem(xy + k, 16)
        remote(ft.at[pl.ds(8 * t, 8)], gf.at[xy], s2.at[t], r2.at[xy], plane(t)).start()
        return carry

    lax.fori_loop(1, 16, send_f, 0)
    lax.fori_loop(1, N_CTX, send_l, 0)
    own = [
        pltpu.make_async_copy(lt.at[pl.ds(4 * m, 4)], gl.at[m], ls.at[0]),
        pltpu.make_async_copy(ft.at[pl.ds(8 * xy, 8)], gf.at[xy], ls.at[1]),
    ]
    for c in own:
        c.start()
    for c in own:
        c.wait()

    def got_f(k, carry):
        t = lax.rem(xy + k, 16)
        remote(gf.at[t], gf.at[t], s2.at[t], r2.at[t], plane(t)).wait_recv()
        return carry + gf[t].astype(F32)

    red[4:] = lax.fori_loop(1, 16, got_f, gf[xy].astype(F32)).astype(BF)

    def got_l(k, carry):
        t = lax.rem(m + k, N_CTX)
        remote(gl.at[t], gl.at[t], s1.at[t], r1.at[t], (me.dp, t)).wait_recv()
        return carry + gl[t].astype(F32)

    red[:4] = lax.fori_loop(1, N_CTX, got_l, gl[m].astype(F32)).astype(BF)

    def vz(j, h):
        ref = out.at[me.y, me.x, lax.rem(j, 2), me.core, lax.div(j, 2)]
        return ref if h is None else ref.at[pl.ds(6 * h, 6)]

    c = pltpu.make_async_copy(red, vz(me.z, None), ls.at[2])
    c.start()
    rz = Ring(me, "z", red, vz, ss.at[0], rs.at[0])
    rz.first()
    rz.second()
    rz.last()
    c.wait()

    def x0(j, h):
        ref = out.at[me.y, j, :, me.core, :, pl.ds(0, 6)]
        return ref if h is None else out.at[me.y, j, h, me.core, :, pl.ds(0, 6)]

    def y0(j, h):
        ref = out.at[j, :, :, me.core, :, pl.ds(0, 6)]
        return ref if h is None else out.at[j, pl.ds(2 * h, 2), :, me.core, :, pl.ds(0, 6)]

    def y1(j, h):
        ref = out.at[j, me.x, :, me.core, :, pl.ds(6, 6)]
        return ref if h is None else out.at[j, me.x, h, me.core, :, pl.ds(6, 6)]

    def x1(j, h):
        ref = out.at[:, j, :, me.core, :, pl.ds(6, 6)]
        return ref if h is None else out.at[pl.ds(2 * h, 2), j, :, me.core, :, pl.ds(6, 6)]

    ra = Ring(me, "x", x0(me.x, None), x0, ss.at[1], rs.at[1])
    rb = Ring(me, "y", y1(me.y, None), y1, ss.at[2], rs.at[2])
    for f in ("first", "second", "last"):
        getattr(ra, f)()
        getattr(rb, f)()
    rc = Ring(me, "y", y0(me.y, None), y0, ss.at[3], rs.at[3])
    rd = Ring(me, "x", x1(me.x, None), x1, ss.at[4], rs.at[4])
    for f in ("first", "second", "last"):
        getattr(rc, f)()
        getattr(rd, f)()
    swaps = []
    for y in range(4):
        ref = out.at[y, :, :, me.core]
        k = remote(ref, ref, cs.at[y], cr.at[y], sib)
        k.start()
        swaps.append(k)
    for r in (rz, ra, rb, rc, rd):
        r.sent()

    def sent_l(k, carry):
        t = lax.rem(m + k, N_CTX)
        remote(lt.at[pl.ds(4 * t, 4)], gl.at[m], s1.at[t], r1.at[m], (me.dp, t)).wait_send()
        return carry

    def sent_f(k, carry):
        t = lax.rem(xy + k, 16)
        remote(ft.at[pl.ds(8 * t, 8)], gf.at[xy], s2.at[t], r2.at[xy], plane(t)).wait_send()
        return carry

    lax.fori_loop(1, 16, sent_f, 0)
    lax.fori_loop(1, N_CTX, sent_l, 0)
    for y in range(4):
        swaps[y].wait_send()
        ref = out.at[y, :, :, 1 - me.core]
        remote(ref, ref, cs.at[y], cr.at[y], sib).wait_recv()


def total(lt, ft):
    return pl.pallas_call(
        total_kernel,
        out_shape=sds((4, 4, 2, 2, 2, 12, R, 128), BF),
        in_specs=[ANY] * 2,
        out_specs=ANY,
        scratch_shapes=[
            pltpu.VMEM((N_CTX, 4, R, 128), BF),
            pltpu.VMEM((16, 8, R, 128), BF),
            pltpu.VMEM((12, R, 128), BF),
            DMA((3,)),
            DMA((N_CTX,)),
            DMA((N_CTX,)),
            DMA((16,)),
            DMA((16,)),
            DMA((5, 4)),
            DMA((5, 4)),
            DMA((4,)),
            DMA((4,)),
            DMA((1,)),
            DMA((1,)),
        ],
        compiler_params=pltpu.CompilerParams(collective_id=6, has_side_effects=True, vmem_limit_bytes=VMEM_LIMIT),
    )(lt, ft)


def spread_kernel(idx, t, ain_o, aff_o, bqkv_o, bres_o, bff_o):
    e = pl.program_id(0)
    for ref in (ain_o, aff_o, bqkv_o, bres_o, bff_o):
        ref[...] = jnp.zeros_like(ref)

    def local_tile(s, n):
        k, j = n // 4, n % 4
        y, zh, x = k // 8, (k // 4) % 2, k % 4
        return t[y, x, s // 2, s % 2, zh, j].astype(F32)

    def ff_tile(piece, n):
        k, j = n // 8, n % 8
        return t[k // 4, k % 4, piece // 4, (piece // 2) % 2, piece % 2, 4 + j].astype(F32)

    for s in range(4):

        @pl.when(idx[s] == e)
        def _():
            for m in range(6):
                for c in range(12):
                    ain_o[0, m, :, 128 * c : 128 * (c + 1)] += local_tile(s, 12 * m + c)
            for m in range(2):
                for c in range(12):
                    bres_o[0, m, :, 128 * c : 128 * (c + 1)] += local_tile(s, 12 * (6 + m) + c)
            for c in range(16):
                bqkv_o[0, :, 128 * c : 128 * (c + 1)] += local_tile(s, 96 + c)
            for piece in range(8):
                tile = 60 if piece == 7 else 35 * piece // 4
                for k in range(3):
                    for c in range(10):
                        cols = slice(128 * (tile + c), 128 * (tile + c + 1))
                        v = ff_tile(piece, s * 30 + k * 10 + c)
                        if k == 0:
                            aff_o[0, :, cols] += v
                        else:
                            bff_o[0, k - 1, :, cols] += v


def spread(idx, t):
    outs = (
        sds((ADAPT, 6, R, D), F32),
        sds((ADAPT, R, FF), F32),
        sds((ADAPT, R, 2048), F32),
        sds((ADAPT, 2, R, D), F32),
        sds((ADAPT, 2, R, FF), F32),
    )

    def one(shape):
        return pl.BlockSpec((1,) + shape[1:], lambda i, idx: (i,) + (0,) * (len(shape) - 1))

    return pl.pallas_call(
        spread_kernel,
        out_shape=outs,
        grid_spec=pltpu.PrefetchScalarGridSpec(
            num_scalar_prefetch=1,
            grid=(ADAPT,),
            in_specs=[whole(t.shape)],
            out_specs=[one(o.shape) for o in outs],
        ),
        compiler_params=pltpu.CompilerParams(vmem_limit_bytes=VMEM_LIMIT),
    )(idx, t)


def local(
    tokens,
    cotangent,
    w_qkv,
    b_qkv,
    w_out,
    w_gu,
    w_down,
    gain_attn,
    gain_mlp,
    adapt_in,
    adapt_in_ff,
    adapt_out_qkv,
    adapt_out_res,
    adapt_out_ff,
    doc_lengths,
    adapter_index,
    window,
):
    member = lax.axis_index("ctx")
    starts = jnp.stack([member * BLK, (NBLK - 1 - member) * BLK])
    pos = (starts[:, None] + jnp.arange(BLK, dtype=jnp.int32)[None]).reshape(ROWS)
    ends = jnp.cumsum(doc_lengths[0])
    begin = jnp.max(jnp.where(ends[None] <= pos[:, None], ends[None], 0), -1)
    low = jnp.maximum(begin, pos - window[0] + 1)
    low = jnp.broadcast_to(low[:, None], (ROWS, 128)).astype(jnp.int32)
    freq = 1000000.0 ** (-(2.0 * jnp.arange(HS // 2, dtype=F32)) / HS)
    ang = pos.astype(F32)[:, None] * freq[None]
    c, sn = jnp.cos(ang), jnp.sin(ang)
    cos = jnp.concatenate([c, c], -1)
    sin = jnp.concatenate([-sn, sn], -1)

    tok = jnp.transpose(tokens[0], (1, 0, 2)).reshape(ROWS, D)
    cot = jnp.transpose(cotangent[0], (1, 0, 2)).reshape(ROWS, D)
    gain1, gain2 = gain_attn[None], gain_mlp[None]
    wq = jnp.pad(w_qkv, ((0, 4), (0, 0)))
    wo = jnp.pad(w_out, ((0, 4), (0, 0)))
    wg = jnp.pad(jnp.transpose(w_gu, (1, 0, 2)), ((0, 0), (0, 4), (0, 0)))
    wd = jnp.pad(w_down, ((0, 10), (0, 0)))
    idx_row = jnp.broadcast_to(adapter_index[:, None], (8, 128)).astype(jnp.int32)

    x, n1, eext, ub, a45, bd = prepare(
        adapter_index, tok, cot, adapt_in, adapt_out_qkv, adapt_out_res, gain1, b_qkv[None]
    )
    oq, oo, og, od, oe, oi = weights(idx_row, wq, wo, wg, wd, eext)
    oq = oq.reshape(D, 2048)
    oo = oo.reshape(D, D)
    og = og.reshape(4, D, 640)
    idx4 = oi[:, 0, 0, 0]
    q, kv = qkv(n1, oq, ub, cos, sin)
    kv_all = halo(kv)
    p, o, hid, n2 = attend(adapter_index, low, q, kv_all, x, oo, adapt_in, adapt_out_res, gain2, a45)
    xg = gather(n2).reshape(8 * ROWS, DX)
    down = compact(od)
    yp, gp, ft = feed(idx4, xg, oe.reshape(8 * ROWS, DX), og, down, adapt_in_ff, adapt_out_ff)
    gn2 = scatter(gp.reshape(2, 2, 2, ROWS, DX), 4)
    gh, gq, win, g45, gbo, ga3 = back(
        adapter_index, gn2, eext, hid, n2, q, o, p, kv_all, oo, adapt_in, adapt_out_res, gain2, a45
    )
    y = scatter(yp.reshape(2, 2, 2, ROWS, DX), 4)
    gkv = give_back(win)
    out, gt, lt = final(
        adapter_index, gkv, gq, x, n1, gh, hid, y, eext, oq, adapt_in, adapt_out_qkv, bd, gain1, cos, sin, g45, gbo, ga3
    )
    tiles = total(lt, ft)
    grads = spread(idx4, tiles)

    def deal(v):
        return jnp.transpose(v.reshape(2, BLK, D), (1, 0, 2))[None]

    return (deal(out), deal(gt)) + tuple(grads)


def solution(mesh):
    return jax.shard_map(
        local,
        mesh=mesh,
        in_specs=(
            P("dp", "ctx", None, None),
            P("dp", "ctx", None, None),
            P(("dp", "ctx"), None),
            P(),
            P(("dp", "ctx"), None),
            P(("dp", "ctx"), None, None),
            P(("dp", "ctx"), None),
            P(),
            P(),
            P(),
            P(),
            P(),
            P(),
            P(),
            P("dp", None),
            P("dp"),
            P("dp"),
        ),
        out_specs=(P("dp", "ctx", None, None), P("dp", "ctx", None, None), P(), P(), P(), P(), P()),
        check_vma=False,
    )
```

```python
import functools

import jax
import jax.numpy as jnp
from jax import lax
from jax.experimental import pallas as pl
from jax.experimental.pallas import tpu as pltpu
from jax.sharding import PartitionSpec as P

D = 1536
HEADS = 12
KV_HEADS = 2
HS = 128
GROUP = HEADS // KV_HEADS
FF = 8960
R = 16
ADAPT = 8
BLK = 64
ROWS = 2 * BLK
N_CTX = 32
NBLK = 2 * N_CTX
WIN = 1024
NWB = WIN // BLK + 1
KEYS = NWB * BLK
EXT = 128
DX = D + EXT
FW = 1280
FV = FF // 8
QW = HEADS * HS
KW = KV_HEADS * HS
SCALE = HS**-0.5
EPS = 1e-6

MESH = pl.DeviceIdType.MESH
BF = jnp.bfloat16
F32 = jnp.float32
ANY = pl.BlockSpec(memory_space=pl.ANY)
VM = pl.BlockSpec(memory_space=pltpu.VMEM)
SM = pl.BlockSpec(memory_space=pltpu.SMEM)
DMA = pltpu.SemaphoreType.DMA
VMEM_LIMIT = 60 * 2**20


def sds(shape, dtype):
    return jax.ShapeDtypeStruct(shape, dtype)


def nt(a, b):
    return lax.dot_general(a, b, (((1,), (1,)), ((), ())), preferred_element_type=F32)


def tn(a, b):
    return lax.dot_general(a, b, (((0,), (0,)), ((), ())), preferred_element_type=F32)


def mm(a, b):
    return jnp.dot(a, b, preferred_element_type=F32)


def iota(shape, dim):
    return lax.broadcasted_iota(jnp.int32, shape, dim)


class Place:
    def __init__(self):
        dp, ctx = lax.axis_index("dp"), lax.axis_index("ctx")
        self.dp, self.ctx = dp, ctx
        self.zlo, self.core = lax.div(dp, 2), lax.rem(dp, 2)
        self.y, self.zhi, self.x = lax.div(ctx, 8), lax.rem(lax.div(ctx, 4), 2), lax.rem(ctx, 4)
        self.z = self.zhi * 2 + self.zlo
        self.slice = 2 * dp + self.zhi

    def at(self, x=None, y=None, z=None, core=None):
        x = self.x if x is None else x
        y = self.y if y is None else y
        z = self.z if z is None else z
        core = self.core if core is None else core
        return (lax.rem(z, 2) * 2 + core, y * 8 + lax.div(z, 2) * 4 + x)

    def step(self, axis, by):
        return lax.rem(getattr(self, axis) + by, 4)

    def ring(self, axis):
        return [self.at(**{axis: self.step(axis, k)}) for k in (1, 2, 3)]

    def sibling(self):
        return self.at(core=1 - self.core)


def window_tile(piece):
    return jnp.minimum(lax.div(35 * piece, 4), 60)


def remote(src, dst, send, recv, device):
    return pltpu.make_async_remote_copy(
        src_ref=src, dst_ref=dst, send_sem=send, recv_sem=recv, device_id=device, device_id_type=MESH
    )


def greet(peers):
    sem = pltpu.get_barrier_semaphore()
    for device in peers:
        pl.semaphore_signal(sem, inc=1, device_id=device, device_id_type=MESH)
    pl.semaphore_wait(sem, len(peers))


class Ring:
    def __init__(self, me, axis, own, view, send, recv):
        self.i = getattr(me, axis)
        self.r, self.o, self.l = (me.step(axis, k) for k in (1, 2, 3))
        self.right, self.left = me.at(**{axis: self.r}), me.at(**{axis: self.l})
        self.own, self.view, self.send, self.recv = own, view, send, recv

    def copy(self, k, src, dst, device):
        return remote(src, dst, self.send.at[k], self.recv.at[k], device)

    def first(self):
        place = self.view(self.i, None)
        self.out = [self.copy(0, self.own, place, self.right), self.copy(1, self.own, place, self.left)]
        for c in self.out:
            c.start()

    def second(self):
        v = self.view
        self.copy(0, v(self.l, None), v(self.l, None), self.right).wait_recv()
        c = self.copy(2, v(self.l, 0), v(self.l, 0), self.right)
        c.start()
        self.out.append(c)
        self.copy(1, v(self.r, None), v(self.r, None), self.left).wait_recv()
        c = self.copy(3, v(self.r, 1), v(self.r, 1), self.left)
        c.start()
        self.out.append(c)

    def last(self):
        v = self.view
        self.copy(2, v(self.o, 0), v(self.o, 0), self.right).wait_recv()
        self.copy(3, v(self.o, 1), v(self.o, 1), self.left).wait_recv()

    def sent(self):
        for c in self.out:
            c.wait_send()


class ZGather:
    def __init__(self, me, own, buf, send, recv, core_send, core_recv, half):
        self.me, self.own, self.buf = me, own, buf
        self.cs, self.cr = core_send, core_recv

        def view(j, h, core=me.core):
            ref = buf.at[lax.rem(j, 2), core, lax.div(j, 2)]
            return ref if h is None else ref.at[pl.ds(h * half, half)]

        self.view = view
        self.ring = Ring(me, "z", own, view, send, recv)
        self.out = []

    def swap(self, src, j):
        c = remote(src, self.view(j, None), self.cs.at[len(self.out)], self.cr.at[len(self.out)], self.me.sibling())
        c.start()
        self.out.append((c, j))

    def first(self):
        self.ring.first()
        self.swap(self.own, self.me.z)

    def second(self):
        self.ring.second()
        self.swap(self.view(self.ring.l, None), self.ring.l)
        self.swap(self.view(self.ring.r, None), self.ring.r)

    def last(self):
        self.ring.last()
        self.swap(self.view(self.ring.o, None), self.ring.o)

    def finish(self):
        self.ring.sent()
        for k, (c, j) in enumerate(self.out):
            c.wait_send()
            place = self.view(j, None, 1 - self.me.core)
            remote(place, place, self.cs.at[k], self.cr.at[k], self.me.sibling()).wait_recv()


def rms(z):
    return lax.rsqrt(jnp.mean(z * z, -1, keepdims=True) + EPS)


def prepare_kernel(idx, tok, cot, a_in, b_qkv_ad, b_res, gain, bias, x_o, n1_o, e_o, ub_o, a45_o, bd_o, a3_o, bo_o):
    s = lax.axis_index("dp")
    for h in range(2):
        rows = slice(h * BLK, (h + 1) * BLK)
        x_o[rows] = tok[:, h, :]
        e_o[rows, :D] = cot[:, h, :]
    x = x_o[...].astype(F32)
    n1 = (x * rms(x) * gain[...].astype(F32)).astype(BF)
    n1_o[...] = n1
    for m, (lo, hi) in enumerate(((0, QW), (QW, QW + KW), (QW + KW, QW + 2 * KW))):
        u = nt(n1, a_in[0, m]).astype(BF)
        ub_o[:, lo:hi] = mm(u, b_qkv_ad[0, :, lo:hi]) + bias[lo:hi].astype(F32)
    at = pl.multiple_of(s * R, R)
    a45_o[...] = jnp.zeros_like(a45_o)
    a45_o[pl.ds(at, R), :] = a_in[0, 4]
    a45_o[pl.ds(at + 64, R), :] = a_in[0, 5]
    bd_o[...] = jnp.zeros_like(bd_o)
    bd_o[pl.ds(at, R), :] = b_res[0, 1]
    a3_o[...] = a_in[0, 3]
    bo_o[...] = b_res[0, 0]
    e_o[:, D:] = nt(e_o[:, :D], bd_o[...]).astype(BF)


def pick(shape):
    return pl.BlockSpec((1,) + shape[1:], lambda i, idx: (idx[0],) + (0,) * (len(shape) - 1))


def whole(shape):
    return pl.BlockSpec(shape, lambda i, idx: (0,) * len(shape))


def prepare(idx, tok, cot, a_in, b_qkv_ad, b_res, gain, bias):
    outs = (
        sds((ROWS, D), BF),
        sds((ROWS, D), BF),
        sds((ROWS, DX), BF),
        sds((ROWS, 2048), F32),
        sds((EXT, D), BF),
        sds((EXT, D), BF),
        sds((R, D), BF),
        sds((R, D), BF),
    )
    return pl.pallas_call(
        prepare_kernel,
        out_shape=outs,
        grid_spec=pltpu.PrefetchScalarGridSpec(
            num_scalar_prefetch=1,
            grid=(1,),
            in_specs=[
                whole((BLK, 2, D)),
                whole((BLK, 2, D)),
                pick(a_in.shape),
                pick(b_qkv_ad.shape),
                pick(b_res.shape),
                whole((D,)),
                whole((2048,)),
            ],
            out_specs=[whole(o.shape) for o in outs],
        ),
        compiler_params=pltpu.CompilerParams(vmem_limit_bytes=VMEM_LIMIT),
    )(idx, tok, cot, a_in, b_qkv_ad, b_res, gain, bias)


def turn(v, cos, sin):
    return v * cos + pltpu.roll(v, 64, 1) * sin


def turn_back(v, cos, sin):
    return v * cos - pltpu.roll(v, 64, 1) * sin


def stack_heads(ref, h, a):
    rows = slice(h * BLK, (h + 1) * BLK)
    return jnp.concatenate(
        [ref[rows, (a * GROUP + g) * HS : (a * GROUP + g + 1) * HS] for g in range(GROUP)], 0
    )


def reads(t, block):
    a, b = t - block, NBLK - 1 - t - block
    return ((a >= 0) & (a < NWB)) | ((b >= 0) & (b < NWB))


ZK = [(dz, dc) for dz in range(4) for dc in range(2) if dz or dc]


def front_kernel(
    idx, wq_i, wo_i, wg, wd_i, eext, n1, ub, cos, sin, low, x, gain, a45, a3, bo,
    oq_o, oo_o, og, od_o, oe, oi, win_o, p_o, xg, q, o_o, hid_o, n2,
    rq, ro, rg, wdp, rd, cq, co, cg, oq, oo, od, kv_own, kv, p, down,
    ss, rs, ls, s1, r1, s2, r2, sc, rc, sd, rdn, sk, rk, ez_sems, si, ri, nz_sems,
):
    me = Place()
    sib = me.sibling()
    m = me.ctx
    bar = pltpu.get_barrier_semaphore()

    def hello(t, carry):
        @pl.when(t != m)
        def _():
            pl.semaphore_signal(bar, inc=1, device_id=(me.dp, t), device_id_type=MESH)

        return carry

    lax.fori_loop(0, N_CTX, hello, 0)
    others = [me.at(z=me.step("z", dz), core=lax.rem(me.core + dc, 2)) for dz, dc in ZK if dz % 2 or dc]
    for d in others:
        pl.semaphore_signal(bar, inc=1, device_id=d, device_id_type=MESH)

    rq[me.x, :12] = wq_i[...]
    rq[me.x, 12:] = jnp.zeros((4, 2048), BF)
    ro[me.x, :12] = wo_i[...]
    ro[me.x, 12:] = jnp.zeros((4, D), BF)
    wdp[:70] = wd_i[...]
    wdp[70:] = jnp.zeros((10, D), BF)
    kv[:16] = jnp.zeros((16, BLK, 2 * KW), BF)

    pl.semaphore_wait(bar, N_CTX - 1 + len(others))

    tiles = [60 if g == 7 else 35 * g // 4 for g in range(8)]

    def panel(g, t):
        col = pl.multiple_of(tiles[g] * 128 + lax.rem(t, 2) * 640, 128)
        return wg.at[lax.div(t, 2), :, pl.ds(col, 640)]

    def strip(t):
        return wdp.at[:, pl.ds(pl.multiple_of(384 * t, 128), 384)]

    def start(c, out):
        c.start()
        out.append(c)

    first = []
    xs = [(k, me.step("x", k), me.at(x=me.step("x", k))) for k in (1, 3, 2)]
    for k, t, d in xs:
        start(remote(rq.at[me.x], rq.at[me.x], s1.at[k - 1, 0], r1.at[k - 1, 0], d), first)
    ez = ZGather(me, eext, oe, *ez_sems, BLK)
    ez.first()
    for k, t, d in xs:
        start(remote(ro.at[me.x], ro.at[me.x], s1.at[k - 1, 1], r1.at[k - 1, 1], d), first)
    for k, t, d in xs:
        for g in range(8):
            start(remote(panel(g, t), rg.at[me.x, g], s1.at[k - 1, 2 + g], r1.at[k - 1, 2 + g], d), first)
        start(remote(strip(t), rd.at[me.x], s1.at[k - 1, 10], r1.at[k - 1, 10], d), first)
    mine = []
    for g in range(8):
        start(pltpu.make_async_copy(panel(g, me.x), rg.at[me.x, g], ls.at[2 + g]), mine)
    start(pltpu.make_async_copy(strip(me.x), rd.at[me.x], ls.at[1]), mine)
    side = []
    start(pltpu.make_async_copy(eext, oe.at[me.zlo, me.core, me.zhi], ls.at[10]), side)
    start(pltpu.make_async_copy(idx, oi.at[me.dp, me.zhi], ls.at[11]), side)
    for n, (dz, dc) in enumerate(ZK):
        d = me.at(z=me.step("z", dz), core=lax.rem(me.core + dc, 2))
        start(remote(idx, oi.at[me.dp, me.zhi], si.at[n], ri.at[n], d), first)

    def from_x(n, ref_of):
        for k in (1, 3, 2):
            f = me.step("x", 4 - k)
            ref = ref_of(f)
            remote(ref, ref, s1.at[k - 1, n], r1.at[k - 1, n], me.at(x=f)).wait_recv()

    row, col = iota((48, 64), 0), iota((48, 64), 1)
    put = jnp.where(
        (lax.rem(col, 16) < 12) & (lax.div(col, 16) * 12 + lax.rem(col, 16) == row), 1.0, 0.0
    ).astype(BF)

    from_x(0, lambda f: rq.at[f])
    cq[...] = mm(put, rq[...].reshape(64, 2048)).astype(BF)
    lo, hi = pl.ds(0, 1024), pl.ds(1024, 1024)

    def qy0(j, h):
        return oq.at[me.zlo, me.core, j, me.zhi, :, lo if h is None else pl.ds(512 * h, 512)]

    def qz0(j, h, core=me.core):
        zl, zh = lax.rem(j, 2), lax.div(j, 2)
        return oq.at[zl, core, :, zh, :, lo] if h is None else oq.at[zl, core, pl.ds(2 * h, 2), zh, :, lo]

    def qz1(j, h):
        cols = hi if h is None else pl.ds(1024 + 512 * h, 512)
        return oq.at[lax.rem(j, 2), me.core, me.y, lax.div(j, 2), :, cols]

    def qy1(j, h, core=me.core):
        return oq.at[:, core, j, :, :, hi] if h is None else oq.at[h, core, j, :, :, hi]

    qa = Ring(me, "y", cq.at[:, lo], qy0, ss.at[0], rs.at[0])
    qb = Ring(me, "z", cq.at[:, hi], qz1, ss.at[1], rs.at[1])
    qa.first()
    qb.first()
    oq[me.zlo, me.core, me.y, me.zhi] = cq[...]
    from_x(1, lambda f: ro.at[f])
    co[...] = mm(put, ro[...].reshape(64, D)).astype(BF)
    for n in range(8):
        from_x(2 + n, lambda f: rg.at[f, n])
    from_x(10, lambda f: rd.at[f])
    for c in mine:
        c.wait()
    for g in range(8):
        cg[g] = mm(put, rg[:, g].reshape(64, 640)).astype(BF)
    qa.second()
    qb.second()

    own_g = pltpu.make_async_copy(cg.at[me.slice], og.at[me.x, me.zlo, me.core, me.y, me.zhi], ls.at[14])
    own_g.start()
    zc = []
    for n, (dz, dc) in enumerate(ZK):
        z, core = me.step("z", dz), lax.rem(me.core + dc, 2)
        piece = 2 * (2 * lax.rem(z, 2) + core) + lax.div(z, 2)
        d = me.at(z=z, core=core)
        start(remote(cg.at[piece], og.at[me.x, me.zlo, me.core, me.y, me.zhi], s2.at[n], r2.at[n], d), zc)
    keeper = lax.div(me.y, 2) == me.zhi
    rows4 = pl.ds(lax.rem(me.y, 2) * 8 + me.zhi * 4, 4)
    across = me.at(z=me.step("z", 2))
    d_local = pltpu.make_async_copy(rd, od.at[me.x, rows4], ls.at[15])
    d_cross = remote(rd, od.at[me.x, rows4], sd.at[0], rdn.at[0], across)

    @pl.when(keeper)
    def _():
        d_local.start()

    @pl.when(jnp.logical_not(keeper))
    def _():
        d_cross.start()

    qa.last()
    qb.last()
    qa2 = Ring(me, "z", qz0(me.z, None), qz0, ss.at[2], rs.at[2])
    qb2 = Ring(me, "y", qy1(me.y, None), qy1, ss.at[3], rs.at[3])
    qa2.first()
    qb2.first()
    swaps = []

    def swap(view, j):
        n = len(swaps)
        c = remote(view(j, None), view(j, None), sc.at[n], rc.at[n], sib)
        c.start()
        swaps.append((c, view, j))

    def swapped(n):
        c, view, j = swaps[n]
        c.wait_send()
        ref = view(j, None, 1 - me.core)
        remote(ref, ref, sc.at[n], rc.at[n], sib).wait_recv()

    swap(qz0, me.z)
    swap(qy1, me.y)
    ez.second()
    def oy(j, h):
        ref = oo.at[me.zlo, me.core, j, me.zhi]
        return ref if h is None else ref.at[:, pl.ds(768 * h, 768)]

    def oz(j, h, core=me.core):
        zl, zh = lax.rem(j, 2), lax.div(j, 2)
        return oo.at[zl, core, :, zh] if h is None else oo.at[zl, core, pl.ds(2 * h, 2), zh]

    wa = Ring(me, "y", co, oy, ss.at[8], rs.at[8])
    qa2.second()
    qb2.second()
    swap(qz0, qa2.l)
    swap(qy1, qb2.l)
    swap(qz0, qa2.r)
    swap(qy1, qb2.r)
    wa.first()
    oo[me.zlo, me.core, me.y, me.zhi] = co[...]

    own_g.wait()
    for n, (dz, dc) in enumerate(ZK):
        z, core = me.step("z", 4 - dz if dz else 0), lax.rem(me.core + dc, 2)
        ref = og.at[me.x, lax.rem(z, 2), core, me.y, lax.div(z, 2)]
        remote(ref, ref, s2.at[n], r2.at[n], me.at(z=z, core=core)).wait_recv()

    def g0a(j, h):
        return og.at[me.x, 0, :, j] if h is None else og.at[me.x, 0, h, j]

    def g0b(j, h):
        return og.at[j, 0] if h is None else og.at[j, 0, h]

    def g1a(j, h):
        return og.at[j, 1, :, me.y] if h is None else og.at[j, 1, h, me.y]

    def g1b(j, h):
        return og.at[:, 1, :, j] if h is None else og.at[:, 1, h, j]

    ga = Ring(me, "y", g0a(me.y, None), g0a, ss.at[4], rs.at[4])
    gb = Ring(me, "x", g1a(me.x, None), g1a, ss.at[5], rs.at[5])
    ga.first()
    gb.first()
    qa2.last()
    qb2.last()
    swap(qz0, qa2.o)
    swap(qy1, qb2.o)

    rows4b = pl.ds(lax.rem(me.y, 2) * 8 + (1 - me.zhi) * 4, 4)
    rows8 = pl.ds(lax.rem(me.y, 2) * 8, 8)
    ys = [(k, me.step("y", k)) for k in (1, 3, 2)]

    @pl.when(keeper)
    def _():
        d_local.wait()
        ref = od.at[me.x, rows4b]
        remote(rd, ref, sd.at[0], rdn.at[0], across).wait_recv()
        for k, t in ys:
            remote(od.at[me.x, rows8], od.at[me.x, rows8], sd.at[k], rdn.at[k], me.at(y=t)).start()

    wa.second()
    ga.second()
    gb.second()
    for n in range(8):
        swapped(n)
    keep_q = pltpu.make_async_copy(oq, oq_o, ls.at[12])
    keep_q.start()

    c, s = cos[...], sin[...]
    n1v = n1[...]
    for h in (12, 14, 0, 2, 4, 6, 8, 10):
        pair = slice(h * HS, (h + 2) * HS)
        j = mm(n1v, oq[:, :, :, :, :, pair].reshape(D, 2 * HS)) + ub[:, pair]
        for i in range(2):
            v = j[:, i * HS : (i + 1) * HS]
            if h + i < HEADS + KV_HEADS:
                v = turn(v, c, s)
            v = v.astype(BF)
            if h + i < HEADS:
                q[:, (h + i) * HS : (h + i + 1) * HS] = v
            else:
                at = slice((h + i - HEADS) * HS, (h + i - HEADS + 1) * HS)
                kv_own[0, :, at] = v[:BLK]
                kv_own[1, :, at] = v[BLK:]
        if h == 14:
            def send(k, carry):
                t = lax.rem(m + k, N_CTX)
                for half in range(2):
                    block = m if half == 0 else NBLK - 1 - m

                    @pl.when(reads(t, block))
                    def _():
                        src, dst = kv_own.at[half], kv.at[16 + block]
                        remote(src, dst, sk.at[half, k], rk.at[block], (me.dp, t)).start()

                return carry

            lax.fori_loop(1, N_CTX, send, 0)
            kv[16 + m] = kv_own[0]
            kv[16 + NBLK - 1 - m] = kv_own[1]

    wa.last()
    wb = Ring(me, "z", oz(me.z, None), oz, ss.at[9], rs.at[9])
    wb.first()
    swap(oz, me.z)
    ga.last()
    gb.last()
    ga2 = Ring(me, "x", g0b(me.x, None), g0b, ss.at[6], rs.at[6])
    gb2 = Ring(me, "y", g1b(me.y, None), g1b, ss.at[7], rs.at[7])
    ga2.first()
    gb2.first()

    def arrived(block):
        src = jnp.where(block < N_CTX, block, NBLK - 1 - block)
        remote(kv_own.at[0], kv.at[16 + block], sk.at[0, 0], rk.at[block], (me.dp, src)).wait_recv()

    def near0(j, carry):
        block = m - (NWB - 1) + j

        @pl.when(block >= 0)
        def _():
            arrived(block)

        return carry

    def near1(j, carry):
        block = NBLK - 1 - m - (NWB - 1) + j

        @pl.when(block > m)
        def _():
            arrived(block)

        return carry

    wins = []
    keep_p = []
    for h in range(2):
        lax.fori_loop(0, NWB - 1, near0 if h == 0 else near1, 0)
        win = kv.at[pl.ds(m if h == 0 else NBLK - 1 - m, NWB)]
        start(pltpu.make_async_copy(win, win_o.at[h], ls.at[16 + h]), wins)
        base = (m if h == 0 else NBLK - 1 - m) * BLK
        kpos = base - WIN + iota((BLK, KEYS), 1)
        qpos = base + iota((BLK, KEYS), 0)
        keep = (kpos <= qpos) & (kpos >= low[h * BLK : (h + 1) * BLK, :1])
        for a in range(KV_HEADS):
            qs = stack_heads(q, h, a)
            k = win[:, :, a * HS : (a + 1) * HS].reshape(KEYS, HS)
            v = win[:, :, KW + a * HS : KW + (a + 1) * HS].reshape(KEYS, HS)
            sco = nt(qs, k) * SCALE
            sco = jnp.where(keep[None], sco.reshape(GROUP, BLK, KEYS), -1e30)
            e = jnp.exp(sco - jnp.max(sco, -1, keepdims=True))
            pr = (e / jnp.sum(e, -1, keepdims=True)).astype(BF).reshape(GROUP * BLK, KEYS)
            p[2 * h + a] = pr
            o = mm(pr, v).astype(BF)
            for g in range(GROUP):
                o_o[h * BLK : (h + 1) * BLK, (a * GROUP + g) * HS : (a * GROUP + g + 1) * HS] = o[
                    g * BLK : (g + 1) * BLK
                ]
        if h == 0:
            wb.second()
            swap(oz, wb.l)
            swap(oz, wb.r)

    start(pltpu.make_async_copy(p, p_o, ls.at[18]), keep_p)
    wb.last()
    swap(oz, wb.o)
    def dx(j, h):
        return od.at[j] if h is None else od.at[j, pl.ds(8 * h, 8)]

    for k, t in ys:
        f = me.step("y", 4 - k)

        @pl.when(lax.div(f, 2) == me.zhi)
        def _():
            ref = od.at[me.x, pl.ds(lax.rem(f, 2) * 8, 8)]
            remote(ref, ref, sd.at[k], rdn.at[k], me.at(y=f)).wait_recv()

    da = Ring(me, "x", od.at[me.x], dx, ss.at[10], rs.at[10])
    da.first()
    for n in range(8, 12):
        swapped(n)
    keep_o = pltpu.make_async_copy(oo, oo_o, ls.at[13])
    keep_o.start()

    ob = o_o[...]
    u3 = nt(ob, a3[...]).astype(BF)
    hid = x[...].astype(F32) + mm(ob, oo[...].reshape(D, D)) + mm(u3, bo[...])
    hid_o[...] = hid
    nv = (hid * rms(hid) * gain[...].astype(F32)).astype(BF)
    n2[:, :D] = nv
    n2[:, D:] = nt(nv, a45[...]).astype(BF)
    nz = ZGather(me, n2, xg, *nz_sems, BLK)
    nz.first()
    start(pltpu.make_async_copy(n2, xg.at[me.zlo, me.core, me.zhi], ls.at[19]), side)
    ga2.second()
    gb2.second()
    da.second()
    ez.last()
    nz.second()
    da.last()

    piece = me.slice
    off = FV * piece - 128 * window_tile(piece)
    for r in range(5):
        base = 256 * r - off
        i0 = jnp.minimum(lax.div(jnp.maximum(base, 0), 70), 11)
        rw, cl = iota((256, 400), 0) + base, iota((256, 400), 1)
        i, k = i0 + lax.div(cl, 80), lax.rem(cl, 80)
        pick70 = jnp.where((k < 70) & (i * 70 + k == rw), 1.0, 0.0).astype(BF)
        for j in range(4):
            src = od[j, pl.ds(i0, 5)].reshape(400, 384)
            down[256 * r : 256 * (r + 1), 384 * j : 384 * (j + 1)] = mm(pick70, src).astype(BF)
    keep_d = pltpu.make_async_copy(down, od_o, ls.at[20])
    keep_d.start()
    nz.last()
    ga2.last()
    gb2.last()

    for r in (qa, qb, qa2, qb2, wa, wb, ga, gb, ga2, gb2, da):
        r.sent()
    for c in first + zc:
        c.wait_send()

    @pl.when(jnp.logical_not(keeper))
    def _():
        d_cross.wait_send()

    @pl.when(keeper)
    def _():
        for k, t in ys:
            remote(od.at[me.x, rows8], od.at[me.x, rows8], sd.at[k], rdn.at[k], me.at(y=t)).wait_send()

    def sent(k, carry):
        t = lax.rem(m + k, N_CTX)
        for half in range(2):
            block = m if half == 0 else NBLK - 1 - m

            @pl.when(reads(t, block))
            def _():
                src, dst = kv_own.at[half], kv.at[16 + block]
                remote(src, dst, sk.at[half, k], rk.at[block], (me.dp, t)).wait_send()

        return carry

    lax.fori_loop(1, N_CTX, sent, 0)
    for n, (dz, dc) in enumerate(ZK):
        z, core = me.step("z", 4 - dz if dz else 0), lax.rem(me.core + dc, 2)
        ref = oi.at[2 * lax.rem(z, 2) + core, lax.div(z, 2)]
        remote(ref, ref, si.at[n], ri.at[n], me.at(z=z, core=core)).wait_recv()
    ez.finish()
    nz.finish()
    for c in side + wins + keep_p + [keep_q, keep_o, keep_d]:
        c.wait()


def front(idx, wq, wo, wg, wd, eext, n1, ub, cos, sin, low, x, gain, a45, a3, bo):
    outs = (
        sds((2, 2, 4, 2, 48, 2048), BF),
        sds((2, 2, 4, 2, 48, D), BF),
        sds((4, 2, 2, 4, 2, 48, 640), BF),
        sds((FW, D), BF),
        sds((2, 2, 2, ROWS, DX), BF),
        sds((4, 2, 8, 128), jnp.int32),
        sds((2, NWB, BLK, 2 * KW), BF),
        sds((4, GROUP * BLK, KEYS), BF),
        sds((2, 2, 2, ROWS, DX), BF),
        sds((ROWS, D), BF),
        sds((ROWS, D), BF),
        sds((ROWS, D), F32),
        sds((ROWS, DX), BF),
    )
    four = (DMA((4,)),) * 4
    scratch = [
        pltpu.VMEM((4, 16, 2048), BF),
        pltpu.VMEM((4, 16, D), BF),
        pltpu.VMEM((4, 8, 16, 640), BF),
        pltpu.VMEM((80, D), BF),
        pltpu.VMEM((4, 80, 384), BF),
        pltpu.VMEM((48, 2048), BF),
        pltpu.VMEM((48, D), BF),
        pltpu.VMEM((8, 48, 640), BF),
        pltpu.VMEM((2, 2, 4, 2, 48, 2048), BF),
        pltpu.VMEM((2, 2, 4, 2, 48, D), BF),
        pltpu.VMEM((4, 16, 80, 384), BF),
        pltpu.VMEM((2, BLK, 2 * KW), BF),
        pltpu.VMEM((16 + NBLK, BLK, 2 * KW), BF),
        pltpu.VMEM((4, GROUP * BLK, KEYS), BF),
        pltpu.VMEM((FW, D), BF),
        DMA((11, 4)),
        DMA((11, 4)),
        DMA((21,)),
        DMA((3, 11)),
        DMA((3, 11)),
        DMA((7,)),
        DMA((7,)),
        DMA((12,)),
        DMA((12,)),
        DMA((4,)),
        DMA((4,)),
        DMA((2, N_CTX)),
        DMA((NBLK,)),
        four,
        DMA((7,)),
        DMA((7,)),
        four,
    ]
    return pl.pallas_call(
        front_kernel,
        out_shape=outs,
        in_specs=[ANY, VM, VM, ANY, VM, ANY] + [VM] * 10,
        out_specs=[ANY] * 9 + [VM] * 4,
        scratch_shapes=scratch,
        compiler_params=pltpu.CompilerParams(collective_id=1, has_side_effects=True, vmem_limit_bytes=VMEM_LIMIT),
    )(idx, wq, wo, wg, wd, eext, n1, ub, cos, sin, low, x, gain, a45, a3, bo)


FSTEPS = 4
FROWS = 8 * ROWS // FSTEPS


def feed_kernel(idx, x, e, og, wd, ad_all, b_all, y_o, g_o, tiles_o, wg, wu, ad, bg, bu, acc, sem):
    piece = 2 * lax.axis_index("dp") + lax.rem(lax.div(lax.axis_index("ctx"), 4), 2)
    tile = window_tile(piece)
    o = FV * piece - 128 * tile
    step = pl.program_id(0)

    @pl.when(step == 0)
    def _():
        cols = pl.ds(pl.multiple_of(tile * 128, 128), FW)
        copies = []
        for q in range(4):
            w = wg if q < 2 else wu
            copies.append(pltpu.make_async_copy(og.at[q], w.at[:, pl.ds(640 * (q % 2), 640)], sem.at[q]))
        for s in range(4):
            rows, rows2 = pl.ds(R * s, R), pl.ds(64 + R * s, R)
            copies.append(pltpu.make_async_copy(ad_all.at[idx[s], :, cols], ad.at[rows], sem.at[4 + s]))
            copies.append(pltpu.make_async_copy(b_all.at[idx[s], 0, :, cols], bg.at[rows], sem.at[8 + s]))
            copies.append(pltpu.make_async_copy(b_all.at[idx[s], 1, :, cols], bu.at[rows2], sem.at[12 + s]))
        for c in copies:
            c.start()
        ad[64:] = jnp.zeros((64, FW), BF)
        bg[64:] = jnp.zeros((64, FW), BF)
        bu[:64] = jnp.zeros((64, FW), BF)
        acc[...] = jnp.zeros_like(acc)
        for c in copies:
            c.wait()
        col = iota((64, FW), 1)
        ad[:64] = jnp.where((col >= o) & (col < o + FV), ad[:64], jnp.zeros((), BF))

    n2, u = x[:, :D], x[:, D:]
    eo, gud = e[:, :D], e[:, D:]
    gate = mm(n2, wg[...]) + mm(u, bg[...])
    up = mm(n2, wu[...]) + mm(u, bu[...])
    gm = nt(eo, wd[...]) + mm(gud, ad[...])
    sig = 1.0 / (1.0 + jnp.exp(-gate))
    sl = gate * sig
    act = (sl * up).astype(BF)
    gg = (gm * up * (sig * (1.0 + gate * (1.0 - sig)))).astype(BF)
    gu = (gm * sl).astype(BF)
    y_o[:, :D] = mm(act, wd[...]).astype(BF)
    y_o[:, D:] = nt(act, ad[...]).astype(BF)
    g_o[:, :D] = (nt(gg, wg[...]) + nt(gu, wu[...])).astype(BF)
    g_o[:, D:] = (nt(gg, bg[...]) + nt(gu, bu[...])).astype(BF)
    acc[0] += tn(gud, act)[:64]
    acc[1] += tn(u, gg)[:64]
    acc[2] += tn(u, gu)[64:]

    @pl.when(step == FSTEPS - 1)
    def _():
        col = iota((64, FW), 1)
        valid = (col >= o) & (col < o + FV)
        for k in range(3):
            v = jnp.where(valid, acc[k], 0.0).astype(BF)
            for s in range(4):
                for t in range(10):
                    tiles_o[s * 30 + k * 10 + t] = v[R * s : R * (s + 1), 128 * t : 128 * (t + 1)]
        for t in range(120, 128):
            tiles_o[t] = jnp.zeros((R, 128), BF)


def feed(idx, x, e, og, wd, ad_all, b_all):
    outs = (sds((8 * ROWS, DX), BF), sds((8 * ROWS, DX), BF), sds((128, R, 128), BF))
    rows = pl.BlockSpec((FROWS, DX), lambda i, idx: (i, 0))
    return pl.pallas_call(
        feed_kernel,
        out_shape=outs,
        grid_spec=pltpu.PrefetchScalarGridSpec(
            num_scalar_prefetch=1,
            grid=(FSTEPS,),
            in_specs=[rows, rows, ANY, whole((FW, D)), ANY, ANY],
            out_specs=[rows, rows, whole((128, R, 128))],
            scratch_shapes=[
                pltpu.VMEM((D, FW), BF),
                pltpu.VMEM((D, FW), BF),
                pltpu.VMEM((EXT, FW), BF),
                pltpu.VMEM((EXT, FW), BF),
                pltpu.VMEM((EXT, FW), BF),
                pltpu.VMEM((3, 64, FW), F32),
                DMA((16,)),
            ],
        ),
        compiler_params=pltpu.CompilerParams(vmem_limit_bytes=VMEM_LIMIT),
    )(idx, x, e, og, wd, ad_all, b_all)


def scatter_kernel(part, out, own, got, got2, red, ls, cs, cr, ss, rs):
    me = Place()
    sib = me.sibling()
    greet(me.ring("z") + [sib])
    sends, mine = [], []
    for j in range(4):
        z = me.step("z", j)
        zl, zh = lax.rem(z, 2), lax.div(z, 2)
        c = remote(part.at[zl, 1 - me.core, zh], got.at[j], cs.at[j], cr.at[j], sib)
        c.start()
        sends.append(c)
        c = pltpu.make_async_copy(part.at[zl, me.core, zh], own.at[j], ls.at[j])
        c.start()
        mine.append(c)
    outs = []
    for j in (2, 1, 3, 0):
        sends[j].wait_recv()
        mine[j].wait()
        total = own[j].astype(F32) + got[j].astype(F32)
        if j == 0:
            out[...] = total
        else:
            red[j - 1] = total.astype(BF)
            c = remote(red.at[j - 1], got2.at[j - 1], ss.at[j - 1], rs.at[j - 1], me.at(z=me.step("z", j)))
            c.start()
            outs.append(c)
    for c in sends:
        c.wait_send()
    for j in (1, 3, 2):
        f = me.at(z=me.step("z", 4 - j))
        remote(red.at[j - 1], got2.at[j - 1], ss.at[j - 1], rs.at[j - 1], f).wait_recv()
        out[...] += got2[j - 1].astype(F32)
    for c in outs:
        c.wait_send()


def scatter(part, cid):
    return pl.pallas_call(
        scatter_kernel,
        out_shape=sds((ROWS, DX), F32),
        in_specs=[ANY],
        out_specs=VM,
        scratch_shapes=[
            pltpu.VMEM((4, ROWS, DX), BF),
            pltpu.VMEM((4, ROWS, DX), BF),
            pltpu.VMEM((3, ROWS, DX), BF),
            pltpu.VMEM((3, ROWS, DX), BF),
            DMA((4,)),
            DMA((4,)),
            DMA((4,)),
            DMA((3,)),
            DMA((3,)),
        ],
        compiler_params=pltpu.CompilerParams(collective_id=cid, has_side_effects=True, vmem_limit_bytes=VMEM_LIMIT),
    )(part)


def norm_back(z, gain, grad):
    r = rms(z)
    t = gain * grad
    return r * t - z * (r * r * r) * jnp.mean(t * z, -1, keepdims=True)


def back_kernel(
    idx, gn2, e, hid, n2, q, o, p, win, w_out, a_in, b_res, gain, a45,
    gh_o, gq_o, win_o, g45_o, gbo_o, ga3_o, go,
):
    s = lax.axis_index("dp")
    gue = gn2[:, D:].astype(BF)
    gn = gn2[:, :D] + mm(gue, a45[...])
    gh = e[:, :D].astype(F32) + norm_back(hid[...], gain[...].astype(F32), gn)
    gh_o[...] = gh
    ghb = gh.astype(BF)
    ob = o[...]
    gu3 = nt(ghb, b_res[0, 0]).astype(BF)
    go[...] = (nt(ghb, w_out[...]) + mm(gu3, a_in[0, 3])).astype(BF)
    u3 = nt(ob, a_in[0, 3]).astype(BF)
    gbo_o[...] = tn(u3, ghb)
    ga3_o[...] = tn(gu3, ob)
    g45_o[...] = tn(gue, n2[:, :D])
    for h in range(2):
        for a in range(KV_HEADS):
            qs, gs, os = stack_heads(q, h, a), stack_heads(go, h, a), stack_heads(o, h, a)
            k = win[h, :, :, a * HS : (a + 1) * HS].reshape(KEYS, HS)
            v = win[h, :, :, KW + a * HS : KW + (a + 1) * HS].reshape(KEYS, HS)
            pr = p[2 * h + a]
            delta = jnp.sum(gs.astype(F32) * os.astype(F32), -1, keepdims=True)
            ds = (pr.astype(F32) * (nt(gs, v) - delta)).astype(BF)
            gq = mm(ds, k) * SCALE
            for g in range(GROUP):
                gq_o[h * BLK : (h + 1) * BLK, (a * GROUP + g) * HS : (a * GROUP + g + 1) * HS] = gq[
                    g * BLK : (g + 1) * BLK
                ]
            win_o[h, :, :, a * HS : (a + 1) * HS] = (tn(ds, qs) * SCALE).astype(BF).reshape(NWB, BLK, HS)
            win_o[h, :, :, KW + a * HS : KW + (a + 1) * HS] = tn(pr, gs).astype(BF).reshape(NWB, BLK, HS)


def back(idx, gn2, e, hid, n2, q, o, p, win, w_out, a_in, b_res, gain, a45):
    outs = (
        sds((ROWS, D), F32),
        sds((ROWS, D), F32),
        sds((2, NWB, BLK, 2 * KW), BF),
        sds((EXT, D), F32),
        sds((R, D), F32),
        sds((R, D), F32),
    )
    return pl.pallas_call(
        back_kernel,
        out_shape=outs,
        grid_spec=pltpu.PrefetchScalarGridSpec(
            num_scalar_prefetch=1,
            grid=(1,),
            in_specs=[
                whole(gn2.shape),
                whole(e.shape),
                whole(hid.shape),
                whole(n2.shape),
                whole(q.shape),
                whole(o.shape),
                whole(p.shape),
                whole(win.shape),
                whole(w_out.shape),
                pick(a_in.shape),
                pick(b_res.shape),
                whole((D,)),
                whole(a45.shape),
            ],
            out_specs=[whole(x.shape) for x in outs],
            scratch_shapes=[pltpu.VMEM((ROWS, D), BF)],
        ),
        compiler_params=pltpu.CompilerParams(vmem_limit_bytes=VMEM_LIMIT),
    )(idx, gn2, e, hid, n2, q, o, p, win, w_out, a_in, b_res, gain, a45)


def return_kernel(win, out, got, ss, rs, ls):
    me = Place()
    m = me.ctx
    bar = pltpu.get_barrier_semaphore()

    def hello(t, carry):
        @pl.when(t != m)
        def _():
            pl.semaphore_signal(bar, inc=1, device_id=(me.dp, t), device_id_type=MESH)

        return carry

    lax.fori_loop(0, N_CTX, hello, 0)
    pl.semaphore_wait(bar, N_CTX - 1)

    def covers(t, w, owner, h):
        block = owner if h == 0 else NBLK - 1 - owner
        j = block - ((t if w == 0 else NBLK - 1 - t) - (NWB - 1))
        return j, (j >= 0) & (j < NWB)

    def send(k, carry):
        t = lax.rem(m + k, N_CTX)
        for w in range(2):
            for h in range(2):
                j, ok = covers(m, w, t, h)

                @pl.when(ok)
                def _():
                    remote(win.at[w, j], got.at[h, w, m], ss.at[h, w, t], rs.at[h, w, m], (me.dp, t)).start()

        return carry

    lax.fori_loop(1, N_CTX, send, 0)
    for w in range(2):
        for h in range(2):
            j, ok = covers(m, w, m, h)

            @pl.when(ok)
            def _():
                c = pltpu.make_async_copy(win.at[w, j], got.at[h, w, m], ls.at[h, w])
                c.start()
                c.wait()

    out[...] = jnp.zeros_like(out)

    def take(k, carry):
        t = lax.rem(m + N_CTX - k, N_CTX)
        for w in range(2):
            for h in range(2):
                _, ok = covers(t, w, m, h)

                @pl.when(ok & (k > 0))
                def _():
                    remote(got.at[h, w, t], got.at[h, w, t], ss.at[h, w, t], rs.at[h, w, t], (me.dp, t)).wait_recv()

                @pl.when(ok)
                def _():
                    out[h] += got[h, w, t].astype(F32)

        return carry

    lax.fori_loop(0, N_CTX, take, 0)

    def sent(k, carry):
        t = lax.rem(m + k, N_CTX)
        for w in range(2):
            for h in range(2):
                j, ok = covers(m, w, t, h)

                @pl.when(ok)
                def _():
                    remote(win.at[w, j], got.at[h, w, m], ss.at[h, w, t], rs.at[h, w, m], (me.dp, t)).wait_send()

        return carry

    lax.fori_loop(1, N_CTX, sent, 0)


def give_back(win):
    return pl.pallas_call(
        return_kernel,
        out_shape=sds((2, BLK, 2 * KW), F32),
        in_specs=[ANY],
        out_specs=VM,
        scratch_shapes=[
            pltpu.VMEM((2, 2, N_CTX, BLK, 2 * KW), BF),
            DMA((2, 2, N_CTX)),
            DMA((2, 2, N_CTX)),
            DMA((2, 2)),
        ],
        compiler_params=pltpu.CompilerParams(collective_id=5, has_side_effects=True, vmem_limit_bytes=VMEM_LIMIT),
    )(win)


def final_kernel(
    idx, gkv, gq, x, n1, gh, hid, y, e, w_qkv, a_in, b_qkv_ad, bd, gain, cos, sin, g45, gbo, ga3,
    out_o, gt_o, tiles_o, gj,
):
    s = lax.axis_index("dp")
    c, sn = cos[...], sin[...]
    for h in range(HEADS):
        cols = slice(h * HS, (h + 1) * HS)
        gj[:, cols] = turn_back(gq[:, cols], c, sn).astype(BF)
    for a in range(KV_HEADS):
        v = jnp.concatenate([gkv[0, :, a * HS : (a + 1) * HS], gkv[1, :, a * HS : (a + 1) * HS]], 0)
        gj[:, QW + a * HS : QW + (a + 1) * HS] = turn_back(v, c, sn).astype(BF)
    gj[:, QW + KW :] = jnp.concatenate([gkv[0, :, KW:], gkv[1, :, KW:]], 0).astype(BF)
    n1b = n1[...]
    gn = nt(gj[...], w_qkv[...])

    def put(at, v):
        for t in range(v.shape[1] // 128):
            tiles_o[at + t] = v[:, 128 * t : 128 * (t + 1)].astype(BF)

    at_qkv = 8 * 12
    for m, (lo, hi) in enumerate(((0, QW), (QW, QW + KW), (QW + KW, QW + 2 * KW))):
        am = a_in[0, m]
        u = nt(n1b, am).astype(BF)
        gjm = gj[:, lo:hi]
        gum = nt(gjm, b_qkv_ad[0, :, lo:hi]).astype(BF)
        gn += mm(gum, am)
        put(at_qkv + lo // 128, tn(u, gjm))
        put(12 * m, tn(gum, n1b))
    put(12 * 3, ga3[...])
    own = pl.multiple_of(s * R, R)
    put(12 * 4, g45[pl.ds(own, R), :])
    put(12 * 5, g45[pl.ds(own + 64, R), :])
    put(12 * 6, gbo[...])
    ud = y[:, D:].astype(BF)
    gbd = tn(ud, e[:, :D])
    own_bd = jnp.where((iota((R, EXT), 1) == iota((R, EXT), 0) + s * R), 1.0, 0.0)
    put(12 * 7, jnp.dot(own_bd, gbd, preferred_element_type=F32))
    for t in range(112, 128):
        tiles_o[t] = jnp.zeros((R, 128), BF)
    gt_o[...] = (gh[...] + norm_back(x[...].astype(F32), gain[...].astype(F32), gn)).astype(BF)
    out_o[...] = (hid[...] + y[:, :D] + mm(ud, bd[...])).astype(BF)


def final(idx, gkv, gq, x, n1, gh, hid, y, e, w_qkv, a_in, b_qkv_ad, bd, gain, cos, sin, g45, gbo, ga3):
    outs = (sds((ROWS, D), BF), sds((ROWS, D), BF), sds((128, R, 128), BF))
    args = (gkv, gq, x, n1, gh, hid, y, e, w_qkv, a_in, b_qkv_ad, bd, gain, cos, sin, g45, gbo, ga3)
    return pl.pallas_call(
        final_kernel,
        out_shape=outs,
        grid_spec=pltpu.PrefetchScalarGridSpec(
            num_scalar_prefetch=1,
            grid=(1,),
            in_specs=[pick(v.shape) if i in (9, 10) else whole(v.shape) for i, v in enumerate(args)],
            out_specs=[whole(x.shape) for x in outs],
            scratch_shapes=[pltpu.VMEM((ROWS, 2048), BF)],
        ),
        compiler_params=pltpu.CompilerParams(vmem_limit_bytes=VMEM_LIMIT),
    )(idx, *args)


def total_kernel(lt, ft, out, gl, gf, red, ls, s1, r1, s2, r2, ss, rs, cs, cr, s3, r3):
    me = Place()
    sib = me.sibling()
    m = me.ctx
    bar = pltpu.get_barrier_semaphore()

    def hello(t, carry):
        @pl.when(t != m)
        def _():
            pl.semaphore_signal(bar, inc=1, device_id=(me.dp, t), device_id_type=MESH)

        return carry

    lax.fori_loop(0, N_CTX, hello, 0)
    others = [me.at(z=me.step("z", 1)), me.at(z=me.step("z", 3)), sib]
    for d in others:
        pl.semaphore_signal(bar, inc=1, device_id=d, device_id_type=MESH)
    pl.semaphore_wait(bar, N_CTX - 1 + len(others))

    xy = me.y * 4 + me.x

    def plane(k):
        return me.at(x=lax.rem(k, 4), y=lax.div(k, 4))

    def send_l(k, carry):
        t = lax.rem(m + k, N_CTX)
        remote(lt.at[pl.ds(4 * t, 4)], gl.at[m], s1.at[t], r1.at[m], (me.dp, t)).start()
        return carry

    def send_f(k, carry):
        t = lax.rem(xy + k, 16)
        remote(ft.at[pl.ds(8 * t, 8)], gf.at[xy], s2.at[t], r2.at[xy], plane(t)).start()
        return carry

    lax.fori_loop(1, 16, send_f, 0)
    lax.fori_loop(1, N_CTX, send_l, 0)
    own = [
        pltpu.make_async_copy(lt.at[pl.ds(4 * m, 4)], gl.at[m], ls.at[0]),
        pltpu.make_async_copy(ft.at[pl.ds(8 * xy, 8)], gf.at[xy], ls.at[1]),
    ]
    for c in own:
        c.start()
    for c in own:
        c.wait()

    def got_f(k, carry):
        t = lax.rem(xy + k, 16)
        remote(gf.at[t], gf.at[t], s2.at[t], r2.at[t], plane(t)).wait_recv()
        return carry + gf[t].astype(F32)

    red[4:] = lax.fori_loop(1, 16, got_f, gf[xy].astype(F32)).astype(BF)

    def got_l(k, carry):
        t = lax.rem(m + k, N_CTX)
        remote(gl.at[t], gl.at[t], s1.at[t], r1.at[t], (me.dp, t)).wait_recv()
        return carry + gl[t].astype(F32)

    red[:4] = lax.fori_loop(1, N_CTX, got_l, gl[m].astype(F32)).astype(BF)

    def vz(j, h):
        ref = out.at[me.y, me.x, lax.rem(j, 2), me.core, lax.div(j, 2)]
        return ref if h is None else ref.at[pl.ds(6 * h, 6)]

    c = pltpu.make_async_copy(red, vz(me.z, None), ls.at[2])
    c.start()
    rz = Ring(me, "z", red, vz, ss.at[0], rs.at[0])
    rz.first()
    rz.second()
    rz.last()
    c.wait()

    def x0(j, h):
        ref = out.at[me.y, j, :, me.core, :, pl.ds(0, 6)]
        return ref if h is None else out.at[me.y, j, h, me.core, :, pl.ds(0, 6)]

    def y0(j, h):
        ref = out.at[j, :, :, me.core, :, pl.ds(0, 6)]
        return ref if h is None else out.at[j, pl.ds(2 * h, 2), :, me.core, :, pl.ds(0, 6)]

    def y1(j, h):
        ref = out.at[j, me.x, :, me.core, :, pl.ds(6, 6)]
        return ref if h is None else out.at[j, me.x, h, me.core, :, pl.ds(6, 6)]

    def x1(j, h):
        ref = out.at[:, j, :, me.core, :, pl.ds(6, 6)]
        return ref if h is None else out.at[pl.ds(2 * h, 2), j, :, me.core, :, pl.ds(6, 6)]

    ra = Ring(me, "x", x0(me.x, None), x0, ss.at[1], rs.at[1])
    rb = Ring(me, "y", y1(me.y, None), y1, ss.at[2], rs.at[2])
    for f in ("first", "second", "last"):
        getattr(ra, f)()
        getattr(rb, f)()
    rc = Ring(me, "y", y0(me.y, None), y0, ss.at[3], rs.at[3])
    rd = Ring(me, "x", x1(me.x, None), x1, ss.at[4], rs.at[4])
    for f in ("first", "second", "last"):
        getattr(rc, f)()
        getattr(rd, f)()
    swaps = []
    for y in range(4):
        ref = out.at[y, :, :, me.core]
        k = remote(ref, ref, cs.at[y], cr.at[y], sib)
        k.start()
        swaps.append(k)
    for r in (rz, ra, rb, rc, rd):
        r.sent()

    def sent_l(k, carry):
        t = lax.rem(m + k, N_CTX)
        remote(lt.at[pl.ds(4 * t, 4)], gl.at[m], s1.at[t], r1.at[m], (me.dp, t)).wait_send()
        return carry

    def sent_f(k, carry):
        t = lax.rem(xy + k, 16)
        remote(ft.at[pl.ds(8 * t, 8)], gf.at[xy], s2.at[t], r2.at[xy], plane(t)).wait_send()
        return carry

    lax.fori_loop(1, 16, sent_f, 0)
    lax.fori_loop(1, N_CTX, sent_l, 0)
    for y in range(4):
        swaps[y].wait_send()
        ref = out.at[y, :, :, 1 - me.core]
        remote(ref, ref, cs.at[y], cr.at[y], sib).wait_recv()


def total(lt, ft):
    return pl.pallas_call(
        total_kernel,
        out_shape=sds((4, 4, 2, 2, 2, 12, R, 128), BF),
        in_specs=[ANY] * 2,
        out_specs=ANY,
        scratch_shapes=[
            pltpu.VMEM((N_CTX, 4, R, 128), BF),
            pltpu.VMEM((16, 8, R, 128), BF),
            pltpu.VMEM((12, R, 128), BF),
            DMA((3,)),
            DMA((N_CTX,)),
            DMA((N_CTX,)),
            DMA((16,)),
            DMA((16,)),
            DMA((5, 4)),
            DMA((5, 4)),
            DMA((4,)),
            DMA((4,)),
            DMA((1,)),
            DMA((1,)),
        ],
        compiler_params=pltpu.CompilerParams(collective_id=6, has_side_effects=True, vmem_limit_bytes=VMEM_LIMIT),
    )(lt, ft)


def spread_kernel(idx, t, ain_o, aff_o, bqkv_o, bres_o, bff_o):
    e = pl.program_id(0)
    for ref in (ain_o, aff_o, bqkv_o, bres_o, bff_o):
        ref[...] = jnp.zeros_like(ref)

    def local_tile(s, n):
        k, j = n // 4, n % 4
        y, zh, x = k // 8, (k // 4) % 2, k % 4
        return t[y, x, s // 2, s % 2, zh, j].astype(F32)

    def ff_tile(piece, n):
        k, j = n // 8, n % 8
        return t[k // 4, k % 4, piece // 4, (piece // 2) % 2, piece % 2, 4 + j].astype(F32)

    for s in range(4):

        @pl.when(idx[s] == e)
        def _():
            for m in range(6):
                for c in range(12):
                    ain_o[0, m, :, 128 * c : 128 * (c + 1)] += local_tile(s, 12 * m + c)
            for m in range(2):
                for c in range(12):
                    bres_o[0, m, :, 128 * c : 128 * (c + 1)] += local_tile(s, 12 * (6 + m) + c)
            for c in range(16):
                bqkv_o[0, :, 128 * c : 128 * (c + 1)] += local_tile(s, 96 + c)
            for piece in range(8):
                tile = 60 if piece == 7 else 35 * piece // 4
                for k in range(3):
                    for c in range(10):
                        cols = slice(128 * (tile + c), 128 * (tile + c + 1))
                        v = ff_tile(piece, s * 30 + k * 10 + c)
                        if k == 0:
                            aff_o[0, :, cols] += v
                        else:
                            bff_o[0, k - 1, :, cols] += v


def spread(idx, t):
    outs = (
        sds((ADAPT, 6, R, D), F32),
        sds((ADAPT, R, FF), F32),
        sds((ADAPT, R, 2048), F32),
        sds((ADAPT, 2, R, D), F32),
        sds((ADAPT, 2, R, FF), F32),
    )

    def one(shape):
        return pl.BlockSpec((1,) + shape[1:], lambda i, idx: (i,) + (0,) * (len(shape) - 1))

    return pl.pallas_call(
        spread_kernel,
        out_shape=outs,
        grid_spec=pltpu.PrefetchScalarGridSpec(
            num_scalar_prefetch=1,
            grid=(ADAPT,),
            in_specs=[whole(t.shape)],
            out_specs=[one(o.shape) for o in outs],
        ),
        compiler_params=pltpu.CompilerParams(vmem_limit_bytes=VMEM_LIMIT),
    )(idx, t)


def local(
    tokens,
    cotangent,
    w_qkv,
    b_qkv,
    w_out,
    w_gu,
    w_down,
    gain_attn,
    gain_mlp,
    adapt_in,
    adapt_in_ff,
    adapt_out_qkv,
    adapt_out_res,
    adapt_out_ff,
    doc_lengths,
    adapter_index,
    window,
):
    member = lax.axis_index("ctx")
    starts = jnp.stack([member * BLK, (NBLK - 1 - member) * BLK])
    pos = (starts[:, None] + jnp.arange(BLK, dtype=jnp.int32)[None]).reshape(ROWS)
    ends = jnp.cumsum(doc_lengths[0])
    begin = jnp.max(jnp.where(ends[None] <= pos[:, None], ends[None], 0), -1)
    low = jnp.maximum(begin, pos - window[0] + 1)
    low = jnp.broadcast_to(low[:, None], (ROWS, 128)).astype(jnp.int32)
    freq = 1000000.0 ** (-(2.0 * jnp.arange(HS // 2, dtype=F32)) / HS)
    ang = pos.astype(F32)[:, None] * freq[None]
    c, sn = jnp.cos(ang), jnp.sin(ang)
    cos = jnp.concatenate([c, c], -1)
    sin = jnp.concatenate([-sn, sn], -1)

    wg = jnp.pad(jnp.transpose(w_gu, (1, 0, 2)), ((0, 0), (0, 4), (0, 0)))
    idx_row = jnp.broadcast_to(adapter_index[:, None], (8, 128)).astype(jnp.int32)

    x, n1, eext, ub, a45, bd, a3, bo = prepare(
        adapter_index, tokens[0], cotangent[0], adapt_in, adapt_out_qkv, adapt_out_res, gain_attn, b_qkv
    )
    oq, oo, og, down, oe, oi, wins, p, xg, q, o, hid, n2 = front(
        idx_row, w_qkv, w_out, wg, w_down, eext, n1, ub, cos, sin, low, x, gain_mlp, a45, a3, bo
    )
    oq = oq.reshape(D, 2048)
    oo = oo.reshape(D, D)
    og = og.reshape(4, D, 640)
    idx4 = oi[:, 0, 0, 0]
    xg = xg.reshape(8 * ROWS, DX)
    yp, gp, ft = feed(idx4, xg, oe.reshape(8 * ROWS, DX), og, down, adapt_in_ff, adapt_out_ff)
    gn2 = scatter(gp.reshape(2, 2, 2, ROWS, DX), 4)
    gh, gq, win, g45, gbo, ga3 = back(
        adapter_index, gn2, eext, hid, n2, q, o, p, wins, oo, adapt_in, adapt_out_res, gain_mlp, a45
    )
    y = scatter(yp.reshape(2, 2, 2, ROWS, DX), 4)
    gkv = give_back(win)
    out, gt, lt = final(
        adapter_index, gkv, gq, x, n1, gh, hid, y, eext, oq, adapt_in, adapt_out_qkv, bd, gain_attn, cos, sin, g45, gbo, ga3
    )
    tiles = total(lt, ft)
    grads = spread(idx4, tiles)

    def deal(v):
        return jnp.transpose(v.reshape(2, BLK, D), (1, 0, 2))[None]

    return (deal(out), deal(gt)) + tuple(grads)


def solution(mesh):
    return jax.shard_map(
        local,
        mesh=mesh,
        in_specs=(
            P("dp", "ctx", None, None),
            P("dp", "ctx", None, None),
            P(("dp", "ctx"), None),
            P(),
            P(("dp", "ctx"), None),
            P(("dp", "ctx"), None, None),
            P(("dp", "ctx"), None),
            P(),
            P(),
            P(),
            P(),
            P(),
            P(),
            P(),
            P("dp", None),
            P("dp"),
            P("dp"),
        ),
        out_specs=(P("dp", "ctx", None, None), P("dp", "ctx", None, None), P(), P(), P(), P(), P()),
        check_vma=False,
    )
```

```python
import functools

import jax
import jax.numpy as jnp
from jax import lax
from jax.experimental import pallas as pl
from jax.experimental.pallas import tpu as pltpu
from jax.sharding import PartitionSpec as P

D = 1536
HEADS = 12
KV_HEADS = 2
HS = 128
GROUP = HEADS // KV_HEADS
FF = 8960
R = 16
ADAPT = 8
BLK = 64
ROWS = 2 * BLK
N_CTX = 32
NBLK = 2 * N_CTX
WIN = 1024
NWB = WIN // BLK + 1
KEYS = NWB * BLK
EXT = 128
DX = D + EXT
FW = 1280
FV = FF // 8
QW = HEADS * HS
KW = KV_HEADS * HS
SCALE = HS**-0.5
EPS = 1e-6

MESH = pl.DeviceIdType.MESH
BF = jnp.bfloat16
F32 = jnp.float32
ANY = pl.BlockSpec(memory_space=pl.ANY)
VM = pl.BlockSpec(memory_space=pltpu.VMEM)
SM = pl.BlockSpec(memory_space=pltpu.SMEM)
DMA = pltpu.SemaphoreType.DMA
VMEM_LIMIT = 60 * 2**20


def sds(shape, dtype):
    return jax.ShapeDtypeStruct(shape, dtype)


def nt(a, b):
    return lax.dot_general(a, b, (((1,), (1,)), ((), ())), preferred_element_type=F32)


def tn(a, b):
    return lax.dot_general(a, b, (((0,), (0,)), ((), ())), preferred_element_type=F32)


def mm(a, b):
    return jnp.dot(a, b, preferred_element_type=F32)


def iota(shape, dim):
    return lax.broadcasted_iota(jnp.int32, shape, dim)


class Place:
    def __init__(self):
        dp, ctx = lax.axis_index("dp"), lax.axis_index("ctx")
        self.dp, self.ctx = dp, ctx
        self.zlo, self.core = lax.div(dp, 2), lax.rem(dp, 2)
        self.y, self.zhi, self.x = lax.div(ctx, 8), lax.rem(lax.div(ctx, 4), 2), lax.rem(ctx, 4)
        self.z = self.zhi * 2 + self.zlo
        self.slice = 2 * dp + self.zhi

    def at(self, x=None, y=None, z=None, core=None):
        x = self.x if x is None else x
        y = self.y if y is None else y
        z = self.z if z is None else z
        core = self.core if core is None else core
        return (lax.rem(z, 2) * 2 + core, y * 8 + lax.div(z, 2) * 4 + x)

    def step(self, axis, by):
        return lax.rem(getattr(self, axis) + by, 4)

    def ring(self, axis):
        return [self.at(**{axis: self.step(axis, k)}) for k in (1, 2, 3)]

    def sibling(self):
        return self.at(core=1 - self.core)


def window_tile(piece):
    return jnp.minimum(lax.div(35 * piece, 4), 60)


def remote(src, dst, send, recv, device):
    return pltpu.make_async_remote_copy(
        src_ref=src, dst_ref=dst, send_sem=send, recv_sem=recv, device_id=device, device_id_type=MESH
    )


def greet(peers):
    sem = pltpu.get_barrier_semaphore()
    for device in peers:
        pl.semaphore_signal(sem, inc=1, device_id=device, device_id_type=MESH)
    pl.semaphore_wait(sem, len(peers))


class Ring:
    def __init__(self, me, axis, own, view, send, recv):
        self.i = getattr(me, axis)
        self.r, self.o, self.l = (me.step(axis, k) for k in (1, 2, 3))
        self.right, self.left = me.at(**{axis: self.r}), me.at(**{axis: self.l})
        self.own, self.view, self.send, self.recv = own, view, send, recv

    def copy(self, k, src, dst, device):
        return remote(src, dst, self.send.at[k], self.recv.at[k], device)

    def first(self):
        place = self.view(self.i, None)
        self.out = [self.copy(0, self.own, place, self.right), self.copy(1, self.own, place, self.left)]
        for c in self.out:
            c.start()

    def second(self):
        v = self.view
        self.copy(0, v(self.l, None), v(self.l, None), self.right).wait_recv()
        c = self.copy(2, v(self.l, 0), v(self.l, 0), self.right)
        c.start()
        self.out.append(c)
        self.copy(1, v(self.r, None), v(self.r, None), self.left).wait_recv()
        c = self.copy(3, v(self.r, 1), v(self.r, 1), self.left)
        c.start()
        self.out.append(c)

    def last(self):
        v = self.view
        self.copy(2, v(self.o, 0), v(self.o, 0), self.right).wait_recv()
        self.copy(3, v(self.o, 1), v(self.o, 1), self.left).wait_recv()

    def sent(self):
        for c in self.out:
            c.wait_send()


class ZGather:
    def __init__(self, me, own, buf, send, recv, core_send, core_recv, half):
        self.me, self.own, self.buf = me, own, buf
        self.cs, self.cr = core_send, core_recv

        def view(j, h, core=me.core):
            ref = buf.at[lax.rem(j, 2), core, lax.div(j, 2)]
            return ref if h is None else ref.at[pl.ds(h * half, half)]

        self.view = view
        self.ring = Ring(me, "z", own, view, send, recv)
        self.out = []

    def swap(self, src, j):
        c = remote(src, self.view(j, None), self.cs.at[len(self.out)], self.cr.at[len(self.out)], self.me.sibling())
        c.start()
        self.out.append((c, j))

    def first(self):
        self.ring.first()
        self.swap(self.own, self.me.z)

    def second(self):
        self.ring.second()
        self.swap(self.view(self.ring.l, None), self.ring.l)
        self.swap(self.view(self.ring.r, None), self.ring.r)

    def last(self):
        self.ring.last()
        self.swap(self.view(self.ring.o, None), self.ring.o)

    def finish(self):
        self.ring.sent()
        for k, (c, j) in enumerate(self.out):
            c.wait_send()
            place = self.view(j, None, 1 - self.me.core)
            remote(place, place, self.cs.at[k], self.cr.at[k], self.me.sibling()).wait_recv()


def rms(z):
    return lax.rsqrt(jnp.mean(z * z, -1, keepdims=True) + EPS)


def prepare_kernel(idx, tok, cot, a_in, b_qkv_ad, b_res, gain, bias, x_o, n1_o, e_o, ub_o, a45_o, bd_o, a3_o, bo_o, a012_o, bqkv_o):
    s = lax.axis_index("dp")
    for h in range(2):
        rows = slice(h * BLK, (h + 1) * BLK)
        x_o[rows] = tok[:, h, :]
        e_o[rows, :D] = cot[:, h, :]
    x = x_o[...].astype(F32)
    n1 = (x * rms(x) * gain[...].astype(F32)).astype(BF)
    n1_o[...] = n1
    for m, (lo, hi) in enumerate(((0, QW), (QW, QW + KW), (QW + KW, QW + 2 * KW))):
        u = nt(n1, a_in[0, m]).astype(BF)
        ub_o[:, lo:hi] = mm(u, b_qkv_ad[0, :, lo:hi]) + bias[lo:hi].astype(F32)
    at = pl.multiple_of(s * R, R)
    a45_o[...] = jnp.zeros_like(a45_o)
    a45_o[pl.ds(at, R), :] = a_in[0, 4]
    a45_o[pl.ds(at + 64, R), :] = a_in[0, 5]
    bd_o[...] = jnp.zeros_like(bd_o)
    bd_o[pl.ds(at, R), :] = b_res[0, 1]
    a3_o[...] = a_in[0, 3]
    bo_o[...] = b_res[0, 0]
    a012_o[...] = a_in[0, :3]
    bqkv_o[...] = b_qkv_ad[0]
    e_o[:, D:] = nt(e_o[:, :D], bd_o[...]).astype(BF)


def pick(shape):
    return pl.BlockSpec((1,) + shape[1:], lambda i, idx: (idx[0],) + (0,) * (len(shape) - 1))


def whole(shape):
    return pl.BlockSpec(shape, lambda i, idx: (0,) * len(shape))


def prepare(idx, tok, cot, a_in, b_qkv_ad, b_res, gain, bias):
    outs = (
        sds((ROWS, D), BF),
        sds((ROWS, D), BF),
        sds((ROWS, DX), BF),
        sds((ROWS, 2048), F32),
        sds((EXT, D), BF),
        sds((EXT, D), BF),
        sds((R, D), BF),
        sds((R, D), BF),
        sds((3, R, D), BF),
        sds((R, 2048), BF),
    )
    return pl.pallas_call(
        prepare_kernel,
        out_shape=outs,
        grid_spec=pltpu.PrefetchScalarGridSpec(
            num_scalar_prefetch=1,
            grid=(1,),
            in_specs=[
                whole((BLK, 2, D)),
                whole((BLK, 2, D)),
                pick(a_in.shape),
                pick(b_qkv_ad.shape),
                pick(b_res.shape),
                whole((D,)),
                whole((2048,)),
            ],
            out_specs=[whole(o.shape) for o in outs],
        ),
        compiler_params=pltpu.CompilerParams(vmem_limit_bytes=VMEM_LIMIT),
    )(idx, tok, cot, a_in, b_qkv_ad, b_res, gain, bias)


def turn(v, cos, sin):
    return v * cos + pltpu.roll(v, 64, 1) * sin


def turn_back(v, cos, sin):
    return v * cos - pltpu.roll(v, 64, 1) * sin


def stack_heads(ref, h, a):
    rows = slice(h * BLK, (h + 1) * BLK)
    return jnp.concatenate(
        [ref[rows, (a * GROUP + g) * HS : (a * GROUP + g + 1) * HS] for g in range(GROUP)], 0
    )


def reads(t, block):
    a, b = t - block, NBLK - 1 - t - block
    return ((a >= 0) & (a < NWB)) | ((b >= 0) & (b < NWB))


ZK = [(dz, dc) for dz in range(4) for dc in range(2) if dz or dc]


def front_kernel(
    idx, wq_i, wo_i, wg, wd_i, eext, n1, ub, cos, sin, low, x, gain, a45, a3, bo,
    oq_o, oo_o, og, od_o, oe, oi, win_o, p_o, xg, q, o_o, hid_o, n2,
    rq, ro, rg, wdp, rd, cq, co, cg, oq, oo, od, kv_own, kv, p, down, pick70,
    ss, rs, ls, s1, r1, s2, r2, sc, rc, sd, rdn, sk, rk, ez_sems, si, ri, nz_sems,
):
    me = Place()
    sib = me.sibling()
    m = me.ctx
    bar = pltpu.get_barrier_semaphore()

    def hello(t, carry):
        @pl.when(t != m)
        def _():
            pl.semaphore_signal(bar, inc=1, device_id=(me.dp, t), device_id_type=MESH)

        return carry

    lax.fori_loop(0, N_CTX, hello, 0)
    others = [me.at(z=me.step("z", dz), core=lax.rem(me.core + dc, 2)) for dz, dc in ZK if dz % 2 or dc]
    for d in others:
        pl.semaphore_signal(bar, inc=1, device_id=d, device_id_type=MESH)

    rq[me.x, :12] = wq_i[...]
    rq[me.x, 12:] = jnp.zeros((4, 2048), BF)
    ro[me.x, :12] = wo_i[...]
    ro[me.x, 12:] = jnp.zeros((4, D), BF)
    wdp[:70] = wd_i[...]
    wdp[70:] = jnp.zeros((10, D), BF)
    kv[:16] = jnp.zeros((16, BLK, 2 * KW), BF)

    pl.semaphore_wait(bar, N_CTX - 1 + len(others))

    tiles = [60 if g == 7 else 35 * g // 4 for g in range(8)]

    def panel(g, t):
        col = pl.multiple_of(tiles[g] * 128 + lax.rem(t, 2) * 640, 128)
        return wg.at[lax.div(t, 2), :, pl.ds(col, 640)]

    def strip(t):
        return wdp.at[:, pl.ds(pl.multiple_of(384 * t, 128), 384)]

    def start(c, out):
        c.start()
        out.append(c)

    first = []
    xs = [(k, me.step("x", k), me.at(x=me.step("x", k))) for k in (1, 3, 2)]
    for k, t, d in xs:
        start(remote(rq.at[me.x], rq.at[me.x], s1.at[k - 1, 0], r1.at[k - 1, 0], d), first)
    for k, t, d in xs:
        start(remote(ro.at[me.x], ro.at[me.x], s1.at[k - 1, 1], r1.at[k - 1, 1], d), first)
    for k, t, d in xs:
        for g in range(8):
            start(remote(panel(g, t), rg.at[me.x, g], s1.at[k - 1, 2 + g], r1.at[k - 1, 2 + g], d), first)
        start(remote(strip(t), rd.at[me.x], s1.at[k - 1, 10], r1.at[k - 1, 10], d), first)
    mine = []
    for g in range(8):
        start(pltpu.make_async_copy(panel(g, me.x), rg.at[me.x, g], ls.at[2 + g]), mine)
    start(pltpu.make_async_copy(strip(me.x), rd.at[me.x], ls.at[1]), mine)
    side = []
    start(pltpu.make_async_copy(eext, oe.at[me.zlo, me.core, me.zhi], ls.at[10]), side)
    start(pltpu.make_async_copy(idx, oi.at[me.dp, me.zhi], ls.at[11]), side)
    for n, (dz, dc) in enumerate(ZK):
        d = me.at(z=me.step("z", dz), core=lax.rem(me.core + dc, 2))
        start(remote(idx, oi.at[me.dp, me.zhi], si.at[n], ri.at[n], d), first)

    def from_x(n, ref_of):
        for k in (1, 3, 2):
            f = me.step("x", 4 - k)
            ref = ref_of(f)
            remote(ref, ref, s1.at[k - 1, n], r1.at[k - 1, n], me.at(x=f)).wait_recv()

    row, col = iota((48, 64), 0), iota((48, 64), 1)
    put = jnp.where(
        (lax.rem(col, 16) < 12) & (lax.div(col, 16) * 12 + lax.rem(col, 16) == row), 1.0, 0.0
    ).astype(BF)

    from_x(0, lambda f: rq.at[f])
    cq[...] = mm(put, rq[...].reshape(64, 2048)).astype(BF)
    lo, hi = pl.ds(0, 1024), pl.ds(1024, 1024)

    def qy0(j, h):
        return oq.at[me.zlo, me.core, j, me.zhi, :, lo if h is None else pl.ds(512 * h, 512)]

    def qz0(j, h, core=me.core):
        zl, zh = lax.rem(j, 2), lax.div(j, 2)
        return oq.at[zl, core, :, zh, :, lo] if h is None else oq.at[zl, core, pl.ds(2 * h, 2), zh, :, lo]

    def qz1(j, h):
        cols = hi if h is None else pl.ds(1024 + 512 * h, 512)
        return oq.at[lax.rem(j, 2), me.core, me.y, lax.div(j, 2), :, cols]

    def qy1(j, h, core=me.core):
        return oq.at[:, core, j, :, :, hi] if h is None else oq.at[h, core, j, :, :, hi]

    qa = Ring(me, "y", cq.at[:, lo], qy0, ss.at[0], rs.at[0])
    qb = Ring(me, "z", cq.at[:, hi], qz1, ss.at[1], rs.at[1])
    qa.first()
    qb.first()
    oq[me.zlo, me.core, me.y, me.zhi] = cq[...]
    from_x(1, lambda f: ro.at[f])
    co[...] = mm(put, ro[...].reshape(64, D)).astype(BF)
    qa.second()
    qb.second()
    for n in range(8):
        from_x(2 + n, lambda f: rg.at[f, n])
    from_x(10, lambda f: rd.at[f])
    for c in mine:
        c.wait()
    for g in range(8):
        cg[g] = mm(put, rg[:, g].reshape(64, 640)).astype(BF)

    own_g = pltpu.make_async_copy(cg.at[me.slice], og.at[me.x, me.zlo, me.core, me.y, me.zhi], ls.at[14])
    own_g.start()
    zc = []
    for n, (dz, dc) in enumerate(ZK):
        z, core = me.step("z", dz), lax.rem(me.core + dc, 2)
        piece = 2 * (2 * lax.rem(z, 2) + core) + lax.div(z, 2)
        d = me.at(z=z, core=core)
        start(remote(cg.at[piece], og.at[me.x, me.zlo, me.core, me.y, me.zhi], s2.at[n], r2.at[n], d), zc)
    keeper = lax.div(me.y, 2) == me.zhi
    rows4 = pl.ds(lax.rem(me.y, 2) * 8 + me.zhi * 4, 4)
    across = me.at(z=me.step("z", 2))
    d_local = pltpu.make_async_copy(rd, od.at[me.x, rows4], ls.at[15])
    d_cross = remote(rd, od.at[me.x, rows4], sd.at[0], rdn.at[0], across)

    @pl.when(keeper)
    def _():
        d_local.start()

    @pl.when(jnp.logical_not(keeper))
    def _():
        d_cross.start()

    qa.last()
    qb.last()
    qa2 = Ring(me, "z", qz0(me.z, None), qz0, ss.at[2], rs.at[2])
    qb2 = Ring(me, "y", qy1(me.y, None), qy1, ss.at[3], rs.at[3])
    qa2.first()
    qb2.first()
    swaps = []

    def swap(view, j):
        n = len(swaps)
        c = remote(view(j, None), view(j, None), sc.at[n], rc.at[n], sib)
        c.start()
        swaps.append((c, view, j))

    def swapped(n):
        c, view, j = swaps[n]
        c.wait_send()
        ref = view(j, None, 1 - me.core)
        remote(ref, ref, sc.at[n], rc.at[n], sib).wait_recv()

    swap(qz0, me.z)
    swap(qy1, me.y)
    own_g.wait()
    for n, (dz, dc) in enumerate(ZK):
        z, core = me.step("z", 4 - dz if dz else 0), lax.rem(me.core + dc, 2)
        ref = og.at[me.x, lax.rem(z, 2), core, me.y, lax.div(z, 2)]
        remote(ref, ref, s2.at[n], r2.at[n], me.at(z=z, core=core)).wait_recv()

    def g0a(j, h):
        return og.at[me.x, 0, :, j] if h is None else og.at[me.x, 0, h, j]

    def g0b(j, h):
        return og.at[j, 0] if h is None else og.at[j, 0, h]

    def g1a(j, h):
        return og.at[j, 1, :, me.y] if h is None else og.at[j, 1, h, me.y]

    def g1b(j, h):
        return og.at[:, 1, :, j] if h is None else og.at[:, 1, h, j]

    ga = Ring(me, "y", g0a(me.y, None), g0a, ss.at[4], rs.at[4])
    gb = Ring(me, "x", g1a(me.x, None), g1a, ss.at[5], rs.at[5])
    ga.first()
    gb.first()
    def oy(j, h):
        ref = oo.at[me.zlo, me.core, j, me.zhi]
        return ref if h is None else ref.at[:, pl.ds(768 * h, 768)]

    def oz(j, h, core=me.core):
        zl, zh = lax.rem(j, 2), lax.div(j, 2)
        return oo.at[zl, core, :, zh] if h is None else oo.at[zl, core, pl.ds(2 * h, 2), zh]

    wa = Ring(me, "y", co, oy, ss.at[8], rs.at[8])
    qa2.second()
    qb2.second()
    swap(qz0, qa2.l)
    swap(qy1, qb2.l)
    swap(qz0, qa2.r)
    swap(qy1, qb2.r)
    oo[me.zlo, me.core, me.y, me.zhi] = co[...]

    ga.second()
    gb.second()
    wa.first()
    qa2.last()
    qb2.last()
    swap(qz0, qa2.o)
    swap(qy1, qb2.o)

    wa.second()
    rows4b = pl.ds(lax.rem(me.y, 2) * 8 + (1 - me.zhi) * 4, 4)
    rows8 = pl.ds(lax.rem(me.y, 2) * 8, 8)
    ys = [(k, me.step("y", k)) for k in (1, 3, 2)]

    @pl.when(keeper)
    def _():
        d_local.wait()
        ref = od.at[me.x, rows4b]
        remote(rd, ref, sd.at[0], rdn.at[0], across).wait_recv()
        for k, t in ys:
            remote(od.at[me.x, rows8], od.at[me.x, rows8], sd.at[k], rdn.at[k], me.at(y=t)).start()

    ga.last()
    gb.last()
    ga2 = Ring(me, "x", g0b(me.x, None), g0b, ss.at[6], rs.at[6])
    gb2 = Ring(me, "y", g1b(me.y, None), g1b, ss.at[7], rs.at[7])

    ga2.first()
    for n in range(8):
        swapped(n)
    keep_q = pltpu.make_async_copy(oq, oq_o, ls.at[12])
    keep_q.start()

    c, s = cos[...], sin[...]
    n1v = n1[...]
    for h in (12, 14, 0, 2, 4, 6, 8, 10):
        pair = slice(h * HS, (h + 2) * HS)
        j = mm(n1v, oq[:, :, :, :, :, pair].reshape(D, 2 * HS)) + ub[:, pair]
        for i in range(2):
            v = j[:, i * HS : (i + 1) * HS]
            if h + i < HEADS + KV_HEADS:
                v = turn(v, c, s)
            v = v.astype(BF)
            if h + i < HEADS:
                q[:, (h + i) * HS : (h + i + 1) * HS] = v
            else:
                at = slice((h + i - HEADS) * HS, (h + i - HEADS + 1) * HS)
                kv_own[0, :, at] = v[:BLK]
                kv_own[1, :, at] = v[BLK:]
        if h == 14:
            def send(k, carry):
                t = lax.rem(m + k, N_CTX)
                for half in range(2):
                    block = m if half == 0 else NBLK - 1 - m

                    @pl.when(reads(t, block))
                    def _():
                        src, dst = kv_own.at[half], kv.at[16 + block]
                        remote(src, dst, sk.at[half, k], rk.at[block], (me.dp, t)).start()

                return carry

            lax.fori_loop(1, N_CTX, send, 0)
            kv[16 + m] = kv_own[0]
            kv[16 + NBLK - 1 - m] = kv_own[1]

    gb2.first()
    wa.last()
    wb = Ring(me, "z", oz(me.z, None), oz, ss.at[9], rs.at[9])
    wb.first()
    swap(oz, me.z)
    ez = ZGather(me, eext, oe, *ez_sems, BLK)
    ez.first()
    def dx(j, h):
        return od.at[j] if h is None else od.at[j, pl.ds(8 * h, 8)]

    def arrived(block):
        src = jnp.where(block < N_CTX, block, NBLK - 1 - block)
        remote(kv_own.at[0], kv.at[16 + block], sk.at[0, 0], rk.at[block], (me.dp, src)).wait_recv()

    def near0(j, carry):
        block = m - (NWB - 1) + j

        @pl.when(block >= 0)
        def _():
            arrived(block)

        return carry

    def near1(j, carry):
        block = NBLK - 1 - m - (NWB - 1) + j

        @pl.when(block > m)
        def _():
            arrived(block)

        return carry

    wins = []
    keep_p = []
    for h in range(2):
        lax.fori_loop(0, NWB - 1, near0 if h == 0 else near1, 0)
        win = kv.at[pl.ds(m if h == 0 else NBLK - 1 - m, NWB)]
        start(pltpu.make_async_copy(win, win_o.at[h], ls.at[16 + h]), wins)
        base = (m if h == 0 else NBLK - 1 - m) * BLK
        kpos = base - WIN + iota((BLK, KEYS), 1)
        qpos = base + iota((BLK, KEYS), 0)
        keep = (kpos <= qpos) & (kpos >= low[h * BLK : (h + 1) * BLK, :1])
        for a in range(KV_HEADS):
            qs = stack_heads(q, h, a)
            k = win[:, :, a * HS : (a + 1) * HS].reshape(KEYS, HS)
            v = win[:, :, KW + a * HS : KW + (a + 1) * HS].reshape(KEYS, HS)
            sco = nt(qs, k) * SCALE
            sco = jnp.where(keep[None], sco.reshape(GROUP, BLK, KEYS), -1e30)
            e = jnp.exp(sco - jnp.max(sco, -1, keepdims=True))
            pr = (e / jnp.sum(e, -1, keepdims=True)).astype(BF).reshape(GROUP * BLK, KEYS)
            p[2 * h + a] = pr
            o = mm(pr, v).astype(BF)
            for g in range(GROUP):
                o_o[h * BLK : (h + 1) * BLK, (a * GROUP + g) * HS : (a * GROUP + g + 1) * HS] = o[
                    g * BLK : (g + 1) * BLK
                ]
        if h == 0:
            for k, t in ys:
                f = me.step("y", 4 - k)

                @pl.when(lax.div(f, 2) == me.zhi)
                def _():
                    ref = od.at[me.x, pl.ds(lax.rem(f, 2) * 8, 8)]
                    remote(ref, ref, sd.at[k], rdn.at[k], me.at(y=f)).wait_recv()

            da = Ring(me, "x", od.at[me.x], dx, ss.at[10], rs.at[10])
            da.first()
            wb.second()
            swap(oz, wb.l)
            swap(oz, wb.r)
            ez.second()
            ga2.second()

    start(pltpu.make_async_copy(p, p_o, ls.at[18]), keep_p)
    wb.last()
    swap(oz, wb.o)
    for n in range(8, 12):
        swapped(n)
    keep_o = pltpu.make_async_copy(oo, oo_o, ls.at[13])
    keep_o.start()

    ob = o_o[...]
    u3 = nt(ob, a3[...]).astype(BF)
    hid = x[...].astype(F32) + mm(ob, oo[...].reshape(D, D)) + mm(u3, bo[...])
    hid_o[...] = hid
    nv = (hid * rms(hid) * gain[...].astype(F32)).astype(BF)
    n2[:, :D] = nv
    n2[:, D:] = nt(nv, a45[...]).astype(BF)
    nz = ZGather(me, n2, xg, *nz_sems, BLK)
    nz.first()
    start(pltpu.make_async_copy(n2, xg.at[me.zlo, me.core, me.zhi], ls.at[19]), side)
    gb2.second()
    nz.second()
    da.second()
    off = FV * me.slice - 128 * window_tile(me.slice)

    def pack(r, strips, fresh):
        base = 256 * r - off
        i0 = jnp.minimum(lax.div(jnp.maximum(base, 0), 70), 11)
        if fresh:
            rw, cl = iota((256, 400), 0) + base, iota((256, 400), 1)
            i, k = i0 + lax.div(cl, 80), lax.rem(cl, 80)
            pick70[r] = jnp.where((k < 70) & (i * 70 + k == rw), 1.0, 0.0).astype(BF)
        for j in strips:
            src = od[j, pl.ds(i0, 5)].reshape(400, 384)
            at = pl.ds(pl.multiple_of(384 * j, 128), 384)
            down[256 * r : 256 * (r + 1), at] = mm(pick70[r], src).astype(BF)

    for r in range(5):
        pack(r, (da.i, da.l, da.r), True)
    nz.last()
    ez.last()
    da.last()
    for r in range(5):
        pack(r, (da.o,), False)
    keep_d = pltpu.make_async_copy(down, od_o, ls.at[20])
    keep_d.start()
    ga2.last()
    gb2.last()

    for r in (qa, qb, qa2, qb2, wa, wb, ga, gb, ga2, gb2, da):
        r.sent()
    for c in first + zc:
        c.wait_send()

    @pl.when(jnp.logical_not(keeper))
    def _():
        d_cross.wait_send()

    @pl.when(keeper)
    def _():
        for k, t in ys:
            remote(od.at[me.x, rows8], od.at[me.x, rows8], sd.at[k], rdn.at[k], me.at(y=t)).wait_send()

    def sent(k, carry):
        t = lax.rem(m + k, N_CTX)
        for half in range(2):
            block = m if half == 0 else NBLK - 1 - m

            @pl.when(reads(t, block))
            def _():
                src, dst = kv_own.at[half], kv.at[16 + block]
                remote(src, dst, sk.at[half, k], rk.at[block], (me.dp, t)).wait_send()

        return carry

    lax.fori_loop(1, N_CTX, sent, 0)
    for n, (dz, dc) in enumerate(ZK):
        z, core = me.step("z", 4 - dz if dz else 0), lax.rem(me.core + dc, 2)
        ref = oi.at[2 * lax.rem(z, 2) + core, lax.div(z, 2)]
        remote(ref, ref, si.at[n], ri.at[n], me.at(z=z, core=core)).wait_recv()
    ez.finish()
    nz.finish()
    for c in side + wins + keep_p + [keep_q, keep_o, keep_d]:
        c.wait()


def front(idx, wq, wo, wg, wd, eext, n1, ub, cos, sin, low, x, gain, a45, a3, bo):
    outs = (
        sds((2, 2, 4, 2, 48, 2048), BF),
        sds((2, 2, 4, 2, 48, D), BF),
        sds((4, 2, 2, 4, 2, 48, 640), BF),
        sds((FW, D), BF),
        sds((2, 2, 2, ROWS, DX), BF),
        sds((4, 2, 8, 128), jnp.int32),
        sds((2, NWB, BLK, 2 * KW), BF),
        sds((4, GROUP * BLK, KEYS), BF),
        sds((2, 2, 2, ROWS, DX), BF),
        sds((ROWS, D), BF),
        sds((ROWS, D), BF),
        sds((ROWS, D), F32),
        sds((ROWS, DX), BF),
    )
    four = (DMA((4,)),) * 4
    scratch = [
        pltpu.VMEM((4, 16, 2048), BF),
        pltpu.VMEM((4, 16, D), BF),
        pltpu.VMEM((4, 8, 16, 640), BF),
        pltpu.VMEM((80, D), BF),
        pltpu.VMEM((4, 80, 384), BF),
        pltpu.VMEM((48, 2048), BF),
        pltpu.VMEM((48, D), BF),
        pltpu.VMEM((8, 48, 640), BF),
        pltpu.VMEM((2, 2, 4, 2, 48, 2048), BF),
        pltpu.VMEM((2, 2, 4, 2, 48, D), BF),
        pltpu.VMEM((4, 16, 80, 384), BF),
        pltpu.VMEM((2, BLK, 2 * KW), BF),
        pltpu.VMEM((16 + NBLK, BLK, 2 * KW), BF),
        pltpu.VMEM((4, GROUP * BLK, KEYS), BF),
        pltpu.VMEM((FW, D), BF),
        pltpu.VMEM((5, 256, 400), BF),
        DMA((11, 4)),
        DMA((11, 4)),
        DMA((21,)),
        DMA((3, 11)),
        DMA((3, 11)),
        DMA((7,)),
        DMA((7,)),
        DMA((12,)),
        DMA((12,)),
        DMA((4,)),
        DMA((4,)),
        DMA((2, N_CTX)),
        DMA((NBLK,)),
        four,
        DMA((7,)),
        DMA((7,)),
        four,
    ]
    return pl.pallas_call(
        front_kernel,
        out_shape=outs,
        in_specs=[ANY, VM, VM, ANY, VM, ANY] + [VM] * 10,
        out_specs=[ANY] * 9 + [VM] * 4,
        scratch_shapes=scratch,
        compiler_params=pltpu.CompilerParams(collective_id=1, has_side_effects=True, vmem_limit_bytes=VMEM_LIMIT),
    )(idx, wq, wo, wg, wd, eext, n1, ub, cos, sin, low, x, gain, a45, a3, bo)


class Fan:
    def __init__(self, me, axis, view, send, recv):
        self.me, self.axis, self.view, self.send, self.recv = me, axis, view, send, recv
        self.i = getattr(me, axis)

    def copy(self, k, j, to):
        ref = self.view(j)
        return remote(ref, ref, self.send.at[k - 1], self.recv.at[k - 1], self.me.at(**{self.axis: to}))

    def first(self):
        self.out = []
        for k in (1, 3, 2):
            c = self.copy(k, self.i, self.me.step(self.axis, k))
            c.start()
            self.out.append(c)

    def last(self):
        for k in (1, 3, 2):
            f = self.me.step(self.axis, 4 - k)
            self.copy(k, f, f).wait_recv()

    def sent(self):
        for c in self.out:
            c.wait_send()


def norm_back(z, gain, grad):
    r = rms(z)
    t = gain * grad
    return r * t - z * (r * r * r) * jnp.mean(t * z, -1, keepdims=True)


def rear_kernel(
    xg, oe, og, wd_i, ad_all, b_all, e_i, hid_i, n2_i, q_i, o_i, p_i, win_i, wo_i, wq_i, x_i, n1_i,
    oi, a012, a3, a45, bqkv, bo, bd, gain1, gain2, cos, sin,
    out_o, gt_o, early, late,
    wgu, wdo, ad_in, b_in, ad, acc, xb, sib_out, sib_got, red, got2, ft,
    e, hid, n2, q, o, p, win, x, n1,
    gn2, ysum, gh, go, gq, gwin, got, gkv, gj, l1, l2, gf, gl1, gl2, red1, red2,
    wl, xl, ld, sb_s, sb_r, rz_s, rz_r, f_s, f_r, a_s, a_r, b_s, b_r, kv_s, kv_r, ls,
    ring_s, ring_r, fan_s, fan_r, core_s, core_r,
):
    me = Place()
    sib = me.sibling()
    m = me.ctx
    tile = window_tile(me.slice)
    off = FV * me.slice - 128 * tile
    bar = pltpu.get_barrier_semaphore()

    def hello(t, carry):
        @pl.when(t != m)
        def _():
            pl.semaphore_signal(bar, inc=1, device_id=(me.dp, t), device_id_type=MESH)

        return carry

    def load(src, dst, sem):
        c = pltpu.make_async_copy(src, dst, sem)
        c.start()
        return c

    cols = pl.ds(pl.multiple_of(tile * 128, 128), FW)
    wloads = [
        load(ad_all.at[:, :, cols], ad_in, wl.at[0]),
        load(b_all.at[:, :, :, cols], b_in, wl.at[1]),
    ]
    for k in range(4):
        wloads.append(load(og.at[k], wgu.at[pl.ds(0, D), pl.ds(640 * k, 640)], wl.at[2 + k]))
    wloads.append(load(wd_i, wdo.at[pl.ds(0, FW), pl.ds(0, D)], wl.at[6]))
    steps = [(1 - me.zlo, 1 - me.core), (1 - me.zlo, me.core), (me.zlo, 1 - me.core), (me.zlo, me.core)]

    def rows_in(n):
        zl, core = steps[n]
        return [load(src.at[zl, core], xb.at[n % 2, k], xl.at[n % 2, k]) for k, src in enumerate((xg, oe))]

    coming = [rows_in(0), rows_in(1)]
    lax.fori_loop(0, N_CTX, hello, 0)
    others = [me.at(z=me.step("z", 1)), me.at(z=me.step("z", 3)), sib]
    for d in others:
        pl.semaphore_signal(bar, inc=1, device_id=d, device_id_type=MESH)
    loads = [
        load(src, dst, ld.at[n])
        for n, (src, dst) in enumerate(
            (
                (e_i, e), (hid_i, hid), (n2_i, n2), (o_i, o), (q_i, q),
                (win_i, win), (p_i, p), (n1_i, n1), (x_i, x),
            )
        )
    ]
    for c in wloads[:2]:
        c.wait()
    row, col = iota((64, 128), 0), iota((64, 128), 1)
    choose = jnp.zeros((64, 128), F32)
    for k in range(4):
        hit = (lax.div(row, R) == k) & (lax.rem(row, R) == lax.rem(col, R)) & (lax.div(col, R) == oi[k, 0, :1, :1])
        choose += jnp.where(hit, 1.0, 0.0)
    choose = choose.astype(BF)
    fcol = iota((64, FW), 1)
    valid = (fcol >= off) & (fcol < off + FV)
    ad[:64] = jnp.where(valid, mm(choose, ad_in[...].reshape(128, FW)), 0.0).astype(BF)
    ad[64:] = jnp.zeros((64, FW), BF)
    eye = jnp.where(iota((EXT, EXT), 0) == iota((EXT, EXT), 1), 1.0, 0.0).astype(BF)
    wdo[:FW, D:] = tn(ad[...], eye).astype(BF)
    none = jnp.zeros((64, FW), BF)
    wgu[D : D + 64, :FW] = mm(choose, b_in[:, 0].reshape(128, FW)).astype(BF)
    wgu[D + 64 :, :FW] = none
    wgu[D : D + 64, FW:] = none
    wgu[D + 64 :, FW:] = mm(choose, b_in[:, 1].reshape(128, FW)).astype(BF)
    acc[...] = jnp.zeros_like(acc)
    for c in wloads[2:]:
        c.wait()
    pl.semaphore_wait(bar, N_CTX - 1 + len(others))
    sib_copies, z_copies = [], []

    def z_push(j, k, slot, z):
        c = remote(red.at[j, k], got2.at[slot, k], rz_s.at[j, k], rz_r.at[slot, k], me.at(z=z))
        c.start()
        z_copies.append(c)

    for n in range(4):
        for c in coming[n]:
            c.wait()
        xv = xb[n % 2, 0].reshape(2 * ROWS, DX)
        ev = xb[n % 2, 1].reshape(2 * ROWS, DX)
        both = mm(xv, wgu[...])
        gate, up = both[:, :FW], both[:, FW:]
        gm = nt(ev, wdo[:FW])
        sig = 1.0 / (1.0 + jnp.exp(-gate))
        sl = gate * sig
        act = (sl * up).astype(BF)
        gg = (gm * up * (sig * (1.0 + gate * (1.0 - sig)))).astype(BF)
        gu = (gm * sl).astype(BF)
        grads = jnp.concatenate([gg, gu], 1)
        acc[0] += tn(ev[:, D:], act)[:64]
        by_u = tn(xv[:, D:], grads)
        acc[1] += by_u[:64, :FW]
        acc[2] += by_u[64:, FW:]
        if n < 2:
            coming.append(rows_in(n + 2))
        for k in (1, 0):
            wide = nt(grads, wgu[...]) if k == 1 else mm(act, wdo[:FW])
            total = gn2 if k == 1 else ysum
            if n % 2 == 0:
                for zh in range(2):
                    rows = slice(zh * ROWS, (zh + 1) * ROWS)
                    sib_out[n // 2, k, zh] = wide[rows].astype(BF)
                c = remote(sib_out.at[n // 2, k], sib_got.at[n // 2, k], sb_s.at[n // 2, k], sb_r.at[n // 2, k], sib)
                c.start()
                sib_copies.append(c)
            else:
                theirs = sib_got.at[n // 2, k]
                remote(theirs, theirs, sb_s.at[n // 2, k], sb_r.at[n // 2, k], sib).wait_recv()
                if n == 1:
                    for zh in range(2):
                        rows = slice(zh * ROWS, (zh + 1) * ROWS)
                        red[zh, k] = (wide[rows] + theirs[zh].astype(F32)).astype(BF)
                        z_push(zh, k, me.zhi, 2 * zh + 1 - me.zlo)
                else:
                    mine = me.zhi == 1
                    far = jnp.where(mine, wide[:ROWS], wide[ROWS:])
                    near = jnp.where(mine, wide[ROWS:], wide[:ROWS])
                    red[2, k] = (far + theirs[1 - me.zhi].astype(F32)).astype(BF)
                    z_push(2, k, 2, me.step("z", 2))
                    total[...] = near + theirs[me.zhi].astype(F32)
    for k in range(3):
        v = jnp.where(valid, acc[k], 0.0).astype(BF)
        for i in range(4):
            for t in range(10):
                ft[i * 30 + k * 10 + t] = v[R * i : R * (i + 1), 128 * t : 128 * (t + 1)]
    for t in range(120, 128):
        ft[t] = jnp.zeros((R, 128), BF)
    xy = me.y * 4 + me.x

    def plane(k):
        return me.at(x=lax.rem(k, 4), y=lax.div(k, 4))

    def f_copy(t):
        return remote(ft.at[pl.ds(8 * t, 8)], gf.at[xy], f_s.at[t], f_r.at[xy], plane(t))

    def f_send(k, carry):
        f_copy(lax.rem(xy + k, 16)).start()
        return carry

    lax.fori_loop(1, 16, f_send, 0)
    gf[xy] = ft[pl.ds(8 * xy, 8)]
    wo_load = load(wo_i, wdo.at[:, pl.ds(0, D)], ld.at[9])
    wq_load = load(wq_i, wgu.at[pl.ds(0, D), pl.ds(0, 2048)], ld.at[10])

    def z_take(k, total):
        for slot in range(3):
            ref = got2.at[slot, k]
            remote(ref, ref, rz_s.at[slot, k], rz_r.at[slot, k], sib).wait_recv()
            total[...] += ref[...].astype(F32)

    z_take(1, gn2)
    for c in loads[:4] + [wo_load]:
        c.wait()

    def put(tiles, at, v):
        for t in range(v.shape[1] // 128):
            tiles[at + t] = v[:, 128 * t : 128 * (t + 1)].astype(BF)

    gue = gn2[:, D:].astype(BF)
    gn = gn2[:, :D] + mm(gue, a45[...])
    ghv = e[:, :D].astype(F32) + norm_back(hid[...], gain2[...].astype(F32), gn)
    gh[...] = ghv
    ghb = ghv.astype(BF)
    ob = o[...]
    gu3 = nt(ghb, bo[...]).astype(BF)
    go[...] = (nt(ghb, wdo[:, :D]) + mm(gu3, a3[...])).astype(BF)
    u3 = nt(ob, a3[...]).astype(BF)
    s = me.dp

    put(l1, 0, tn(gu3, ob))
    g45b = tn(gue, n2[:, :D]).astype(BF)
    pick_own = jnp.where((iota((R, EXT), 1) == iota((R, EXT), 0) + s * R), 1.0, 0.0).astype(BF)
    pick_up = jnp.where((iota((R, EXT), 1) == iota((R, EXT), 0) + s * R + 64), 1.0, 0.0).astype(BF)
    put(l1, 12, mm(pick_own, g45b))
    put(l1, 24, mm(pick_up, g45b))
    put(l1, 36, tn(u3, ghb))
    for t in range(48, 64):
        l1[t] = jnp.zeros((R, 128), BF)

    def l_copy(tiles, buf, ss, rs, t):
        return remote(tiles.at[pl.ds(2 * t, 2)], buf.at[m], ss.at[t], rs.at[m], (me.dp, t))

    def l_send(tiles, buf, ss, rs):
        def one(k, carry):
            l_copy(tiles, buf, ss, rs, lax.rem(m + k, N_CTX)).start()
            return carry

        lax.fori_loop(1, N_CTX, one, 0)
        buf[m] = tiles[pl.ds(2 * m, 2)]

    def l_sum(buf, ss, rs):
        def one(k, carry):
            t = lax.rem(m + k, N_CTX)
            remote(buf.at[t], buf.at[t], ss.at[t], rs.at[t], (me.dp, t)).wait_recv()
            return carry + buf[t].astype(F32)

        return lax.fori_loop(1, N_CTX, one, buf[m].astype(F32)).astype(BF)

    def l_sent(tiles, buf, ss, rs):
        def one(k, carry):
            l_copy(tiles, buf, ss, rs, lax.rem(m + k, N_CTX)).wait_send()
            return carry

        lax.fori_loop(1, N_CTX, one, 0)

    l_send(l1, gl1, a_s, a_r)

    def covers(t, w, owner, h):
        block = owner if h == 0 else NBLK - 1 - owner
        j = block - ((t if w == 0 else NBLK - 1 - t) - (NWB - 1))
        return j, (j >= 0) & (j < NWB)

    def kv_copy(w, h, t, j):
        return remote(gwin.at[w, j], got.at[h, w, j], kv_s.at[h, w, t], kv_r.at[h, w, j], (me.dp, t))

    for c in loads[4:7]:
        c.wait()
    for w in range(2):
        for a in range(KV_HEADS):
            qs, gv, ov = stack_heads(q, w, a), stack_heads(go, w, a), stack_heads(o, w, a)
            k = win[w, :, :, a * HS : (a + 1) * HS].reshape(KEYS, HS)
            v = win[w, :, :, KW + a * HS : KW + (a + 1) * HS].reshape(KEYS, HS)
            pr = p[2 * w + a]
            delta = jnp.sum(gv.astype(F32) * ov.astype(F32), -1, keepdims=True)
            ds = (pr.astype(F32) * (nt(gv, v) - delta)).astype(BF)
            gqv = mm(ds, k) * SCALE
            for g in range(GROUP):
                cols = slice((a * GROUP + g) * HS, (a * GROUP + g + 1) * HS)
                gq[w * BLK : (w + 1) * BLK, cols] = gqv[g * BLK : (g + 1) * BLK]
            gwin[w, :, :, a * HS : (a + 1) * HS] = (tn(ds, qs) * SCALE).astype(BF).reshape(NWB, BLK, HS)
            gwin[w, :, :, KW + a * HS : KW + (a + 1) * HS] = tn(pr, gv).astype(BF).reshape(NWB, BLK, HS)

        def kv_send(k, carry):
            t = lax.rem(m + k, N_CTX)
            for h in range(2):
                j, ok = covers(m, w, t, h)

                @pl.when(ok)
                def _():
                    kv_copy(w, h, t, j).start()

            return carry

        lax.fori_loop(1, N_CTX, kv_send, 0)
        for h in range(2):
            j, ok = covers(m, w, m, h)

            @pl.when(ok)
            def _():
                c = pltpu.make_async_copy(gwin.at[w, j], got.at[h, w, j], ls.at[2 * w + h])
                c.start()
                c.wait()


    def f_take(k, carry):
        t = lax.rem(xy + k, 16)
        remote(gf.at[t], gf.at[t], f_s.at[t], f_r.at[t], plane(t)).wait_recv()
        return carry + gf[t].astype(F32)

    red1[:8] = lax.fori_loop(1, 16, f_take, gf[xy].astype(F32)).astype(BF)
    red1[8:] = l_sum(gl1, a_s, a_r)

    def vz(j, h):
        ref = early.at[me.y, me.x, lax.rem(j, 2), me.core, lax.div(j, 2)]
        return ref if h is None else ref.at[pl.ds(5 * h, 5)]

    own_e = pltpu.make_async_copy(red1, vz(me.z, None), ls.at[5])
    own_e.start()
    rz = Ring(me, "z", red1, vz, ring_s.at[0], ring_r.at[0])
    rz.first()
    ta, tb = pl.ds(0, 5), pl.ds(5, 5)

    def x0(j, h):
        return early.at[me.y, j, :, me.core, :, ta] if h is None else early.at[me.y, j, h, me.core, :, ta]

    def y0(j, h):
        return early.at[j, :, :, me.core, :, ta] if h is None else early.at[j, pl.ds(2 * h, 2), :, me.core, :, ta]

    def y1(j, h):
        return early.at[j, me.x, :, me.core, :, tb] if h is None else early.at[j, me.x, h, me.core, :, tb]

    def x1(j, h):
        return early.at[:, j, :, me.core, :, tb] if h is None else early.at[pl.ds(2 * h, 2), j, :, me.core, :, tb]

    gkv[...] = jnp.zeros_like(gkv)

    def take(k, carry):
        t = lax.rem(m + N_CTX - k, N_CTX)
        for w in range(2):
            for h in range(2):
                j, ok = covers(t, w, m, h)

                @pl.when(ok & (k > 0))
                def _():
                    ref = got.at[h, w, j]
                    remote(ref, ref, kv_s.at[h, w, t], kv_r.at[h, w, j], (me.dp, t)).wait_recv()

                @pl.when(ok)
                def _():
                    gkv[h] += got[h, w, j].astype(F32)

        return carry

    lax.fori_loop(0, N_CTX, take, 0)
    rz.second()
    rz.last()
    own_e.wait()
    ra = Ring(me, "x", x0(me.x, None), x0, ring_s.at[1], ring_r.at[1])
    rb = Ring(me, "y", y1(me.y, None), y1, ring_s.at[2], ring_r.at[2])
    ra.first()
    rb.first()

    ra.second()
    rb.second()

    for c in loads[7:] + [wq_load]:
        c.wait()
    c, sn = cos[...], sin[...]
    for h in range(HEADS):
        cols = slice(h * HS, (h + 1) * HS)
        gj[:, cols] = turn_back(gq[:, cols], c, sn).astype(BF)
    for a in range(KV_HEADS):
        v = jnp.concatenate([gkv[0, :, a * HS : (a + 1) * HS], gkv[1, :, a * HS : (a + 1) * HS]], 0)
        gj[:, QW + a * HS : QW + (a + 1) * HS] = turn_back(v, c, sn).astype(BF)
    gj[:, QW + KW :] = jnp.concatenate([gkv[0, :, KW:], gkv[1, :, KW:]], 0).astype(BF)
    n1b = n1[...]
    more = jnp.zeros((ROWS, D), F32)
    for i, (lo, hi) in enumerate(((0, QW), (QW, QW + KW), (QW + KW, QW + 2 * KW))):
        am = a012[i]
        u = nt(n1b, am).astype(BF)
        gjm = gj[:, lo:hi]
        gum = nt(gjm, bqkv[:, lo:hi]).astype(BF)
        more += mm(gum, am)
        put(l2, 36 + lo // 128, tn(u, gjm))
        put(l2, 12 * i, tn(gum, n1b))
    z_take(0, ysum)
    ud = ysum[:, D:].astype(BF)
    y = hid[...] + ysum[:, :D] + mm(ud, bd[...])
    for h in range(2):
        out_o[:, h, :] = y[h * BLK : (h + 1) * BLK].astype(BF)
    put(l2, 52, mm(pick_own, tn(ud, e[:, :D]).astype(BF)))
    l_send(l2, gl2, b_s, b_r)
    ra.last()
    rb.last()
    rc = Ring(me, "y", y0(me.y, None), y0, ring_s.at[3], ring_r.at[3])
    rd = Ring(me, "x", x1(me.x, None), x1, ring_s.at[4], ring_r.at[4])
    rc.first()
    rd.first()
    gn = nt(gj[...], wgu[:D, :2048]) + more
    gt = gh[...] + norm_back(x[...].astype(F32), gain1[...].astype(F32), gn)
    for h in range(2):
        gt_o[:, h, :] = gt[h * BLK : (h + 1) * BLK].astype(BF)

    red2[...] = l_sum(gl2, b_s, b_r)

    def uz(j):
        return late.at[me.y, me.x, lax.rem(j, 2), me.core, lax.div(j, 2)]

    own_l = pltpu.make_async_copy(red2, uz(me.z), ls.at[6])
    own_l.start()
    own_l.wait()
    fz = Fan(me, "z", uz, fan_s.at[0], fan_r.at[0])
    fz.first()
    rc.second()
    rd.second()
    fz.last()

    def ux(j):
        return late.at[me.y, j, :, me.core]

    def uy(j):
        return late.at[j, :, :, me.core]

    fx = Fan(me, "x", ux, fan_s.at[1], fan_r.at[1])
    fx.first()
    rc.last()
    rd.last()
    swaps = []

    def swap(view, n):
        c = remote(view(me.core), view(me.core), core_s.at[n], core_r.at[n], sib)
        c.start()
        swaps.append((c, view, n))

    for k in range(4):
        swap(lambda core, k=k: early.at[k, :, :, core], k)
    fx.last()
    fy = Fan(me, "y", uy, fan_s.at[2], fan_r.at[2])
    fy.first()
    fy.last()
    for k in range(4):
        swap(lambda core, k=k: late.at[k, :, :, core], 4 + k)

    for c in sib_copies + z_copies:
        c.wait_send()
    for r in (rz, ra, rb, rc, rd, fz, fx, fy):
        r.sent()

    def f_sent(k, carry):
        f_copy(lax.rem(xy + k, 16)).wait_send()
        return carry

    lax.fori_loop(1, 16, f_sent, 0)
    l_sent(l1, gl1, a_s, a_r)
    l_sent(l2, gl2, b_s, b_r)

    def kv_sent(k, carry):
        t = lax.rem(m + k, N_CTX)
        for w in range(2):
            for h in range(2):
                j, ok = covers(m, w, t, h)

                @pl.when(ok)
                def _():
                    kv_copy(w, h, t, j).wait_send()

        return carry

    lax.fori_loop(1, N_CTX, kv_sent, 0)
    for c, view, n in swaps:
        c.wait_send()
        ref = view(1 - me.core)
        remote(ref, ref, core_s.at[n], core_r.at[n], sib).wait_recv()


def rear(xg, oe, og, wd, ad_all, b_all, e, hid, n2, q, o, p, win, wo, wq, x, n1, *small):
    outs = (
        sds((BLK, 2, D), BF),
        sds((BLK, 2, D), BF),
        sds((4, 4, 2, 2, 2, 10, R, 128), BF),
        sds((4, 4, 2, 2, 2, 2, R, 128), BF),
    )
    block = (ROWS, DX)
    scratch = [
        pltpu.VMEM((DX, 2 * FW), BF),
        pltpu.VMEM((D, DX), BF),
        pltpu.VMEM((ADAPT, R, FW), BF),
        pltpu.VMEM((ADAPT, 2, R, FW), BF),
        pltpu.VMEM((EXT, FW), BF),
        pltpu.VMEM((3, 64, FW), F32),
        pltpu.VMEM((2, 2, 2) + block, BF),
        pltpu.VMEM((2, 2, 2) + block, BF),
        pltpu.VMEM((2, 2, 2) + block, BF),
        pltpu.VMEM((3, 2) + block, BF),
        pltpu.VMEM((3, 2) + block, BF),
        pltpu.VMEM((128, R, 128), BF),
    ]
    scratch += [pltpu.VMEM(v.shape, v.dtype) for v in (e, hid, n2, q, o, p, win, x, n1)]
    scratch += [
        pltpu.VMEM(block, F32),
        pltpu.VMEM(block, F32),
        pltpu.VMEM((ROWS, D), F32),
        pltpu.VMEM((ROWS, D), BF),
        pltpu.VMEM((ROWS, D), F32),
        pltpu.VMEM((2, NWB, BLK, 2 * KW), BF),
        pltpu.VMEM((2, 2, NWB, BLK, 2 * KW), BF),
        pltpu.VMEM((2, BLK, 2 * KW), F32),
        pltpu.VMEM((ROWS, 2048), BF),
        pltpu.VMEM((64, R, 128), BF),
        pltpu.VMEM((64, R, 128), BF),
        pltpu.VMEM((16, 8, R, 128), BF),
        pltpu.VMEM((N_CTX, 2, R, 128), BF),
        pltpu.VMEM((N_CTX, 2, R, 128), BF),
        pltpu.VMEM((10, R, 128), BF),
        pltpu.VMEM((2, R, 128), BF),
        DMA((7,)),
        DMA((2, 2)),
        DMA((11,)),
        DMA((2, 2)),
        DMA((2, 2)),
        DMA((3, 2)),
        DMA((3, 2)),
        DMA((16,)),
        DMA((16,)),
        DMA((N_CTX,)),
        DMA((N_CTX,)),
        DMA((N_CTX,)),
        DMA((N_CTX,)),
        DMA((2, 2, N_CTX)),
        DMA((2, 2, NWB)),
        DMA((7,)),
        DMA((5, 4)),
        DMA((5, 4)),
        DMA((3, 3)),
        DMA((3, 3)),
        DMA((8,)),
        DMA((8,)),
    ]
    return pl.pallas_call(
        rear_kernel,
        out_shape=outs,
        in_specs=[ANY] * 17 + [VM] * len(small),
        out_specs=[VM, VM, ANY, ANY],
        scratch_shapes=scratch,
        compiler_params=pltpu.CompilerParams(collective_id=2, has_side_effects=True, vmem_limit_bytes=VMEM_LIMIT),
    )(xg, oe, og, wd, ad_all, b_all, e, hid, n2, q, o, p, win, wo, wq, x, n1, *small)


def spread_kernel(oi, early, late, ain_o, aff_o, bqkv_o, bres_o, bff_o):
    e = pl.program_id(0)
    for ref in (ain_o, aff_o, bqkv_o, bres_o, bff_o):
        ref[...] = jnp.zeros_like(ref)

    def local_tile(ref, at, s, n):
        k, j = n // 2, n % 2
        return ref[k // 8, k % 4, s // 2, s % 2, (k // 4) % 2, at + j].astype(F32)

    def ff_tile(piece, n):
        k, j = n // 8, n % 8
        return early[k // 4, k % 4, piece // 4, (piece // 2) % 2, piece % 2, j].astype(F32)

    for s in range(4):

        @pl.when(oi[s, 0, 0, 0] == e)
        def _():
            for c in range(12):
                cols = slice(128 * c, 128 * (c + 1))
                for m in range(3):
                    ain_o[0, m, :, cols] += local_tile(late, 0, s, 12 * m + c)
                    ain_o[0, 3 + m, :, cols] += local_tile(early, 8, s, 12 * m + c)
                bres_o[0, 0, :, cols] += local_tile(early, 8, s, 36 + c)
                bres_o[0, 1, :, cols] += local_tile(late, 0, s, 52 + c)
            for c in range(16):
                bqkv_o[0, :, 128 * c : 128 * (c + 1)] += local_tile(late, 0, s, 36 + c)
            for piece in range(8):
                tile = 60 if piece == 7 else 35 * piece // 4
                for k in range(3):
                    for c in range(10):
                        cols = slice(128 * (tile + c), 128 * (tile + c + 1))
                        v = ff_tile(piece, s * 30 + k * 10 + c)
                        if k == 0:
                            aff_o[0, :, cols] += v
                        else:
                            bff_o[0, k - 1, :, cols] += v


def spread(oi, early, late):
    outs = (
        sds((ADAPT, 6, R, D), F32),
        sds((ADAPT, R, FF), F32),
        sds((ADAPT, R, 2048), F32),
        sds((ADAPT, 2, R, D), F32),
        sds((ADAPT, 2, R, FF), F32),
    )

    def one(shape):
        return pl.BlockSpec((1,) + shape[1:], lambda i: (i,) + (0,) * (len(shape) - 1))

    return pl.pallas_call(
        spread_kernel,
        out_shape=outs,
        grid=(ADAPT,),
        in_specs=[
            SM,
            pl.BlockSpec(early.shape, lambda i: (0,) * 8),
            pl.BlockSpec(late.shape, lambda i: (0,) * 8),
        ],
        out_specs=[one(o.shape) for o in outs],
        compiler_params=pltpu.CompilerParams(vmem_limit_bytes=VMEM_LIMIT),
    )(oi, early, late)


def local(
    tokens,
    cotangent,
    w_qkv,
    b_qkv,
    w_out,
    w_gu,
    w_down,
    gain_attn,
    gain_mlp,
    adapt_in,
    adapt_in_ff,
    adapt_out_qkv,
    adapt_out_res,
    adapt_out_ff,
    doc_lengths,
    adapter_index,
    window,
):
    member = lax.axis_index("ctx")
    starts = jnp.stack([member * BLK, (NBLK - 1 - member) * BLK])
    pos = (starts[:, None] + jnp.arange(BLK, dtype=jnp.int32)[None]).reshape(ROWS)
    ends = jnp.cumsum(doc_lengths[0])
    begin = jnp.max(jnp.where(ends[None] <= pos[:, None], ends[None], 0), -1)
    low = jnp.maximum(begin, pos - window[0] + 1)
    low = jnp.broadcast_to(low[:, None], (ROWS, 128)).astype(jnp.int32)
    freq = 1000000.0 ** (-(2.0 * jnp.arange(HS // 2, dtype=F32)) / HS)
    ang = pos.astype(F32)[:, None] * freq[None]
    c, sn = jnp.cos(ang), jnp.sin(ang)
    cos = jnp.concatenate([c, c], -1)
    sin = jnp.concatenate([-sn, sn], -1)

    wg = jnp.pad(jnp.transpose(w_gu, (1, 0, 2)), ((0, 0), (0, 4), (0, 0)))
    idx_row = jnp.broadcast_to(adapter_index[:, None], (8, 128)).astype(jnp.int32)

    x, n1, eext, ub, a45, bd, a3, bo, a012, bqkv = prepare(
        adapter_index, tokens[0], cotangent[0], adapt_in, adapt_out_qkv, adapt_out_res, gain_attn, b_qkv
    )
    oq, oo, og, down, oe, oi, wins, p, xg, q, o, hid, n2 = front(
        idx_row, w_qkv, w_out, wg, w_down, eext, n1, ub, cos, sin, low, x, gain_mlp, a45, a3, bo
    )
    oq = oq.reshape(D, 2048)
    oo = oo.reshape(D, D)
    og = og.reshape(4, D, 640)
    out, gt, early, late = rear(
        xg, oe, og, down, adapt_in_ff, adapt_out_ff, eext, hid, n2, q, o, p, wins, oo, oq, x, n1,
        oi, a012, a3, a45, bqkv, bo, bd, gain_attn, gain_mlp, cos, sin,
    )
    return (out[None], gt[None]) + tuple(spread(oi, early, late))


def solution(mesh):
    return jax.shard_map(
        local,
        mesh=mesh,
        in_specs=(
            P("dp", "ctx", None, None),
            P("dp", "ctx", None, None),
            P(("dp", "ctx"), None),
            P(),
            P(("dp", "ctx"), None),
            P(("dp", "ctx"), None, None),
            P(("dp", "ctx"), None),
            P(),
            P(),
            P(),
            P(),
            P(),
            P(),
            P(),
            P("dp", None),
            P("dp"),
            P("dp"),
        ),
        out_specs=(P("dp", "ctx", None, None), P("dp", "ctx", None, None), P(), P(), P(), P(), P()),
        check_vma=False,
    )
```

```python
import functools

import jax
import jax.numpy as jnp
from jax import lax
from jax.experimental import pallas as pl
from jax.experimental.pallas import tpu as pltpu
from jax.sharding import PartitionSpec as P

D = 1536
HEADS = 12
KV_HEADS = 2
HS = 128
GROUP = HEADS // KV_HEADS
FF = 8960
R = 16
ADAPT = 8
BLK = 64
ROWS = 2 * BLK
N_CTX = 32
NBLK = 2 * N_CTX
WIN = 1024
NWB = WIN // BLK + 1
KEYS = NWB * BLK
EXT = 128
DX = D + EXT
FW = 1280
FV = FF // 8
QW = HEADS * HS
KW = KV_HEADS * HS
SCALE = HS**-0.5
EPS = 1e-6

MESH = pl.DeviceIdType.MESH
BF = jnp.bfloat16
F32 = jnp.float32
ANY = pl.BlockSpec(memory_space=pl.ANY)
VM = pl.BlockSpec(memory_space=pltpu.VMEM)
SM = pl.BlockSpec(memory_space=pltpu.SMEM)
DMA = pltpu.SemaphoreType.DMA
VMEM_LIMIT = 60 * 2**20


def sds(shape, dtype):
    return jax.ShapeDtypeStruct(shape, dtype)


def nt(a, b):
    return lax.dot_general(a, b, (((1,), (1,)), ((), ())), preferred_element_type=F32)


def tn(a, b):
    return lax.dot_general(a, b, (((0,), (0,)), ((), ())), preferred_element_type=F32)


def mm(a, b):
    return jnp.dot(a, b, preferred_element_type=F32)


def iota(shape, dim):
    return lax.broadcasted_iota(jnp.int32, shape, dim)


class Place:
    def __init__(self):
        dp, ctx = lax.axis_index("dp"), lax.axis_index("ctx")
        self.dp, self.ctx = dp, ctx
        self.zlo, self.core = lax.div(dp, 2), lax.rem(dp, 2)
        self.y, self.zhi, self.x = lax.div(ctx, 8), lax.rem(lax.div(ctx, 4), 2), lax.rem(ctx, 4)
        self.z = self.zhi * 2 + self.zlo
        self.slice = 2 * dp + self.zhi

    def at(self, x=None, y=None, z=None, core=None):
        x = self.x if x is None else x
        y = self.y if y is None else y
        z = self.z if z is None else z
        core = self.core if core is None else core
        return (lax.rem(z, 2) * 2 + core, y * 8 + lax.div(z, 2) * 4 + x)

    def step(self, axis, by):
        return lax.rem(getattr(self, axis) + by, 4)

    def ring(self, axis):
        return [self.at(**{axis: self.step(axis, k)}) for k in (1, 2, 3)]

    def sibling(self):
        return self.at(core=1 - self.core)


def window_tile(piece):
    return jnp.minimum(lax.div(35 * piece, 4), 60)


def remote(src, dst, send, recv, device):
    return pltpu.make_async_remote_copy(
        src_ref=src, dst_ref=dst, send_sem=send, recv_sem=recv, device_id=device, device_id_type=MESH
    )


def greet(peers):
    sem = pltpu.get_barrier_semaphore()
    for device in peers:
        pl.semaphore_signal(sem, inc=1, device_id=device, device_id_type=MESH)
    pl.semaphore_wait(sem, len(peers))


class Ring:
    def __init__(self, me, axis, own, view, send, recv):
        self.i = getattr(me, axis)
        self.r, self.o, self.l = (me.step(axis, k) for k in (1, 2, 3))
        self.right, self.left = me.at(**{axis: self.r}), me.at(**{axis: self.l})
        self.own, self.view, self.send, self.recv = own, view, send, recv

    def copy(self, k, src, dst, device):
        return remote(src, dst, self.send.at[k], self.recv.at[k], device)

    def first(self):
        place = self.view(self.i, None)
        self.out = [self.copy(0, self.own, place, self.right), self.copy(1, self.own, place, self.left)]
        for c in self.out:
            c.start()

    def second(self):
        v = self.view
        self.copy(0, v(self.l, None), v(self.l, None), self.right).wait_recv()
        c = self.copy(2, v(self.l, 0), v(self.l, 0), self.right)
        c.start()
        self.out.append(c)
        self.copy(1, v(self.r, None), v(self.r, None), self.left).wait_recv()
        c = self.copy(3, v(self.r, 1), v(self.r, 1), self.left)
        c.start()
        self.out.append(c)

    def last(self):
        v = self.view
        self.copy(2, v(self.o, 0), v(self.o, 0), self.right).wait_recv()
        self.copy(3, v(self.o, 1), v(self.o, 1), self.left).wait_recv()

    def sent(self):
        for c in self.out:
            c.wait_send()


class ZGather:
    def __init__(self, me, own, buf, send, recv, core_send, core_recv, half):
        self.me, self.own, self.buf = me, own, buf
        self.cs, self.cr = core_send, core_recv

        def view(j, h, core=me.core):
            ref = buf.at[lax.rem(j, 2), core, lax.div(j, 2)]
            return ref if h is None else ref.at[pl.ds(h * half, half)]

        self.view = view
        self.ring = Ring(me, "z", own, view, send, recv)
        self.out = []

    def swap(self, src, j):
        c = remote(src, self.view(j, None), self.cs.at[len(self.out)], self.cr.at[len(self.out)], self.me.sibling())
        c.start()
        self.out.append((c, j))

    def first(self):
        self.ring.first()
        self.swap(self.own, self.me.z)

    def second(self):
        self.ring.second()
        self.swap(self.view(self.ring.l, None), self.ring.l)
        self.swap(self.view(self.ring.r, None), self.ring.r)

    def last(self):
        self.ring.last()
        self.swap(self.view(self.ring.o, None), self.ring.o)

    def finish(self):
        self.ring.sent()
        for k, (c, j) in enumerate(self.out):
            c.wait_send()
            place = self.view(j, None, 1 - self.me.core)
            remote(place, place, self.cs.at[k], self.cr.at[k], self.me.sibling()).wait_recv()


def rms(z):
    return lax.rsqrt(jnp.mean(z * z, -1, keepdims=True) + EPS)


def turn(v, cos, sin):
    return v * cos + pltpu.roll(v, 64, 1) * sin


def turn_back(v, cos, sin):
    return v * cos - pltpu.roll(v, 64, 1) * sin


def stack_heads(ref, h, a):
    rows = slice(h * BLK, (h + 1) * BLK)
    return jnp.concatenate(
        [ref[rows, (a * GROUP + g) * HS : (a * GROUP + g + 1) * HS] for g in range(GROUP)], 0
    )


def reads(t, block):
    a, b = t - block, NBLK - 1 - t - block
    return ((a >= 0) & (a < NWB)) | ((b >= 0) & (b < NWB))


ZK = [(dz, dc) for dz in range(4) for dc in range(2) if dz or dc]


def front_kernel(
    idx_i, docs, span, wq_i, wo_i, wg_i, wd_i, tok, cot, ain_i, aqkv_i, ares_i, gain1, bias, cos, sin, gain,
    oq_o, oo_o, og, od_o, oe, oi, win_o, p_o, xg, q, o_o, hid_o, n2,
    x, n1, eext, a45, bd, a3, bo, a012, bqkv,
    ub, idx, wg, ain, aqkv, ares, rq, ro, rg, wdp, rd, cq, co, cg, oq, oo, od, kv_own, kv, p, down, pick70,
    ss, rs, ls, s1, r1, s2, r2, sc, rc, sd, rdn, sk, rk, ez_sems, si, ri, nz_sems,
):
    me = Place()
    sib = me.sibling()
    m = me.ctx
    bar = pltpu.get_barrier_semaphore()

    def hello(t, carry):
        @pl.when(t != m)
        def _():
            pl.semaphore_signal(bar, inc=1, device_id=(me.dp, t), device_id_type=MESH)

        return carry

    lax.fori_loop(0, N_CTX, hello, 0)
    others = [me.at(z=me.step("z", dz), core=lax.rem(me.core + dc, 2)) for dz, dc in ZK if dz % 2 or dc]
    for d in others:
        pl.semaphore_signal(bar, inc=1, device_id=d, device_id_type=MESH)

    adapters = []
    for n, (src, dst) in enumerate(((ain_i, ain), (aqkv_i, aqkv), (ares_i, ares))):
        adapters.append(pltpu.make_async_copy(src, dst, ls.at[21 + n]))
        adapters[-1].start()
    rq[me.x, :12] = wq_i[...]
    rq[me.x, 12:] = jnp.zeros((4, 2048), BF)
    ro[me.x, :12] = wo_i[...]
    ro[me.x, 12:] = jnp.zeros((4, D), BF)
    wdp[:70] = wd_i[...]
    wdp[70:] = jnp.zeros((10, D), BF)
    idx[...] = jnp.full((8, 128), idx_i[0], jnp.int32)

    pl.semaphore_wait(bar, N_CTX - 1 + len(others))

    tiles = [60 if g == 7 else 35 * g // 4 for g in range(8)]

    def panel(g, t):
        col = pl.multiple_of(tiles[g] * 128 + lax.rem(t, 2) * 640, 128)
        return wg.at[lax.div(t, 2), :, pl.ds(col, 640)]

    def strip(t):
        return wdp.at[:, pl.ds(pl.multiple_of(384 * t, 128), 384)]

    def start(c, out):
        c.start()
        out.append(c)

    first = []
    xs = [(k, me.step("x", k), me.at(x=me.step("x", k))) for k in (1, 3, 2)]
    for k, t, d in xs:
        start(remote(rq.at[me.x], rq.at[me.x], s1.at[k - 1, 0], r1.at[k - 1, 0], d), first)
    for k, t, d in xs:
        start(remote(ro.at[me.x], ro.at[me.x], s1.at[k - 1, 1], r1.at[k - 1, 1], d), first)
    for k in range(2):
        wg[k, :12] = wg_i[:, k, :]
        wg[k, 12:] = jnp.zeros((4, FF), BF)
    for k, t, d in xs:
        for g in range(8):
            start(remote(panel(g, t), rg.at[me.x, g], s1.at[k - 1, 2 + g], r1.at[k - 1, 2 + g], d), first)
        start(remote(strip(t), rd.at[me.x], s1.at[k - 1, 10], r1.at[k - 1, 10], d), first)
    mine = []
    for g in range(8):
        start(pltpu.make_async_copy(panel(g, me.x), rg.at[me.x, g], ls.at[2 + g]), mine)
    start(pltpu.make_async_copy(strip(me.x), rd.at[me.x], ls.at[1]), mine)
    side = []
    start(pltpu.make_async_copy(idx, oi.at[me.dp, me.zhi], ls.at[11]), side)
    for n, (dz, dc) in enumerate(ZK):
        d = me.at(z=me.step("z", dz), core=lax.rem(me.core + dc, 2))
        start(remote(idx, oi.at[me.dp, me.zhi], si.at[n], ri.at[n], d), first)

    def from_x(n, ref_of):
        for k in (1, 3, 2):
            f = me.step("x", 4 - k)
            ref = ref_of(f)
            remote(ref, ref, s1.at[k - 1, n], r1.at[k - 1, n], me.at(x=f)).wait_recv()

    row, col = iota((48, 64), 0), iota((48, 64), 1)
    put = jnp.where(
        (lax.rem(col, 16) < 12) & (lax.div(col, 16) * 12 + lax.rem(col, 16) == row), 1.0, 0.0
    ).astype(BF)

    kv[:16] = jnp.zeros((16, BLK, 2 * KW), BF)
    for h in range(2):
        rows = slice(h * BLK, (h + 1) * BLK)
        x[rows] = tok[:, h, :]
        eext[rows, :D] = cot[:, h, :]
    xf = x[...].astype(F32)
    n1[...] = (xf * rms(xf) * gain1[...].astype(F32)).astype(BF)
    row, col = iota((R, 128), 0), iota((R, 128), 1)
    choose = jnp.where((lax.div(col, R) == idx_i[0]) & (lax.rem(col, R) == row), 1.0, 0.0).astype(BF)

    def chosen(ref):
        return mm(choose, ref.reshape(ADAPT * R, ref.shape[-1])).astype(BF)

    for c in adapters:
        c.wait()
    for k in range(3):
        a012[k] = chosen(ain[:, k])
    a3[...] = chosen(ain[:, 3])
    at = pl.multiple_of(me.dp * R, R)
    a45[...] = jnp.zeros_like(a45)
    a45[pl.ds(at, R), :] = chosen(ain[:, 4])
    a45[pl.ds(at + 64, R), :] = chosen(ain[:, 5])
    bqkv[...] = chosen(aqkv[...])
    bo[...] = chosen(ares[:, 0])
    bd[...] = jnp.zeros_like(bd)
    bd[pl.ds(at, R), :] = chosen(ares[:, 1])
    for k, (c0, c1) in enumerate(((0, QW), (QW, QW + KW), (QW + KW, QW + 2 * KW))):
        u = nt(n1[...], a012[k]).astype(BF)
        ub[:, c0:c1] = mm(u, bqkv[:, c0:c1]) + bias[c0:c1].astype(F32)
    eext[:, D:] = nt(eext[:, :D], bd[...]).astype(BF)
    start(pltpu.make_async_copy(eext, oe.at[me.zlo, me.core, me.zhi], ls.at[10]), side)
    from_x(0, lambda f: rq.at[f])
    cq[...] = mm(put, rq[...].reshape(64, 2048)).astype(BF)
    lo, hi = pl.ds(0, 1024), pl.ds(1024, 1024)

    def qy0(j, h):
        return oq.at[me.zlo, me.core, j, me.zhi, :, lo if h is None else pl.ds(512 * h, 512)]

    def qz0(j, h, core=me.core):
        zl, zh = lax.rem(j, 2), lax.div(j, 2)
        return oq.at[zl, core, :, zh, :, lo] if h is None else oq.at[zl, core, pl.ds(2 * h, 2), zh, :, lo]

    def qz1(j, h):
        cols = hi if h is None else pl.ds(1024 + 512 * h, 512)
        return oq.at[lax.rem(j, 2), me.core, me.y, lax.div(j, 2), :, cols]

    def qy1(j, h, core=me.core):
        return oq.at[:, core, j, :, :, hi] if h is None else oq.at[h, core, j, :, :, hi]

    qa = Ring(me, "y", cq.at[:, lo], qy0, ss.at[0], rs.at[0])
    qb = Ring(me, "z", cq.at[:, hi], qz1, ss.at[1], rs.at[1])
    qa.first()
    qb.first()
    oq[me.zlo, me.core, me.y, me.zhi] = cq[...]
    from_x(1, lambda f: ro.at[f])
    co[...] = mm(put, ro[...].reshape(64, D)).astype(BF)
    qa.second()
    qb.second()
    for n in range(8):
        from_x(2 + n, lambda f: rg.at[f, n])
    from_x(10, lambda f: rd.at[f])
    for c in mine:
        c.wait()
    for g in range(8):
        cg[g] = mm(put, rg[:, g].reshape(64, 640)).astype(BF)

    own_g = pltpu.make_async_copy(cg.at[me.slice], og.at[me.x, me.zlo, me.core, me.y, me.zhi], ls.at[14])
    own_g.start()
    zc = []
    for n, (dz, dc) in enumerate(ZK):
        z, core = me.step("z", dz), lax.rem(me.core + dc, 2)
        piece = 2 * (2 * lax.rem(z, 2) + core) + lax.div(z, 2)
        d = me.at(z=z, core=core)
        start(remote(cg.at[piece], og.at[me.x, me.zlo, me.core, me.y, me.zhi], s2.at[n], r2.at[n], d), zc)
    keeper = lax.div(me.y, 2) == me.zhi
    rows4 = pl.ds(lax.rem(me.y, 2) * 8 + me.zhi * 4, 4)
    across = me.at(z=me.step("z", 2))
    d_local = pltpu.make_async_copy(rd, od.at[me.x, rows4], ls.at[15])
    d_cross = remote(rd, od.at[me.x, rows4], sd.at[0], rdn.at[0], across)

    @pl.when(keeper)
    def _():
        d_local.start()

    @pl.when(jnp.logical_not(keeper))
    def _():
        d_cross.start()

    qa.last()
    qb.last()
    qa2 = Ring(me, "z", qz0(me.z, None), qz0, ss.at[2], rs.at[2])
    qb2 = Ring(me, "y", qy1(me.y, None), qy1, ss.at[3], rs.at[3])
    qa2.first()
    qb2.first()
    swaps = []

    def swap(view, j):
        n = len(swaps)
        c = remote(view(j, None), view(j, None), sc.at[n], rc.at[n], sib)
        c.start()
        swaps.append((c, view, j))

    def swapped(n):
        c, view, j = swaps[n]
        c.wait_send()
        ref = view(j, None, 1 - me.core)
        remote(ref, ref, sc.at[n], rc.at[n], sib).wait_recv()

    swap(qz0, me.z)
    swap(qy1, me.y)
    own_g.wait()
    for n, (dz, dc) in enumerate(ZK):
        z, core = me.step("z", 4 - dz if dz else 0), lax.rem(me.core + dc, 2)
        ref = og.at[me.x, lax.rem(z, 2), core, me.y, lax.div(z, 2)]
        remote(ref, ref, s2.at[n], r2.at[n], me.at(z=z, core=core)).wait_recv()

    def g0a(j, h):
        return og.at[me.x, 0, :, j] if h is None else og.at[me.x, 0, h, j]

    def g0b(j, h):
        return og.at[j, 0] if h is None else og.at[j, 0, h]

    def g1a(j, h):
        return og.at[j, 1, :, me.y] if h is None else og.at[j, 1, h, me.y]

    def g1b(j, h):
        return og.at[:, 1, :, j] if h is None else og.at[:, 1, h, j]

    ga = Ring(me, "y", g0a(me.y, None), g0a, ss.at[4], rs.at[4])
    gb = Ring(me, "x", g1a(me.x, None), g1a, ss.at[5], rs.at[5])
    ga.first()
    gb.first()
    def oy(j, h):
        ref = oo.at[me.zlo, me.core, j, me.zhi]
        return ref if h is None else ref.at[:, pl.ds(768 * h, 768)]

    def oz(j, h, core=me.core):
        zl, zh = lax.rem(j, 2), lax.div(j, 2)
        return oo.at[zl, core, :, zh] if h is None else oo.at[zl, core, pl.ds(2 * h, 2), zh]

    wa = Ring(me, "y", co, oy, ss.at[8], rs.at[8])
    qa2.second()
    qb2.second()
    swap(qz0, qa2.l)
    swap(qy1, qb2.l)
    swap(qz0, qa2.r)
    swap(qy1, qb2.r)
    oo[me.zlo, me.core, me.y, me.zhi] = co[...]

    ga.second()
    gb.second()
    wa.first()
    qa2.last()
    qb2.last()
    swap(qz0, qa2.o)
    swap(qy1, qb2.o)

    wa.second()
    rows4b = pl.ds(lax.rem(me.y, 2) * 8 + (1 - me.zhi) * 4, 4)
    rows8 = pl.ds(lax.rem(me.y, 2) * 8, 8)
    ys = [(k, me.step("y", k)) for k in (1, 3, 2)]

    @pl.when(keeper)
    def _():
        d_local.wait()
        ref = od.at[me.x, rows4b]
        remote(rd, ref, sd.at[0], rdn.at[0], across).wait_recv()
        for k, t in ys:
            remote(od.at[me.x, rows8], od.at[me.x, rows8], sd.at[k], rdn.at[k], me.at(y=t)).start()

    ga.last()
    gb.last()
    ga2 = Ring(me, "x", g0b(me.x, None), g0b, ss.at[6], rs.at[6])
    gb2 = Ring(me, "y", g1b(me.y, None), g1b, ss.at[7], rs.at[7])

    ga2.first()
    for n in range(8):
        swapped(n)
    keep_q = pltpu.make_async_copy(oq, oq_o, ls.at[12])
    keep_q.start()

    c, s = cos[...], sin[...]
    n1v = n1[...]
    for h in (12, 14, 0, 2, 4, 6, 8, 10):
        pair = slice(h * HS, (h + 2) * HS)
        j = mm(n1v, oq[:, :, :, :, :, pair].reshape(D, 2 * HS)) + ub[:, pair]
        for i in range(2):
            v = j[:, i * HS : (i + 1) * HS]
            if h + i < HEADS + KV_HEADS:
                v = turn(v, c, s)
            v = v.astype(BF)
            if h + i < HEADS:
                q[:, (h + i) * HS : (h + i + 1) * HS] = v
            else:
                at = slice((h + i - HEADS) * HS, (h + i - HEADS + 1) * HS)
                kv_own[0, :, at] = v[:BLK]
                kv_own[1, :, at] = v[BLK:]
        if h == 14:
            def send(k, carry):
                t = lax.rem(m + k, N_CTX)
                for half in range(2):
                    block = m if half == 0 else NBLK - 1 - m

                    @pl.when(reads(t, block))
                    def _():
                        src, dst = kv_own.at[half], kv.at[16 + block]
                        remote(src, dst, sk.at[half, k], rk.at[block], (me.dp, t)).start()

                return carry

            lax.fori_loop(1, N_CTX, send, 0)
            kv[16 + m] = kv_own[0]
            kv[16 + NBLK - 1 - m] = kv_own[1]

    gb2.first()
    wa.last()
    wb = Ring(me, "z", oz(me.z, None), oz, ss.at[9], rs.at[9])
    wb.first()
    swap(oz, me.z)
    ez = ZGather(me, eext, oe, *ez_sems, BLK)
    ez.first()
    def dx(j, h):
        return od.at[j] if h is None else od.at[j, pl.ds(8 * h, 8)]

    def arrived(block):
        src = jnp.where(block < N_CTX, block, NBLK - 1 - block)
        remote(kv_own.at[0], kv.at[16 + block], sk.at[0, 0], rk.at[block], (me.dp, src)).wait_recv()

    def near0(j, carry):
        block = m - (NWB - 1) + j

        @pl.when(block >= 0)
        def _():
            arrived(block)

        return carry

    def near1(j, carry):
        block = NBLK - 1 - m - (NWB - 1) + j

        @pl.when(block > m)
        def _():
            arrived(block)

        return carry

    wins = []
    keep_p = []
    for h in range(2):
        lax.fori_loop(0, NWB - 1, near0 if h == 0 else near1, 0)
        win = kv.at[pl.ds(m if h == 0 else NBLK - 1 - m, NWB)]
        start(pltpu.make_async_copy(win, win_o.at[h], ls.at[16 + h]), wins)
        base = (m if h == 0 else NBLK - 1 - m) * BLK
        kpos = base - WIN + iota((BLK, KEYS), 1)
        qpos = base + iota((BLK, KEYS), 0)
        pos = base + iota((BLK, 1), 0)
        begin, end = jnp.zeros((BLK, 1), jnp.int32), 0
        for i in range(8):
            end = end + docs[0, i]
            begin = jnp.where(end <= pos, end, begin)
        low = jnp.maximum(begin, pos - span[0] + 1)
        keep = (kpos <= qpos) & (kpos >= low)
        for a in range(KV_HEADS):
            qs = stack_heads(q, h, a)
            k = win[:, :, a * HS : (a + 1) * HS].reshape(KEYS, HS)
            v = win[:, :, KW + a * HS : KW + (a + 1) * HS].reshape(KEYS, HS)
            sco = nt(qs, k) * SCALE
            sco = jnp.where(keep[None], sco.reshape(GROUP, BLK, KEYS), -1e30)
            e = jnp.exp(sco - jnp.max(sco, -1, keepdims=True))
            pr = (e / jnp.sum(e, -1, keepdims=True)).astype(BF).reshape(GROUP * BLK, KEYS)
            p[2 * h + a] = pr
            o = mm(pr, v).astype(BF)
            for g in range(GROUP):
                o_o[h * BLK : (h + 1) * BLK, (a * GROUP + g) * HS : (a * GROUP + g + 1) * HS] = o[
                    g * BLK : (g + 1) * BLK
                ]
        if h == 0:
            for k, t in ys:
                f = me.step("y", 4 - k)

                @pl.when(lax.div(f, 2) == me.zhi)
                def _():
                    ref = od.at[me.x, pl.ds(lax.rem(f, 2) * 8, 8)]
                    remote(ref, ref, sd.at[k], rdn.at[k], me.at(y=f)).wait_recv()

            da = Ring(me, "x", od.at[me.x], dx, ss.at[10], rs.at[10])
            da.first()
            wb.second()
            swap(oz, wb.l)
            swap(oz, wb.r)
            ez.second()
            ga2.second()

    start(pltpu.make_async_copy(p, p_o, ls.at[18]), keep_p)
    wb.last()
    swap(oz, wb.o)
    for n in range(8, 12):
        swapped(n)
    keep_o = pltpu.make_async_copy(oo, oo_o, ls.at[13])
    keep_o.start()

    ob = o_o[...]
    u3 = nt(ob, a3[...]).astype(BF)
    hid = x[...].astype(F32) + mm(ob, oo[...].reshape(D, D)) + mm(u3, bo[...])
    hid_o[...] = hid
    nv = (hid * rms(hid) * gain[...].astype(F32)).astype(BF)
    n2[:, :D] = nv
    n2[:, D:] = nt(nv, a45[...]).astype(BF)
    nz = ZGather(me, n2, xg, *nz_sems, BLK)
    nz.first()
    start(pltpu.make_async_copy(n2, xg.at[me.zlo, me.core, me.zhi], ls.at[19]), side)
    gb2.second()
    nz.second()
    da.second()
    off = FV * me.slice - 128 * window_tile(me.slice)

    def pack(r, strips, fresh):
        base = 256 * r - off
        i0 = jnp.minimum(lax.div(jnp.maximum(base, 0), 70), 11)
        if fresh:
            rw, cl = iota((256, 400), 0) + base, iota((256, 400), 1)
            i, k = i0 + lax.div(cl, 80), lax.rem(cl, 80)
            pick70[r] = jnp.where((k < 70) & (i * 70 + k == rw), 1.0, 0.0).astype(BF)
        for j in strips:
            src = od[j, pl.ds(i0, 5)].reshape(400, 384)
            at = pl.ds(pl.multiple_of(384 * j, 128), 384)
            down[256 * r : 256 * (r + 1), at] = mm(pick70[r], src).astype(BF)

    for r in range(5):
        pack(r, (da.i, da.l, da.r), True)
    nz.last()
    ez.last()
    da.last()
    for r in range(5):
        pack(r, (da.o,), False)
    keep_d = pltpu.make_async_copy(down, od_o, ls.at[20])
    keep_d.start()
    ga2.last()
    gb2.last()

    for r in (qa, qb, qa2, qb2, wa, wb, ga, gb, ga2, gb2, da):
        r.sent()
    for c in first + zc:
        c.wait_send()

    @pl.when(jnp.logical_not(keeper))
    def _():
        d_cross.wait_send()

    @pl.when(keeper)
    def _():
        for k, t in ys:
            remote(od.at[me.x, rows8], od.at[me.x, rows8], sd.at[k], rdn.at[k], me.at(y=t)).wait_send()

    def sent(k, carry):
        t = lax.rem(m + k, N_CTX)
        for half in range(2):
            block = m if half == 0 else NBLK - 1 - m

            @pl.when(reads(t, block))
            def _():
                src, dst = kv_own.at[half], kv.at[16 + block]
                remote(src, dst, sk.at[half, k], rk.at[block], (me.dp, t)).wait_send()

        return carry

    lax.fori_loop(1, N_CTX, sent, 0)
    for n, (dz, dc) in enumerate(ZK):
        z, core = me.step("z", 4 - dz if dz else 0), lax.rem(me.core + dc, 2)
        ref = oi.at[2 * lax.rem(z, 2) + core, lax.div(z, 2)]
        remote(ref, ref, si.at[n], ri.at[n], me.at(z=z, core=core)).wait_recv()
    ez.finish()
    nz.finish()
    for c in side + wins + keep_p + [keep_q, keep_o, keep_d]:
        c.wait()


def front(*args):
    outs = (
        sds((2, 2, 4, 2, 48, 2048), BF),
        sds((2, 2, 4, 2, 48, D), BF),
        sds((4, 2, 2, 4, 2, 48, 640), BF),
        sds((FW, D), BF),
        sds((2, 2, 2, ROWS, DX), BF),
        sds((4, 2, 8, 128), jnp.int32),
        sds((2, NWB, BLK, 2 * KW), BF),
        sds((4, GROUP * BLK, KEYS), BF),
        sds((2, 2, 2, ROWS, DX), BF),
        sds((ROWS, D), BF),
        sds((ROWS, D), BF),
        sds((ROWS, D), F32),
        sds((ROWS, DX), BF),
        sds((ROWS, D), BF),
        sds((ROWS, D), BF),
        sds((ROWS, DX), BF),
        sds((EXT, D), BF),
        sds((EXT, D), BF),
        sds((R, D), BF),
        sds((R, D), BF),
        sds((3, R, D), BF),
        sds((R, 2048), BF),
    )
    four = (DMA((4,)),) * 4
    scratch = [
        pltpu.VMEM((ROWS, 2048), F32),
        pltpu.VMEM((8, 128), jnp.int32),
        pltpu.VMEM((2, 16, FF), BF),
        pltpu.VMEM((ADAPT, 6, R, D), BF),
        pltpu.VMEM((ADAPT, R, 2048), BF),
        pltpu.VMEM((ADAPT, 2, R, D), BF),
        pltpu.VMEM((4, 16, 2048), BF),
        pltpu.VMEM((4, 16, D), BF),
        pltpu.VMEM((4, 8, 16, 640), BF),
        pltpu.VMEM((80, D), BF),
        pltpu.VMEM((4, 80, 384), BF),
        pltpu.VMEM((48, 2048), BF),
        pltpu.VMEM((48, D), BF),
        pltpu.VMEM((8, 48, 640), BF),
        pltpu.VMEM((2, 2, 4, 2, 48, 2048), BF),
        pltpu.VMEM((2, 2, 4, 2, 48, D), BF),
        pltpu.VMEM((4, 16, 80, 384), BF),
        pltpu.VMEM((2, BLK, 2 * KW), BF),
        pltpu.VMEM((16 + NBLK, BLK, 2 * KW), BF),
        pltpu.VMEM((4, GROUP * BLK, KEYS), BF),
        pltpu.VMEM((FW, D), BF),
        pltpu.VMEM((5, 256, 400), BF),
        DMA((11, 4)),
        DMA((11, 4)),
        DMA((24,)),
        DMA((3, 11)),
        DMA((3, 11)),
        DMA((7,)),
        DMA((7,)),
        DMA((12,)),
        DMA((12,)),
        DMA((4,)),
        DMA((4,)),
        DMA((2, N_CTX)),
        DMA((NBLK,)),
        four,
        DMA((7,)),
        DMA((7,)),
        four,
    ]
    return pl.pallas_call(
        front_kernel,
        out_shape=outs,
        in_specs=[SM] * 3 + [VM] * 6 + [ANY] * 3 + [VM] * 5,
        out_specs=[ANY] * 9 + [VM] * 13,
        scratch_shapes=scratch,
        compiler_params=pltpu.CompilerParams(collective_id=1, has_side_effects=True, vmem_limit_bytes=VMEM_LIMIT),
    )(*args)


class Fan:
    def __init__(self, me, axis, view, send, recv):
        self.me, self.axis, self.view, self.send, self.recv = me, axis, view, send, recv
        self.i = getattr(me, axis)

    def copy(self, k, j, to):
        ref = self.view(j)
        return remote(ref, ref, self.send.at[k - 1], self.recv.at[k - 1], self.me.at(**{self.axis: to}))

    def first(self):
        self.out = []
        for k in (1, 3, 2):
            c = self.copy(k, self.i, self.me.step(self.axis, k))
            c.start()
            self.out.append(c)

    def last(self):
        for k in (1, 3, 2):
            f = self.me.step(self.axis, 4 - k)
            self.copy(k, f, f).wait_recv()

    def sent(self):
        for c in self.out:
            c.wait_send()


def norm_back(z, gain, grad):
    r = rms(z)
    t = gain * grad
    return r * t - z * (r * r * r) * jnp.mean(t * z, -1, keepdims=True)


def rear_kernel(
    xg, oe, og, wd_i, ad_all, b_all, e_i, hid_i, n2_i, q_i, o_i, p_i, win_i, wo_i, wq_i, x_i, n1_i,
    oi, a012, a3, a45, bqkv, bo, bd, gain1, gain2, cos, sin,
    out_o, gt_o, early, late,
    wgu, wdo, ad_in, b_in, ad, acc, xb, sib_out, sib_got, red, got2, ft,
    e, hid, n2, q, o, p, win, x, n1,
    gn2, ysum, gh, go, gq, gwin, got, gkv, gj, l1, l2, gf, gl1, gl2, red1, red2,
    wl, xl, ld, sb_s, sb_r, rz_s, rz_r, f_s, f_r, a_s, a_r, b_s, b_r, kv_s, kv_r, ls,
    ring_s, ring_r, fan_s, fan_r, core_s, core_r,
):
    me = Place()
    sib = me.sibling()
    m = me.ctx
    tile = window_tile(me.slice)
    off = FV * me.slice - 128 * tile
    bar = pltpu.get_barrier_semaphore()

    def hello(t, carry):
        @pl.when(t != m)
        def _():
            pl.semaphore_signal(bar, inc=1, device_id=(me.dp, t), device_id_type=MESH)

        return carry

    def load(src, dst, sem):
        c = pltpu.make_async_copy(src, dst, sem)
        c.start()
        return c

    cols = pl.ds(pl.multiple_of(tile * 128, 128), FW)
    wloads = [
        load(ad_all.at[:, :, cols], ad_in, wl.at[0]),
        load(b_all.at[:, :, :, cols], b_in, wl.at[1]),
    ]
    for k in range(4):
        wloads.append(load(og.at[k], wgu.at[pl.ds(0, D), pl.ds(640 * k, 640)], wl.at[2 + k]))
    wloads.append(load(wd_i, wdo.at[pl.ds(0, FW), pl.ds(0, D)], wl.at[6]))
    steps = [(1 - me.zlo, 1 - me.core), (1 - me.zlo, me.core), (me.zlo, 1 - me.core), (me.zlo, me.core)]

    def rows_in(n):
        zl, core = steps[n]
        return [load(src.at[zl, core], xb.at[n % 2, k], xl.at[n % 2, k]) for k, src in enumerate((xg, oe))]

    coming = [rows_in(0), rows_in(1)]
    lax.fori_loop(0, N_CTX, hello, 0)
    others = [me.at(z=me.step("z", 1)), me.at(z=me.step("z", 3)), sib]
    for d in others:
        pl.semaphore_signal(bar, inc=1, device_id=d, device_id_type=MESH)
    loads = [
        load(src, dst, ld.at[n])
        for n, (src, dst) in enumerate(
            (
                (e_i, e), (hid_i, hid), (n2_i, n2), (o_i, o), (q_i, q),
                (win_i, win), (p_i, p), (n1_i, n1), (x_i, x),
            )
        )
    ]
    for c in wloads[:2]:
        c.wait()
    row, col = iota((64, 128), 0), iota((64, 128), 1)
    choose = jnp.zeros((64, 128), F32)
    for k in range(4):
        hit = (lax.div(row, R) == k) & (lax.rem(row, R) == lax.rem(col, R)) & (lax.div(col, R) == oi[k, 0, :1, :1])
        choose += jnp.where(hit, 1.0, 0.0)
    choose = choose.astype(BF)
    fcol = iota((64, FW), 1)
    valid = (fcol >= off) & (fcol < off + FV)
    ad[:64] = jnp.where(valid, mm(choose, ad_in[...].reshape(128, FW)), 0.0).astype(BF)
    ad[64:] = jnp.zeros((64, FW), BF)
    eye = jnp.where(iota((EXT, EXT), 0) == iota((EXT, EXT), 1), 1.0, 0.0).astype(BF)
    wdo[:FW, D:] = tn(ad[...], eye).astype(BF)
    none = jnp.zeros((64, FW), BF)
    wgu[D : D + 64, :FW] = mm(choose, b_in[:, 0].reshape(128, FW)).astype(BF)
    wgu[D + 64 :, :FW] = none
    wgu[D : D + 64, FW:] = none
    wgu[D + 64 :, FW:] = mm(choose, b_in[:, 1].reshape(128, FW)).astype(BF)
    acc[...] = jnp.zeros_like(acc)
    for c in wloads[2:6]:
        c.wait()
    sib_copies, z_copies = [], []

    def z_push(j, k, slot, z):
        c = remote(red.at[j, k], got2.at[slot, k], rz_s.at[j, k], rz_r.at[slot, k], me.at(z=z))
        c.start()
        z_copies.append(c)

    for n in range(4):
        for c in coming[n]:
            c.wait()
        xv = xb[n % 2, 0].reshape(2 * ROWS, DX)
        ev = xb[n % 2, 1].reshape(2 * ROWS, DX)
        both = mm(xv, wgu[...])
        gate, up = both[:, :FW], both[:, FW:]
        if n == 0:
            wloads[6].wait()
        gm = nt(ev, wdo[:FW])
        sig = 1.0 / (1.0 + jnp.exp(-gate))
        sl = gate * sig
        act = (sl * up).astype(BF)
        gg = (gm * up * (sig * (1.0 + gate * (1.0 - sig)))).astype(BF)
        gu = (gm * sl).astype(BF)
        grads = jnp.concatenate([gg, gu], 1)
        acc[0] += tn(ev[:, D:], act)[:64]
        by_u = tn(xv[:, D:], grads)
        acc[1] += by_u[:64, :FW]
        acc[2] += by_u[64:, FW:]
        if n < 2:
            coming.append(rows_in(n + 2))
        if n == 0:
            pl.semaphore_wait(bar, N_CTX - 1 + len(others))
        for k in (1, 0):
            wide = nt(grads, wgu[...]) if k == 1 else mm(act, wdo[:FW])
            total = gn2 if k == 1 else ysum
            if n % 2 == 0:
                for zh in range(2):
                    rows = slice(zh * ROWS, (zh + 1) * ROWS)
                    sib_out[n // 2, k, zh] = wide[rows].astype(BF)
                c = remote(sib_out.at[n // 2, k], sib_got.at[n // 2, k], sb_s.at[n // 2, k], sb_r.at[n // 2, k], sib)
                c.start()
                sib_copies.append(c)
            else:
                theirs = sib_got.at[n // 2, k]
                remote(theirs, theirs, sb_s.at[n // 2, k], sb_r.at[n // 2, k], sib).wait_recv()
                if n == 1:
                    for zh in range(2):
                        rows = slice(zh * ROWS, (zh + 1) * ROWS)
                        red[zh, k] = (wide[rows] + theirs[zh].astype(F32)).astype(BF)
                        z_push(zh, k, me.zhi, 2 * zh + 1 - me.zlo)
                else:
                    mine = me.zhi == 1
                    far = jnp.where(mine, wide[:ROWS], wide[ROWS:])
                    near = jnp.where(mine, wide[ROWS:], wide[:ROWS])
                    red[2, k] = (far + theirs[1 - me.zhi].astype(F32)).astype(BF)
                    z_push(2, k, 2, me.step("z", 2))
                    total[...] = near + theirs[me.zhi].astype(F32)
    for k in range(3):
        v = jnp.where(valid, acc[k], 0.0).astype(BF)
        for i in range(4):
            for t in range(10):
                ft[i * 30 + k * 10 + t] = v[R * i : R * (i + 1), 128 * t : 128 * (t + 1)]
    for t in range(120, 128):
        ft[t] = jnp.zeros((R, 128), BF)
    xy = me.y * 4 + me.x

    def plane(k):
        return me.at(x=lax.rem(k, 4), y=lax.div(k, 4))

    def f_copy(t):
        return remote(ft.at[pl.ds(8 * t, 8)], gf.at[xy], f_s.at[t], f_r.at[xy], plane(t))

    def f_send(k, carry):
        f_copy(lax.rem(xy + k, 16)).start()
        return carry

    lax.fori_loop(1, 16, f_send, 0)
    gf[xy] = ft[pl.ds(8 * xy, 8)]
    wo_load = load(wo_i, wdo.at[:, pl.ds(0, D)], ld.at[9])
    wq_load = load(wq_i, wgu.at[pl.ds(0, D), pl.ds(0, 2048)], ld.at[10])

    def z_take(k, total):
        for slot in range(3):
            ref = got2.at[slot, k]
            remote(ref, ref, rz_s.at[slot, k], rz_r.at[slot, k], sib).wait_recv()
            total[...] += ref[...].astype(F32)

    z_take(1, gn2)
    for c in loads[:4] + [wo_load]:
        c.wait()

    def put(tiles, at, v):
        for t in range(v.shape[1] // 128):
            tiles[at + t] = v[:, 128 * t : 128 * (t + 1)].astype(BF)

    gue = gn2[:, D:].astype(BF)
    gn = gn2[:, :D] + mm(gue, a45[...])
    ghv = e[:, :D].astype(F32) + norm_back(hid[...], gain2[...].astype(F32), gn)
    gh[...] = ghv
    ghb = ghv.astype(BF)
    ob = o[...]
    gu3 = nt(ghb, bo[...]).astype(BF)
    go[...] = (nt(ghb, wdo[:, :D]) + mm(gu3, a3[...])).astype(BF)
    u3 = nt(ob, a3[...]).astype(BF)
    s = me.dp

    put(l1, 0, tn(gu3, ob))
    g45b = tn(gue, n2[:, :D]).astype(BF)
    pick_own = jnp.where((iota((R, EXT), 1) == iota((R, EXT), 0) + s * R), 1.0, 0.0).astype(BF)
    pick_up = jnp.where((iota((R, EXT), 1) == iota((R, EXT), 0) + s * R + 64), 1.0, 0.0).astype(BF)
    put(l1, 12, mm(pick_own, g45b))
    put(l1, 24, mm(pick_up, g45b))
    put(l1, 36, tn(u3, ghb))
    for t in range(48, 64):
        l1[t] = jnp.zeros((R, 128), BF)

    def l_copy(tiles, buf, ss, rs, t):
        return remote(tiles.at[pl.ds(2 * t, 2)], buf.at[m], ss.at[t], rs.at[m], (me.dp, t))

    def l_send(tiles, buf, ss, rs):
        def one(k, carry):
            l_copy(tiles, buf, ss, rs, lax.rem(m + k, N_CTX)).start()
            return carry

        lax.fori_loop(1, N_CTX, one, 0)
        buf[m] = tiles[pl.ds(2 * m, 2)]

    def l_sum(buf, ss, rs):
        def one(k, carry):
            t = lax.rem(m + k, N_CTX)
            remote(buf.at[t], buf.at[t], ss.at[t], rs.at[t], (me.dp, t)).wait_recv()
            return carry + buf[t].astype(F32)

        return lax.fori_loop(1, N_CTX, one, buf[m].astype(F32)).astype(BF)

    def l_sent(tiles, buf, ss, rs):
        def one(k, carry):
            l_copy(tiles, buf, ss, rs, lax.rem(m + k, N_CTX)).wait_send()
            return carry

        lax.fori_loop(1, N_CTX, one, 0)

    l_send(l1, gl1, a_s, a_r)

    def covers(t, w, owner, h):
        block = owner if h == 0 else NBLK - 1 - owner
        j = block - ((t if w == 0 else NBLK - 1 - t) - (NWB - 1))
        ok = (j >= 0) & (j < NWB)
        return j, ok if w == 0 else ok & (block > t)

    def kv_copy(w, h, t, j):
        return remote(gwin.at[w, j], got.at[h, w, j], kv_s.at[h, w, t], kv_r.at[h, w, j], (me.dp, t))

    for c in loads[4:7]:
        c.wait()
    for w in (1, 0):
        for a in range(KV_HEADS):
            qs, gv, ov = stack_heads(q, w, a), stack_heads(go, w, a), stack_heads(o, w, a)
            k = win[w, :, :, a * HS : (a + 1) * HS].reshape(KEYS, HS)
            v = win[w, :, :, KW + a * HS : KW + (a + 1) * HS].reshape(KEYS, HS)
            pr = p[2 * w + a]
            delta = jnp.sum(gv.astype(F32) * ov.astype(F32), -1, keepdims=True)
            ds = (pr.astype(F32) * (nt(gv, v) - delta)).astype(BF)
            gqv = mm(ds, k) * SCALE
            for g in range(GROUP):
                cols = slice((a * GROUP + g) * HS, (a * GROUP + g + 1) * HS)
                gq[w * BLK : (w + 1) * BLK, cols] = gqv[g * BLK : (g + 1) * BLK]
            gwin[w, :, :, a * HS : (a + 1) * HS] = (tn(ds, qs) * SCALE).astype(BF).reshape(NWB, BLK, HS)
            gwin[w, :, :, KW + a * HS : KW + (a + 1) * HS] = tn(pr, gv).astype(BF).reshape(NWB, BLK, HS)

        if w == 0:
            def both_windows(j, carry):
                j1 = j + 2 * m - (NBLK - 1)

                @pl.when(j1 >= 0)
                def _():
                    gwin[0, j] = (gwin[0, j].astype(F32) + gwin[1, j1].astype(F32)).astype(BF)

                return carry

            lax.fori_loop(0, NWB, both_windows, 0)

        def kv_send(k, carry):
            t = lax.rem(m + k, N_CTX)
            for h in range(2):
                j, ok = covers(m, w, t, h)

                @pl.when(ok)
                def _():
                    kv_copy(w, h, t, j).start()

            return carry

        lax.fori_loop(1, N_CTX, kv_send, 0)
        for h in range(2):
            j, ok = covers(m, w, m, h)

            @pl.when(ok)
            def _():
                c = pltpu.make_async_copy(gwin.at[w, j], got.at[h, w, j], ls.at[2 * w + h])
                c.start()
                c.wait()


    def f_take(k, carry):
        t = lax.rem(xy + k, 16)
        remote(gf.at[t], gf.at[t], f_s.at[t], f_r.at[t], plane(t)).wait_recv()
        return carry + gf[t].astype(F32)

    red1[:8] = lax.fori_loop(1, 16, f_take, gf[xy].astype(F32)).astype(BF)
    red1[8:] = l_sum(gl1, a_s, a_r)

    def vz(j, h):
        ref = early.at[me.y, me.x, lax.rem(j, 2), me.core, lax.div(j, 2)]
        return ref if h is None else ref.at[pl.ds(5 * h, 5)]

    own_e = pltpu.make_async_copy(red1, vz(me.z, None), ls.at[5])
    own_e.start()
    rz = Ring(me, "z", red1, vz, ring_s.at[0], ring_r.at[0])
    rz.first()
    ta, tb = pl.ds(0, 5), pl.ds(5, 5)

    def x0(j, h):
        return early.at[me.y, j, :, me.core, :, ta] if h is None else early.at[me.y, j, h, me.core, :, ta]

    def y0(j, h):
        return early.at[j, :, :, me.core, :, ta] if h is None else early.at[j, pl.ds(2 * h, 2), :, me.core, :, ta]

    def y1(j, h):
        return early.at[j, me.x, :, me.core, :, tb] if h is None else early.at[j, me.x, h, me.core, :, tb]

    def x1(j, h):
        return early.at[:, j, :, me.core, :, tb] if h is None else early.at[pl.ds(2 * h, 2), j, :, me.core, :, tb]

    gkv[...] = jnp.zeros_like(gkv)

    def take(k, carry):
        t = lax.rem(m + N_CTX - k, N_CTX)
        for w in range(2):
            for h in range(2):
                j, ok = covers(t, w, m, h)

                @pl.when(ok & (k > 0))
                def _():
                    ref = got.at[h, w, j]
                    remote(ref, ref, kv_s.at[h, w, t], kv_r.at[h, w, j], (me.dp, t)).wait_recv()

                @pl.when(ok)
                def _():
                    gkv[h] += got[h, w, j].astype(F32)

        return carry

    lax.fori_loop(0, N_CTX, take, 0)

    for c in loads[7:] + [wq_load]:
        c.wait()
    c, sn = cos[...], sin[...]
    for h in range(HEADS):
        cols = slice(h * HS, (h + 1) * HS)
        gj[:, cols] = turn_back(gq[:, cols], c, sn).astype(BF)
    for a in range(KV_HEADS):
        v = jnp.concatenate([gkv[0, :, a * HS : (a + 1) * HS], gkv[1, :, a * HS : (a + 1) * HS]], 0)
        gj[:, QW + a * HS : QW + (a + 1) * HS] = turn_back(v, c, sn).astype(BF)
    gj[:, QW + KW :] = jnp.concatenate([gkv[0, :, KW:], gkv[1, :, KW:]], 0).astype(BF)
    n1b = n1[...]
    more = jnp.zeros((ROWS, D), F32)
    for i, (lo, hi) in enumerate(((0, QW), (QW, QW + KW), (QW + KW, QW + 2 * KW))):
        am = a012[i]
        u = nt(n1b, am).astype(BF)
        gjm = gj[:, lo:hi]
        gum = nt(gjm, bqkv[:, lo:hi]).astype(BF)
        more += mm(gum, am)
        put(l2, 36 + lo // 128, tn(u, gjm))
        put(l2, 12 * i, tn(gum, n1b))
    z_take(0, ysum)
    ud = ysum[:, D:].astype(BF)
    y = hid[...] + ysum[:, :D] + mm(ud, bd[...])
    for h in range(2):
        out_o[:, h, :] = y[h * BLK : (h + 1) * BLK].astype(BF)
    put(l2, 52, mm(pick_own, tn(ud, e[:, :D]).astype(BF)))
    l_send(l2, gl2, b_s, b_r)
    rz.second()
    rz.last()
    own_e.wait()
    ra = Ring(me, "x", x0(me.x, None), x0, ring_s.at[1], ring_r.at[1])
    rb = Ring(me, "y", y1(me.y, None), y1, ring_s.at[2], ring_r.at[2])
    ra.first()
    rb.first()

    gn = nt(gj[...], wgu[:D, :2048]) + more
    gt = gh[...] + norm_back(x[...].astype(F32), gain1[...].astype(F32), gn)
    for h in range(2):
        gt_o[:, h, :] = gt[h * BLK : (h + 1) * BLK].astype(BF)

    ra.second()
    rb.second()
    red2[...] = l_sum(gl2, b_s, b_r)

    def uz(j):
        return late.at[me.y, me.x, lax.rem(j, 2), me.core, lax.div(j, 2)]

    own_l = pltpu.make_async_copy(red2, uz(me.z), ls.at[6])
    own_l.start()
    own_l.wait()
    def f_sent(k, carry):
        f_copy(lax.rem(xy + k, 16)).wait_send()
        return carry

    def kv_sent(k, carry):
        t = lax.rem(m + k, N_CTX)
        for w in range(2):
            for h in range(2):
                j, ok = covers(m, w, t, h)

                @pl.when(ok)
                def _():
                    kv_copy(w, h, t, j).wait_send()

        return carry

    fz = Fan(me, "z", uz, fan_s.at[0], fan_r.at[0])
    fz.first()
    ra.last()
    rb.last()
    rc = Ring(me, "y", y0(me.y, None), y0, ring_s.at[3], ring_r.at[3])
    rd = Ring(me, "x", x1(me.x, None), x1, ring_s.at[4], ring_r.at[4])
    rc.first()
    rd.first()
    swaps = []

    def swap(view, j):
        n = len(swaps)
        c = remote(view(j, me.core), view(j, me.core), core_s.at[n], core_r.at[n], sib)
        c.start()
        swaps.append((c, view, j))

    def ey(j, core):
        return early.at[j, :, :, core, :, ta]

    def ex(j, core):
        return early.at[:, j, :, core, :, tb]

    def late_all(j, core):
        return late.at[j, :, :, core]

    swap(ey, me.y)
    swap(ex, me.x)
    l_sent(l1, gl1, a_s, a_r)
    lax.fori_loop(1, 16, f_sent, 0)
    fz.last()
    t0, t1 = pl.ds(0, 1), pl.ds(1, 1)
    fx = Fan(me, "x", lambda j: late.at[me.y, j, :, me.core, :, t0], fan_s.at[1], fan_r.at[1])
    fy = Fan(me, "y", lambda j: late.at[j, me.x, :, me.core, :, t1], fan_s.at[2], fan_r.at[2])
    fx.first()
    fy.first()
    lax.fori_loop(1, N_CTX, kv_sent, 0)
    rc.second()
    rd.second()
    swap(ey, rc.l)
    swap(ex, rd.l)
    swap(ey, rc.r)
    swap(ex, rd.r)
    fx.last()
    fy.last()
    fy2 = Fan(me, "y", lambda j: late.at[j, :, :, me.core, :, t0], fan_s.at[3], fan_r.at[3])
    fx2 = Fan(me, "x", lambda j: late.at[:, j, :, me.core, :, t1], fan_s.at[4], fan_r.at[4])
    fy2.first()
    fx2.first()
    l_sent(l2, gl2, b_s, b_r)
    rc.last()
    rd.last()
    swap(ey, rc.o)
    swap(ex, rd.o)
    fy2.last()
    fx2.last()
    for k in range(4):
        swap(late_all, k)

    for c in sib_copies + z_copies:
        c.wait_send()
    for r in (rz, ra, rb, rc, rd, fz, fx, fy, fx2, fy2):
        r.sent()


    for n, (c, view, j) in enumerate(swaps):
        c.wait_send()
        ref = view(j, 1 - me.core)
        remote(ref, ref, core_s.at[n], core_r.at[n], sib).wait_recv()


def rear(xg, oe, og, wd, ad_all, b_all, e, hid, n2, q, o, p, win, wo, wq, x, n1, *small):
    outs = (
        sds((BLK, 2, D), BF),
        sds((BLK, 2, D), BF),
        sds((4, 4, 2, 2, 2, 10, R, 128), BF),
        sds((4, 4, 2, 2, 2, 2, R, 128), BF),
    )
    block = (ROWS, DX)
    scratch = [
        pltpu.VMEM((DX, 2 * FW), BF),
        pltpu.VMEM((D, DX), BF),
        pltpu.VMEM((ADAPT, R, FW), BF),
        pltpu.VMEM((ADAPT, 2, R, FW), BF),
        pltpu.VMEM((EXT, FW), BF),
        pltpu.VMEM((3, 64, FW), F32),
        pltpu.VMEM((2, 2, 2) + block, BF),
        pltpu.VMEM((2, 2, 2) + block, BF),
        pltpu.VMEM((2, 2, 2) + block, BF),
        pltpu.VMEM((3, 2) + block, BF),
        pltpu.VMEM((3, 2) + block, BF),
        pltpu.VMEM((128, R, 128), BF),
    ]
    scratch += [pltpu.VMEM(v.shape, v.dtype) for v in (e, hid, n2, q, o, p, win, x, n1)]
    scratch += [
        pltpu.VMEM(block, F32),
        pltpu.VMEM(block, F32),
        pltpu.VMEM((ROWS, D), F32),
        pltpu.VMEM((ROWS, D), BF),
        pltpu.VMEM((ROWS, D), F32),
        pltpu.VMEM((2, NWB, BLK, 2 * KW), BF),
        pltpu.VMEM((2, 2, NWB, BLK, 2 * KW), BF),
        pltpu.VMEM((2, BLK, 2 * KW), F32),
        pltpu.VMEM((ROWS, 2048), BF),
        pltpu.VMEM((64, R, 128), BF),
        pltpu.VMEM((64, R, 128), BF),
        pltpu.VMEM((16, 8, R, 128), BF),
        pltpu.VMEM((N_CTX, 2, R, 128), BF),
        pltpu.VMEM((N_CTX, 2, R, 128), BF),
        pltpu.VMEM((10, R, 128), BF),
        pltpu.VMEM((2, R, 128), BF),
        DMA((7,)),
        DMA((2, 2)),
        DMA((11,)),
        DMA((2, 2)),
        DMA((2, 2)),
        DMA((3, 2)),
        DMA((3, 2)),
        DMA((16,)),
        DMA((16,)),
        DMA((N_CTX,)),
        DMA((N_CTX,)),
        DMA((N_CTX,)),
        DMA((N_CTX,)),
        DMA((2, 2, N_CTX)),
        DMA((2, 2, NWB)),
        DMA((7,)),
        DMA((5, 4)),
        DMA((5, 4)),
        DMA((5, 3)),
        DMA((5, 3)),
        DMA((12,)),
        DMA((12,)),
    ]
    return pl.pallas_call(
        rear_kernel,
        out_shape=outs,
        in_specs=[ANY] * 17 + [VM] * len(small),
        out_specs=[VM, VM, ANY, ANY],
        scratch_shapes=scratch,
        compiler_params=pltpu.CompilerParams(collective_id=2, has_side_effects=True, vmem_limit_bytes=VMEM_LIMIT),
    )(xg, oe, og, wd, ad_all, b_all, e, hid, n2, q, o, p, win, wo, wq, x, n1, *small)


def spread_kernel(oi, early, late, ain_o, aff_o, bqkv_o, bres_o, bff_o):
    e = pl.program_id(0)
    for ref in (ain_o, aff_o, bqkv_o, bres_o, bff_o):
        ref[...] = jnp.zeros_like(ref)

    def local_tile(ref, at, s, n):
        k, j = n // 2, n % 2
        return ref[k // 8, k % 4, s // 2, s % 2, (k // 4) % 2, at + j].astype(F32)

    def ff_tile(piece, n):
        k, j = n // 8, n % 8
        return early[k // 4, k % 4, piece // 4, (piece // 2) % 2, piece % 2, j].astype(F32)

    for s in range(4):

        @pl.when(oi[s, 0, 0, 0] == e)
        def _():
            for c in range(12):
                cols = slice(128 * c, 128 * (c + 1))
                for m in range(3):
                    ain_o[0, m, :, cols] += local_tile(late, 0, s, 12 * m + c)
                    ain_o[0, 3 + m, :, cols] += local_tile(early, 8, s, 12 * m + c)
                bres_o[0, 0, :, cols] += local_tile(early, 8, s, 36 + c)
                bres_o[0, 1, :, cols] += local_tile(late, 0, s, 52 + c)
            for c in range(16):
                bqkv_o[0, :, 128 * c : 128 * (c + 1)] += local_tile(late, 0, s, 36 + c)
            for piece in range(8):
                tile = 60 if piece == 7 else 35 * piece // 4
                for k in range(3):
                    for c in range(10):
                        cols = slice(128 * (tile + c), 128 * (tile + c + 1))
                        v = ff_tile(piece, s * 30 + k * 10 + c)
                        if k == 0:
                            aff_o[0, :, cols] += v
                        else:
                            bff_o[0, k - 1, :, cols] += v


def spread(oi, early, late):
    outs = (
        sds((ADAPT, 6, R, D), F32),
        sds((ADAPT, R, FF), F32),
        sds((ADAPT, R, 2048), F32),
        sds((ADAPT, 2, R, D), F32),
        sds((ADAPT, 2, R, FF), F32),
    )

    def one(shape):
        return pl.BlockSpec((1,) + shape[1:], lambda i: (i,) + (0,) * (len(shape) - 1))

    return pl.pallas_call(
        spread_kernel,
        out_shape=outs,
        grid=(ADAPT,),
        in_specs=[
            SM,
            pl.BlockSpec(early.shape, lambda i: (0,) * 8),
            pl.BlockSpec(late.shape, lambda i: (0,) * 8),
        ],
        out_specs=[one(o.shape) for o in outs],
        compiler_params=pltpu.CompilerParams(vmem_limit_bytes=VMEM_LIMIT),
    )(oi, early, late)


def local(
    tokens,
    cotangent,
    w_qkv,
    b_qkv,
    w_out,
    w_gu,
    w_down,
    gain_attn,
    gain_mlp,
    adapt_in,
    adapt_in_ff,
    adapt_out_qkv,
    adapt_out_res,
    adapt_out_ff,
    doc_lengths,
    adapter_index,
    window,
):
    member = lax.axis_index("ctx")
    starts = jnp.stack([member * BLK, (NBLK - 1 - member) * BLK])
    pos = (starts[:, None] + jnp.arange(BLK, dtype=jnp.int32)[None]).reshape(ROWS)
    freq = 1000000.0 ** (-(2.0 * jnp.arange(HS // 2, dtype=F32)) / HS)
    ang = pos.astype(F32)[:, None] * freq[None]
    c, sn = jnp.cos(ang), jnp.sin(ang)
    cos = jnp.concatenate([c, c], -1)
    sin = jnp.concatenate([-sn, sn], -1)

    (
        oq, oo, og, down, oe, oi, wins, p, xg, q, o, hid, n2,
        x, n1, eext, a45, bd, a3, bo, a012, bqkv,
    ) = front(
        adapter_index, doc_lengths, window, w_qkv, w_out, w_gu, w_down, tokens[0], cotangent[0],
        adapt_in, adapt_out_qkv, adapt_out_res, gain_attn, b_qkv, cos, sin, gain_mlp,
    )
    oq = oq.reshape(D, 2048)
    oo = oo.reshape(D, D)
    og = og.reshape(4, D, 640)
    out, gt, early, late = rear(
        xg, oe, og, down, adapt_in_ff, adapt_out_ff, eext, hid, n2, q, o, p, wins, oo, oq, x, n1,
        oi, a012, a3, a45, bqkv, bo, bd, gain_attn, gain_mlp, cos, sin,
    )
    return (out[None], gt[None]) + tuple(spread(oi, early, late))


def solution(mesh):
    return jax.shard_map(
        local,
        mesh=mesh,
        in_specs=(
            P("dp", "ctx", None, None),
            P("dp", "ctx", None, None),
            P(("dp", "ctx"), None),
            P(),
            P(("dp", "ctx"), None),
            P(("dp", "ctx"), None, None),
            P(("dp", "ctx"), None),
            P(),
            P(),
            P(),
            P(),
            P(),
            P(),
            P(),
            P("dp", None),
            P("dp"),
            P("dp"),
        ),
        out_specs=(P("dp", "ctx", None, None), P("dp", "ctx", None, None), P(), P(), P(), P(), P()),
        check_vma=False,
    )
```

```python
import functools

import jax
import jax.numpy as jnp
from jax import lax
from jax.experimental import pallas as pl
from jax.experimental.pallas import tpu as pltpu
from jax.sharding import PartitionSpec as P

D = 1536
HEADS = 12
KV_HEADS = 2
HS = 128
GROUP = HEADS // KV_HEADS
FF = 8960
R = 16
ADAPT = 8
BLK = 64
ROWS = 2 * BLK
N_CTX = 32
NBLK = 2 * N_CTX
WIN = 1024
NWB = WIN // BLK + 1
KEYS = NWB * BLK
EXT = 128
DX = D + EXT
FW = 1280
FV = FF // 8
QW = HEADS * HS
KW = KV_HEADS * HS
SCALE = HS**-0.5
EPS = 1e-6

MESH = pl.DeviceIdType.MESH
BF = jnp.bfloat16
F32 = jnp.float32
ANY = pl.BlockSpec(memory_space=pl.ANY)
VM = pl.BlockSpec(memory_space=pltpu.VMEM)
SM = pl.BlockSpec(memory_space=pltpu.SMEM)
DMA = pltpu.SemaphoreType.DMA
VMEM_LIMIT = 60 * 2**20


def sds(shape, dtype):
    return jax.ShapeDtypeStruct(shape, dtype)


def nt(a, b):
    return lax.dot_general(a, b, (((1,), (1,)), ((), ())), preferred_element_type=F32)


def tn(a, b):
    return lax.dot_general(a, b, (((0,), (0,)), ((), ())), preferred_element_type=F32)


def mm(a, b):
    return jnp.dot(a, b, preferred_element_type=F32)


def iota(shape, dim):
    return lax.broadcasted_iota(jnp.int32, shape, dim)


class Place:
    def __init__(self):
        dp, ctx = lax.axis_index("dp"), lax.axis_index("ctx")
        self.dp, self.ctx = dp, ctx
        self.zlo, self.core = lax.div(dp, 2), lax.rem(dp, 2)
        self.y, self.zhi, self.x = lax.div(ctx, 8), lax.rem(lax.div(ctx, 4), 2), lax.rem(ctx, 4)
        self.z = self.zhi * 2 + self.zlo
        self.slice = 2 * dp + self.zhi

    def at(self, x=None, y=None, z=None, core=None):
        x = self.x if x is None else x
        y = self.y if y is None else y
        z = self.z if z is None else z
        core = self.core if core is None else core
        return (lax.rem(z, 2) * 2 + core, y * 8 + lax.div(z, 2) * 4 + x)

    def step(self, axis, by):
        return lax.rem(getattr(self, axis) + by, 4)

    def ring(self, axis):
        return [self.at(**{axis: self.step(axis, k)}) for k in (1, 2, 3)]

    def sibling(self):
        return self.at(core=1 - self.core)


def window_tile(piece):
    return jnp.minimum(lax.div(35 * piece, 4), 60)


def remote(src, dst, send, recv, device):
    return pltpu.make_async_remote_copy(
        src_ref=src, dst_ref=dst, send_sem=send, recv_sem=recv, device_id=device, device_id_type=MESH
    )


def greet(peers):
    sem = pltpu.get_barrier_semaphore()
    for device in peers:
        pl.semaphore_signal(sem, inc=1, device_id=device, device_id_type=MESH)
    pl.semaphore_wait(sem, len(peers))


class Ring:
    def __init__(self, me, axis, own, view, send, recv):
        self.i = getattr(me, axis)
        self.r, self.o, self.l = (me.step(axis, k) for k in (1, 2, 3))
        self.right, self.left = me.at(**{axis: self.r}), me.at(**{axis: self.l})
        self.own, self.view, self.send, self.recv = own, view, send, recv

    def copy(self, k, src, dst, device):
        return remote(src, dst, self.send.at[k], self.recv.at[k], device)

    def first(self):
        place = self.view(self.i, None)
        self.out = [self.copy(0, self.own, place, self.right), self.copy(1, self.own, place, self.left)]
        for c in self.out:
            c.start()

    def second(self):
        v = self.view
        self.copy(0, v(self.l, None), v(self.l, None), self.right).wait_recv()
        c = self.copy(2, v(self.l, 0), v(self.l, 0), self.right)
        c.start()
        self.out.append(c)
        self.copy(1, v(self.r, None), v(self.r, None), self.left).wait_recv()
        c = self.copy(3, v(self.r, 1), v(self.r, 1), self.left)
        c.start()
        self.out.append(c)

    def last(self):
        v = self.view
        self.copy(2, v(self.o, 0), v(self.o, 0), self.right).wait_recv()
        self.copy(3, v(self.o, 1), v(self.o, 1), self.left).wait_recv()

    def sent(self):
        for c in self.out:
            c.wait_send()


class ZGather:
    def __init__(self, me, own, buf, send, recv, core_send, core_recv, half):
        self.me, self.own, self.buf = me, own, buf
        self.cs, self.cr = core_send, core_recv

        def view(j, h, core=me.core):
            ref = buf.at[lax.rem(j, 2), core, lax.div(j, 2)]
            return ref if h is None else ref.at[pl.ds(h * half, half)]

        self.view = view
        self.ring = Ring(me, "z", own, view, send, recv)
        self.out = []

    def swap(self, src, j):
        c = remote(src, self.view(j, None), self.cs.at[len(self.out)], self.cr.at[len(self.out)], self.me.sibling())
        c.start()
        self.out.append((c, j))

    def first(self):
        self.ring.first()
        self.swap(self.own, self.me.z)

    def second(self):
        self.ring.second()
        self.swap(self.view(self.ring.l, None), self.ring.l)
        self.swap(self.view(self.ring.r, None), self.ring.r)

    def last(self):
        self.ring.last()
        self.swap(self.view(self.ring.o, None), self.ring.o)

    def finish(self):
        self.ring.sent()
        for k, (c, j) in enumerate(self.out):
            c.wait_send()
            place = self.view(j, None, 1 - self.me.core)
            remote(place, place, self.cs.at[k], self.cr.at[k], self.me.sibling()).wait_recv()


def rms(z):
    return lax.rsqrt(jnp.mean(z * z, -1, keepdims=True) + EPS)


def turn(v, cos, sin):
    return v * cos + pltpu.roll(v, 64, 1) * sin


def turn_back(v, cos, sin):
    return v * cos - pltpu.roll(v, 64, 1) * sin


def stack_heads(ref, h, a):
    rows = slice(h * BLK, (h + 1) * BLK)
    return jnp.concatenate(
        [ref[rows, (a * GROUP + g) * HS : (a * GROUP + g + 1) * HS] for g in range(GROUP)], 0
    )


def reads(t, block):
    a, b = t - block, NBLK - 1 - t - block
    return ((a >= 0) & (a < NWB)) | ((b >= 0) & (b < NWB))


ZK = [(dz, dc) for dz in range(4) for dc in range(2) if dz or dc]


def front_kernel(
    idx_i, docs, span, wq_i, wo_i, wg_i, wd_i, tok, cot, ain_i, aqkv_i, ares_i, gain1, bias, cos, sin, gain,
    oq_o, oo_o, og, od_o, oe, oi, win_o, p_o, xg, q_h, o_h, hid_h, n2_h,
    x_h, n1_h, e_h, a45_h, bd_h, a3_h, bo_h, a012_h, bqkv_h,
    q, o_o, hid_o, n2, x, n1, eext, a45, bd, a3, bo, a012, bqkv, keep_s,
    ub, idx, wg, ain, aqkv, ares, rq, ro, rg, wdp, rd, cq, co, cg, oq, oo, od, kv_own, kv, p, down, pick70,
    ss, rs, ls, s1, r1, s2, r2, sc, rc, sd, rdn, sk, rk, ez_sems, si, ri, nz_sems,
):
    me = Place()
    sib = me.sibling()
    m = me.ctx
    bar = pltpu.get_barrier_semaphore()

    def hello(t, carry):
        @pl.when(t != m)
        def _():
            pl.semaphore_signal(bar, inc=1, device_id=(me.dp, t), device_id_type=MESH)

        return carry

    lax.fori_loop(0, N_CTX, hello, 0)
    others = [me.at(z=me.step("z", dz), core=lax.rem(me.core + dc, 2)) for dz, dc in ZK if dz % 2 or dc]
    for d in others:
        pl.semaphore_signal(bar, inc=1, device_id=d, device_id_type=MESH)

    adapters = []
    for n, (src, dst) in enumerate(((ain_i, ain), (aqkv_i, aqkv), (ares_i, ares))):
        adapters.append(pltpu.make_async_copy(src, dst, ls.at[21 + n]))
        adapters[-1].start()
    rq[me.x, :12] = wq_i[...]
    rq[me.x, 12:] = jnp.zeros((4, 2048), BF)
    ro[me.x, :12] = wo_i[...]
    ro[me.x, 12:] = jnp.zeros((4, D), BF)
    wdp[:70] = wd_i[...]
    wdp[70:] = jnp.zeros((10, D), BF)
    idx[...] = jnp.full((8, 128), idx_i[0], jnp.int32)

    pl.semaphore_wait(bar, N_CTX - 1 + len(others))

    tiles = [60 if g == 7 else 35 * g // 4 for g in range(8)]

    def panel(g, t):
        col = pl.multiple_of(tiles[g] * 128 + lax.rem(t, 2) * 640, 128)
        return wg.at[lax.div(t, 2), :, pl.ds(col, 640)]

    def strip(t):
        return wdp.at[:, pl.ds(pl.multiple_of(384 * t, 128), 384)]

    def start(c, out):
        c.start()
        out.append(c)

    first = []
    xs = [(k, me.step("x", k), me.at(x=me.step("x", k))) for k in (1, 3, 2)]
    for k, t, d in xs:
        start(remote(rq.at[me.x], rq.at[me.x], s1.at[k - 1, 0], r1.at[k - 1, 0], d), first)
    for k in range(2):
        wg[k, :12] = wg_i[:, k, :]
        wg[k, 12:] = jnp.zeros((4, FF), BF)
    for k, t, d in xs:
        for g in range(8):
            start(remote(panel(g, t), rg.at[me.x, g], s1.at[k - 1, 2 + g], r1.at[k - 1, 2 + g], d), first)
        start(remote(strip(t), rd.at[me.x], s1.at[k - 1, 10], r1.at[k - 1, 10], d), first)
    for k, t, d in xs:
        start(remote(ro.at[me.x], ro.at[me.x], s1.at[k - 1, 1], r1.at[k - 1, 1], d), first)
    mine = []
    for g in range(8):
        start(pltpu.make_async_copy(panel(g, me.x), rg.at[me.x, g], ls.at[2 + g]), mine)
    start(pltpu.make_async_copy(strip(me.x), rd.at[me.x], ls.at[1]), mine)
    side = []
    start(pltpu.make_async_copy(idx, oi.at[me.dp, me.zhi], ls.at[11]), side)
    for n, (dz, dc) in enumerate(ZK):
        d = me.at(z=me.step("z", dz), core=lax.rem(me.core + dc, 2))
        start(remote(idx, oi.at[me.dp, me.zhi], si.at[n], ri.at[n], d), first)

    def from_x(n, ref_of):
        for k in (1, 3, 2):
            f = me.step("x", 4 - k)
            ref = ref_of(f)
            remote(ref, ref, s1.at[k - 1, n], r1.at[k - 1, n], me.at(x=f)).wait_recv()

    row, col = iota((48, 64), 0), iota((48, 64), 1)
    put = jnp.where(
        (lax.rem(col, 16) < 12) & (lax.div(col, 16) * 12 + lax.rem(col, 16) == row), 1.0, 0.0
    ).astype(BF)

    kv[:16] = jnp.zeros((16, BLK, 2 * KW), BF)
    for h in range(2):
        rows = slice(h * BLK, (h + 1) * BLK)
        x[rows] = tok[:, h, :]
        eext[rows, :D] = cot[:, h, :]
    xf = x[...].astype(F32)
    n1[...] = (xf * rms(xf) * gain1[...].astype(F32)).astype(BF)
    row, col = iota((R, 128), 0), iota((R, 128), 1)
    choose = jnp.where((lax.div(col, R) == idx_i[0]) & (lax.rem(col, R) == row), 1.0, 0.0).astype(BF)

    def chosen(ref):
        return mm(choose, ref.reshape(ADAPT * R, ref.shape[-1])).astype(BF)

    for c in adapters:
        c.wait()
    for k in range(3):
        a012[k] = chosen(ain[:, k])
    a3[...] = chosen(ain[:, 3])
    at = pl.multiple_of(me.dp * R, R)
    a45[...] = jnp.zeros_like(a45)
    a45[pl.ds(at, R), :] = chosen(ain[:, 4])
    a45[pl.ds(at + 64, R), :] = chosen(ain[:, 5])
    bqkv[...] = chosen(aqkv[...])
    bo[...] = chosen(ares[:, 0])
    bd[...] = jnp.zeros_like(bd)
    bd[pl.ds(at, R), :] = chosen(ares[:, 1])
    for k, (c0, c1) in enumerate(((0, QW), (QW, QW + KW), (QW + KW, QW + 2 * KW))):
        u = nt(n1[...], a012[k]).astype(BF)
        ub[:, c0:c1] = mm(u, bqkv[:, c0:c1]) + bias[c0:c1].astype(F32)
    eext[:, D:] = nt(eext[:, :D], bd[...]).astype(BF)
    start(pltpu.make_async_copy(eext, oe.at[me.zlo, me.core, me.zhi], ls.at[10]), side)
    kept = []

    def keep_all(*pairs):
        for ref, place in pairs:
            start(pltpu.make_async_copy(ref, place, keep_s.at[len(kept)]), kept)

    keep_all(
        (x, x_h), (n1, n1_h), (eext, e_h), (a45, a45_h), (bd, bd_h), (a3, a3_h), (bo, bo_h), (a012, a012_h), (bqkv, bqkv_h)
    )
    from_x(0, lambda f: rq.at[f])
    cq[...] = mm(put, rq[...].reshape(64, 2048)).astype(BF)
    lo, hi = pl.ds(0, 1024), pl.ds(1024, 1024)

    def qy0(j, h):
        return oq.at[me.zlo, me.core, j, me.zhi, :, lo if h is None else pl.ds(512 * h, 512)]

    def qz0(j, h, core=me.core):
        zl, zh = lax.rem(j, 2), lax.div(j, 2)
        return oq.at[zl, core, :, zh, :, lo] if h is None else oq.at[zl, core, pl.ds(2 * h, 2), zh, :, lo]

    def qz1(j, h):
        cols = hi if h is None else pl.ds(1024 + 512 * h, 512)
        return oq.at[lax.rem(j, 2), me.core, me.y, lax.div(j, 2), :, cols]

    def qy1(j, h, core=me.core):
        return oq.at[:, core, j, :, :, hi] if h is None else oq.at[h, core, j, :, :, hi]

    qa = Ring(me, "y", cq.at[:, lo], qy0, ss.at[0], rs.at[0])
    qb = Ring(me, "z", cq.at[:, hi], qz1, ss.at[1], rs.at[1])
    qa.first()
    qb.first()
    oq[me.zlo, me.core, me.y, me.zhi] = cq[...]
    qa.second()
    qb.second()
    for n in range(8):
        from_x(2 + n, lambda f: rg.at[f, n])
    from_x(10, lambda f: rd.at[f])
    for c in mine:
        c.wait()
    for g in range(8):
        cg[g] = mm(put, rg[:, g].reshape(64, 640)).astype(BF)

    own_g = pltpu.make_async_copy(cg.at[me.slice], og.at[me.x, me.zlo, me.core, me.y, me.zhi], ls.at[14])
    own_g.start()
    zc = []
    for n, (dz, dc) in enumerate(ZK):
        z, core = me.step("z", dz), lax.rem(me.core + dc, 2)
        piece = 2 * (2 * lax.rem(z, 2) + core) + lax.div(z, 2)
        d = me.at(z=z, core=core)
        start(remote(cg.at[piece], og.at[me.x, me.zlo, me.core, me.y, me.zhi], s2.at[n], r2.at[n], d), zc)
    keeper = lax.div(me.y, 2) == me.zhi
    rows4 = pl.ds(lax.rem(me.y, 2) * 8 + me.zhi * 4, 4)
    across = me.at(z=me.step("z", 2))
    d_local = pltpu.make_async_copy(rd, od.at[me.x, rows4], ls.at[15])
    d_cross = remote(rd, od.at[me.x, rows4], sd.at[0], rdn.at[0], across)

    @pl.when(keeper)
    def _():
        d_local.start()

    @pl.when(jnp.logical_not(keeper))
    def _():
        d_cross.start()

    qa.last()
    qb.last()
    qa2 = Ring(me, "z", qz0(me.z, None), qz0, ss.at[2], rs.at[2])
    qb2 = Ring(me, "y", qy1(me.y, None), qy1, ss.at[3], rs.at[3])
    qa2.first()
    qb2.first()
    swaps = []

    def swap(view, j):
        n = len(swaps)
        c = remote(view(j, None), view(j, None), sc.at[n], rc.at[n], sib)
        c.start()
        swaps.append((c, view, j))

    def swapped(n):
        c, view, j = swaps[n]
        c.wait_send()
        ref = view(j, None, 1 - me.core)
        remote(ref, ref, sc.at[n], rc.at[n], sib).wait_recv()

    swap(qz0, me.z)
    swap(qy1, me.y)
    from_x(1, lambda f: ro.at[f])
    co[...] = mm(put, ro[...].reshape(64, D)).astype(BF)
    own_g.wait()
    for n, (dz, dc) in enumerate(ZK):
        z, core = me.step("z", 4 - dz if dz else 0), lax.rem(me.core + dc, 2)
        ref = og.at[me.x, lax.rem(z, 2), core, me.y, lax.div(z, 2)]
        remote(ref, ref, s2.at[n], r2.at[n], me.at(z=z, core=core)).wait_recv()

    def g0a(j, h):
        return og.at[me.x, 0, :, j] if h is None else og.at[me.x, 0, h, j]

    def g0b(j, h):
        return og.at[j, 0] if h is None else og.at[j, 0, h]

    def g1a(j, h):
        return og.at[j, 1, :, me.y] if h is None else og.at[j, 1, h, me.y]

    def g1b(j, h):
        return og.at[:, 1, :, j] if h is None else og.at[:, 1, h, j]

    ga = Ring(me, "y", g0a(me.y, None), g0a, ss.at[4], rs.at[4])
    gb = Ring(me, "x", g1a(me.x, None), g1a, ss.at[5], rs.at[5])
    ga.first()
    gb.first()
    def oy(j, h):
        ref = oo.at[me.zlo, me.core, j, me.zhi]
        return ref if h is None else ref.at[:, pl.ds(768 * h, 768)]

    def oz(j, h, core=me.core):
        zl, zh = lax.rem(j, 2), lax.div(j, 2)
        return oo.at[zl, core, :, zh] if h is None else oo.at[zl, core, pl.ds(2 * h, 2), zh]

    wa = Ring(me, "y", co, oy, ss.at[8], rs.at[8])
    qa2.second()
    qb2.second()
    swap(qz0, qa2.l)
    swap(qy1, qb2.l)
    swap(qz0, qa2.r)
    swap(qy1, qb2.r)
    oo[me.zlo, me.core, me.y, me.zhi] = co[...]

    ga.second()
    gb.second()
    wa.first()
    ga.last()
    gb.last()
    ga2 = Ring(me, "x", g0b(me.x, None), g0b, ss.at[6], rs.at[6])
    gb2 = Ring(me, "y", g1b(me.y, None), g1b, ss.at[7], rs.at[7])

    ga2.first()
    qa2.last()
    qb2.last()
    swap(qz0, qa2.o)
    swap(qy1, qb2.o)

    wa.second()
    rows4b = pl.ds(lax.rem(me.y, 2) * 8 + (1 - me.zhi) * 4, 4)
    rows8 = pl.ds(lax.rem(me.y, 2) * 8, 8)
    ys = [(k, me.step("y", k)) for k in (1, 3, 2)]

    @pl.when(keeper)
    def _():
        d_local.wait()
        ref = od.at[me.x, rows4b]
        remote(rd, ref, sd.at[0], rdn.at[0], across).wait_recv()
        for k, t in ys:
            remote(od.at[me.x, rows8], od.at[me.x, rows8], sd.at[k], rdn.at[k], me.at(y=t)).start()

    for n in range(8):
        swapped(n)
    keep_q = pltpu.make_async_copy(oq, oq_o, ls.at[12])
    keep_q.start()

    c, s = cos[...], sin[...]
    n1v = n1[...]
    for h in (12, 14, 0, 2, 4, 6, 8, 10):
        pair = slice(h * HS, (h + 2) * HS)
        j = mm(n1v, oq[:, :, :, :, :, pair].reshape(D, 2 * HS)) + ub[:, pair]
        for i in range(2):
            v = j[:, i * HS : (i + 1) * HS]
            if h + i < HEADS + KV_HEADS:
                v = turn(v, c, s)
            v = v.astype(BF)
            if h + i < HEADS:
                q[:, (h + i) * HS : (h + i + 1) * HS] = v
            else:
                at = slice((h + i - HEADS) * HS, (h + i - HEADS + 1) * HS)
                kv_own[0, :, at] = v[:BLK]
                kv_own[1, :, at] = v[BLK:]
        if h == 14:
            def send(k, carry):
                t = lax.rem(m + k, N_CTX)
                for half in range(2):
                    block = m if half == 0 else NBLK - 1 - m

                    @pl.when(reads(t, block))
                    def _():
                        src, dst = kv_own.at[half], kv.at[16 + block]
                        remote(src, dst, sk.at[half, k], rk.at[block], (me.dp, t)).start()

                return carry

            lax.fori_loop(1, N_CTX, send, 0)
            kv[16 + m] = kv_own[0]
            kv[16 + NBLK - 1 - m] = kv_own[1]

    gb2.first()
    wa.last()
    wb = Ring(me, "z", oz(me.z, None), oz, ss.at[9], rs.at[9])
    wb.first()
    swap(oz, me.z)
    ez = ZGather(me, eext, oe, *ez_sems, BLK)
    ez.first()
    def dx(j, h):
        return od.at[j] if h is None else od.at[j, pl.ds(8 * h, 8)]

    def arrived(block):
        src = jnp.where(block < N_CTX, block, NBLK - 1 - block)
        remote(kv_own.at[0], kv.at[16 + block], sk.at[0, 0], rk.at[block], (me.dp, src)).wait_recv()

    def near0(j, carry):
        block = m - (NWB - 1) + j

        @pl.when(block >= 0)
        def _():
            arrived(block)

        return carry

    def near1(j, carry):
        block = NBLK - 1 - m - (NWB - 1) + j

        @pl.when(block > m)
        def _():
            arrived(block)

        return carry

    wins = []
    keep_p = []
    for h in range(2):
        lax.fori_loop(0, NWB - 1, near0 if h == 0 else near1, 0)
        win = kv.at[pl.ds(m if h == 0 else NBLK - 1 - m, NWB)]
        start(pltpu.make_async_copy(win, win_o.at[h], ls.at[16 + h]), wins)
        base = (m if h == 0 else NBLK - 1 - m) * BLK
        kpos = base - WIN + iota((BLK, KEYS), 1)
        qpos = base + iota((BLK, KEYS), 0)
        pos = base + iota((BLK, 1), 0)
        begin, end = jnp.zeros((BLK, 1), jnp.int32), 0
        for i in range(8):
            end = end + docs[0, i]
            begin = jnp.where(end <= pos, end, begin)
        low = jnp.maximum(begin, pos - span[0] + 1)
        keep = (kpos <= qpos) & (kpos >= low)
        for a in range(KV_HEADS):
            qs = stack_heads(q, h, a)
            k = win[:, :, a * HS : (a + 1) * HS].reshape(KEYS, HS)
            v = win[:, :, KW + a * HS : KW + (a + 1) * HS].reshape(KEYS, HS)
            sco = nt(qs, k) * SCALE
            sco = jnp.where(keep[None], sco.reshape(GROUP, BLK, KEYS), -1e30)
            e = jnp.exp(sco - jnp.max(sco, -1, keepdims=True))
            pr = (e / jnp.sum(e, -1, keepdims=True)).astype(BF).reshape(GROUP * BLK, KEYS)
            p[2 * h + a] = pr
            o = mm(pr, v).astype(BF)
            for g in range(GROUP):
                o_o[h * BLK : (h + 1) * BLK, (a * GROUP + g) * HS : (a * GROUP + g + 1) * HS] = o[
                    g * BLK : (g + 1) * BLK
                ]
        if h == 0:
            for k, t in ys:
                f = me.step("y", 4 - k)

                @pl.when(lax.div(f, 2) == me.zhi)
                def _():
                    ref = od.at[me.x, pl.ds(lax.rem(f, 2) * 8, 8)]
                    remote(ref, ref, sd.at[k], rdn.at[k], me.at(y=f)).wait_recv()

            da = Ring(me, "x", od.at[me.x], dx, ss.at[10], rs.at[10])
            da.first()
            wb.second()
            swap(oz, wb.l)
            swap(oz, wb.r)
            ga2.second()

    start(pltpu.make_async_copy(p, p_o, ls.at[18]), keep_p)
    ez.second()
    wb.last()
    swap(oz, wb.o)
    for n in range(8, 12):
        swapped(n)
    keep_o = pltpu.make_async_copy(oo, oo_o, ls.at[13])
    keep_o.start()

    ob = o_o[...]
    u3 = nt(ob, a3[...]).astype(BF)
    hid = x[...].astype(F32) + mm(ob, oo[...].reshape(D, D)) + mm(u3, bo[...])
    hid_o[...] = hid
    nv = (hid * rms(hid) * gain[...].astype(F32)).astype(BF)
    n2[:, :D] = nv
    n2[:, D:] = nt(nv, a45[...]).astype(BF)
    nz = ZGather(me, n2, xg, *nz_sems, BLK)
    nz.first()
    keep_all((q, q_h), (o_o, o_h), (hid_o, hid_h), (n2, n2_h))
    start(pltpu.make_async_copy(n2, xg.at[me.zlo, me.core, me.zhi], ls.at[19]), side)
    gb2.second()
    nz.second()
    da.second()
    off = FV * me.slice - 128 * window_tile(me.slice)

    def pack(r, strips, fresh):
        base = 256 * r - off
        i0 = jnp.minimum(lax.div(jnp.maximum(base, 0), 70), 11)
        if fresh:
            rw, cl = iota((256, 400), 0) + base, iota((256, 400), 1)
            i, k = i0 + lax.div(cl, 80), lax.rem(cl, 80)
            pick70[r] = jnp.where((k < 70) & (i * 70 + k == rw), 1.0, 0.0).astype(BF)
        for j in strips:
            src = od[j, pl.ds(i0, 5)].reshape(400, 384)
            at = pl.ds(pl.multiple_of(384 * j, 128), 384)
            down[256 * r : 256 * (r + 1), at] = mm(pick70[r], src).astype(BF)

    for r in range(5):
        pack(r, (da.i, da.l, da.r), True)
    nz.last()
    ez.last()
    da.last()
    for r in range(5):
        pack(r, (da.o,), False)
    keep_d = pltpu.make_async_copy(down, od_o, ls.at[20])
    keep_d.start()
    ga2.last()
    gb2.last()

    for r in (qa, qb, qa2, qb2, wa, wb, ga, gb, ga2, gb2, da):
        r.sent()
    for c in first + zc:
        c.wait_send()

    @pl.when(jnp.logical_not(keeper))
    def _():
        d_cross.wait_send()

    @pl.when(keeper)
    def _():
        for k, t in ys:
            remote(od.at[me.x, rows8], od.at[me.x, rows8], sd.at[k], rdn.at[k], me.at(y=t)).wait_send()

    def sent(k, carry):
        t = lax.rem(m + k, N_CTX)
        for half in range(2):
            block = m if half == 0 else NBLK - 1 - m

            @pl.when(reads(t, block))
            def _():
                src, dst = kv_own.at[half], kv.at[16 + block]
                remote(src, dst, sk.at[half, k], rk.at[block], (me.dp, t)).wait_send()

        return carry

    lax.fori_loop(1, N_CTX, sent, 0)
    for n, (dz, dc) in enumerate(ZK):
        z, core = me.step("z", 4 - dz if dz else 0), lax.rem(me.core + dc, 2)
        ref = oi.at[2 * lax.rem(z, 2) + core, lax.div(z, 2)]
        remote(ref, ref, si.at[n], ri.at[n], me.at(z=z, core=core)).wait_recv()
    ez.finish()
    nz.finish()
    for c in side + wins + keep_p + kept + [keep_q, keep_o, keep_d]:
        c.wait()


def front(*args):
    outs = (
        sds((2, 2, 4, 2, 48, 2048), BF),
        sds((2, 2, 4, 2, 48, D), BF),
        sds((4, 2, 2, 4, 2, 48, 640), BF),
        sds((FW, D), BF),
        sds((2, 2, 2, ROWS, DX), BF),
        sds((4, 2, 8, 128), jnp.int32),
        sds((2, NWB, BLK, 2 * KW), BF),
        sds((4, GROUP * BLK, KEYS), BF),
        sds((2, 2, 2, ROWS, DX), BF),
        sds((ROWS, D), BF),
        sds((ROWS, D), BF),
        sds((ROWS, D), F32),
        sds((ROWS, DX), BF),
        sds((ROWS, D), BF),
        sds((ROWS, D), BF),
        sds((ROWS, DX), BF),
        sds((EXT, D), BF),
        sds((EXT, D), BF),
        sds((R, D), BF),
        sds((R, D), BF),
        sds((3, R, D), BF),
        sds((R, 2048), BF),
    )
    four = (DMA((4,)),) * 4
    scratch = [pltpu.VMEM(v.shape, v.dtype) for v in outs[9:]] + [
        DMA((13,)),
        pltpu.VMEM((ROWS, 2048), F32),
        pltpu.VMEM((8, 128), jnp.int32),
        pltpu.VMEM((2, 16, FF), BF),
        pltpu.VMEM((ADAPT, 6, R, D), BF),
        pltpu.VMEM((ADAPT, R, 2048), BF),
        pltpu.VMEM((ADAPT, 2, R, D), BF),
        pltpu.VMEM((4, 16, 2048), BF),
        pltpu.VMEM((4, 16, D), BF),
        pltpu.VMEM((4, 8, 16, 640), BF),
        pltpu.VMEM((80, D), BF),
        pltpu.VMEM((4, 80, 384), BF),
        pltpu.VMEM((48, 2048), BF),
        pltpu.VMEM((48, D), BF),
        pltpu.VMEM((8, 48, 640), BF),
        pltpu.VMEM((2, 2, 4, 2, 48, 2048), BF),
        pltpu.VMEM((2, 2, 4, 2, 48, D), BF),
        pltpu.VMEM((4, 16, 80, 384), BF),
        pltpu.VMEM((2, BLK, 2 * KW), BF),
        pltpu.VMEM((16 + NBLK, BLK, 2 * KW), BF),
        pltpu.VMEM((4, GROUP * BLK, KEYS), BF),
        pltpu.VMEM((FW, D), BF),
        pltpu.VMEM((5, 256, 400), BF),
        DMA((11, 4)),
        DMA((11, 4)),
        DMA((24,)),
        DMA((3, 11)),
        DMA((3, 11)),
        DMA((7,)),
        DMA((7,)),
        DMA((12,)),
        DMA((12,)),
        DMA((4,)),
        DMA((4,)),
        DMA((2, N_CTX)),
        DMA((NBLK,)),
        four,
        DMA((7,)),
        DMA((7,)),
        four,
    ]
    return pl.pallas_call(
        front_kernel,
        out_shape=outs,
        in_specs=[SM] * 3 + [VM] * 6 + [ANY] * 3 + [VM] * 5,
        out_specs=[ANY] * 22,
        scratch_shapes=scratch,
        compiler_params=pltpu.CompilerParams(collective_id=1, has_side_effects=True, vmem_limit_bytes=VMEM_LIMIT),
    )(*args)


class Fan:
    def __init__(self, me, axis, view, send, recv):
        self.me, self.axis, self.view, self.send, self.recv = me, axis, view, send, recv
        self.i = getattr(me, axis)

    def copy(self, k, j, to):
        ref = self.view(j)
        return remote(ref, ref, self.send.at[k - 1], self.recv.at[k - 1], self.me.at(**{self.axis: to}))

    def first(self):
        self.out = []
        for k in (1, 3, 2):
            c = self.copy(k, self.i, self.me.step(self.axis, k))
            c.start()
            self.out.append(c)

    def last(self):
        for k in (1, 3, 2):
            f = self.me.step(self.axis, 4 - k)
            self.copy(k, f, f).wait_recv()

    def sent(self):
        for c in self.out:
            c.wait_send()


def norm_back(z, gain, grad):
    r = rms(z)
    t = gain * grad
    return r * t - z * (r * r * r) * jnp.mean(t * z, -1, keepdims=True)


def rear_kernel(
    xg, oe, og, wd_i, ad_all, b_all, e_i, hid_i, n2_i, q_i, o_i, p_i, win_i, wo_i, wq_i, x_i, n1_i,
    a012_i, a3_i, a45_i, bqkv_i, bo_i, bd_i, cos_i, sin_i, oi, gain1, gain2,
    out_h, gt_h, early, late,
    a012, a3, a45, bqkv, bo, bd, cos, sin, out_o, gt_o, ld2,
    wgu, wdo, ad_in, b_in, ad, acc, xb, sib_out, sib_got, red, got2, ft,
    e, hid, n2, q, o, p, win, x, n1,
    gn2, ysum, gh, go, gq, gwin, got, gkv, gj, l1, l2, gf, gl1, gl2, red1, red2,
    wl, xl, ld, sb_s, sb_r, rz_s, rz_r, f_s, f_r, a_s, a_r, b_s, b_r, kv_s, kv_r, ls,
    ring_s, ring_r, fan_s, fan_r, core_s, core_r,
):
    me = Place()
    sib = me.sibling()
    m = me.ctx
    tile = window_tile(me.slice)
    off = FV * me.slice - 128 * tile
    bar = pltpu.get_barrier_semaphore()

    def hello(t, carry):
        @pl.when(t != m)
        def _():
            pl.semaphore_signal(bar, inc=1, device_id=(me.dp, t), device_id_type=MESH)

        return carry

    def load(src, dst, sem):
        c = pltpu.make_async_copy(src, dst, sem)
        c.start()
        return c

    cols = pl.ds(pl.multiple_of(tile * 128, 128), FW)
    wloads = [
        load(ad_all.at[:, :, cols], ad_in, wl.at[0]),
        load(b_all.at[:, :, :, cols], b_in, wl.at[1]),
    ]
    for k in range(4):
        wloads.append(load(og.at[k], wgu.at[pl.ds(0, D), pl.ds(640 * k, 640)], wl.at[2 + k]))
    wloads.append(load(wd_i, wdo.at[pl.ds(0, FW), pl.ds(0, D)], wl.at[6]))
    steps = [(1 - me.zlo, 1 - me.core), (1 - me.zlo, me.core), (me.zlo, 1 - me.core), (me.zlo, me.core)]

    def rows_in(n):
        zl, core = steps[n]
        return [load(src.at[zl, core], xb.at[n % 2, k], xl.at[n % 2, k]) for k, src in enumerate((xg, oe))]

    coming = [rows_in(0), rows_in(1)]
    lax.fori_loop(0, N_CTX, hello, 0)
    others = [me.at(z=me.step("z", 1)), me.at(z=me.step("z", 3)), sib]
    for d in others:
        pl.semaphore_signal(bar, inc=1, device_id=d, device_id_type=MESH)
    loads = [
        load(src, dst, ld.at[n])
        for n, (src, dst) in enumerate(
            (
                (e_i, e), (hid_i, hid), (n2_i, n2), (o_i, o), (q_i, q),
                (win_i, win), (p_i, p), (n1_i, n1), (x_i, x),
            )
        )
    ]
    small = [
        load(src, dst, ld2.at[n])
        for n, (src, dst) in enumerate(
            (
                (a45_i, a45), (bo_i, bo), (a3_i, a3), (a012_i, a012), (bqkv_i, bqkv), (bd_i, bd), (cos_i, cos), (sin_i, sin),
            )
        )
    ]
    for c in wloads[:2]:
        c.wait()
    row, col = iota((64, 128), 0), iota((64, 128), 1)
    choose = jnp.zeros((64, 128), F32)
    for k in range(4):
        hit = (lax.div(row, R) == k) & (lax.rem(row, R) == lax.rem(col, R)) & (lax.div(col, R) == oi[k, 0, :1, :1])
        choose += jnp.where(hit, 1.0, 0.0)
    choose = choose.astype(BF)
    fcol = iota((64, FW), 1)
    valid = (fcol >= off) & (fcol < off + FV)
    ad[:64] = jnp.where(valid, mm(choose, ad_in[...].reshape(128, FW)), 0.0).astype(BF)
    ad[64:] = jnp.zeros((64, FW), BF)
    eye = jnp.where(iota((EXT, EXT), 0) == iota((EXT, EXT), 1), 1.0, 0.0).astype(BF)
    wdo[:FW, D:] = tn(ad[...], eye).astype(BF)
    none = jnp.zeros((64, FW), BF)
    wgu[D : D + 64, :FW] = mm(choose, b_in[:, 0].reshape(128, FW)).astype(BF)
    wgu[D + 64 :, :FW] = none
    wgu[D : D + 64, FW:] = none
    wgu[D + 64 :, FW:] = mm(choose, b_in[:, 1].reshape(128, FW)).astype(BF)
    acc[...] = jnp.zeros_like(acc)
    for c in wloads[2:6]:
        c.wait()
    sib_copies, z_copies = [], []

    def z_push(j, k, slot, z):
        c = remote(red.at[j, k], got2.at[slot, k], rz_s.at[j, k], rz_r.at[slot, k], me.at(z=z))
        c.start()
        z_copies.append(c)

    for n in range(4):
        for c in coming[n]:
            c.wait()
        xv = xb[n % 2, 0].reshape(2 * ROWS, DX)
        ev = xb[n % 2, 1].reshape(2 * ROWS, DX)
        both = mm(xv, wgu[...])
        gate, up = both[:, :FW], both[:, FW:]
        if n == 0:
            wloads[6].wait()
        gm = nt(ev, wdo[:FW])
        sig = 1.0 / (1.0 + jnp.exp(-gate))
        sl = gate * sig
        act = (sl * up).astype(BF)
        gg = (gm * up * (sig * (1.0 + gate * (1.0 - sig)))).astype(BF)
        gu = (gm * sl).astype(BF)
        grads = jnp.concatenate([gg, gu], 1)
        acc[0] += tn(ev[:, D:], act)[:64]
        by_u = tn(xv[:, D:], grads)
        acc[1] += by_u[:64, :FW]
        acc[2] += by_u[64:, FW:]
        if n < 2:
            coming.append(rows_in(n + 2))
        if n == 0:
            pl.semaphore_wait(bar, N_CTX - 1 + len(others))
        for k in (1, 0):
            wide = nt(grads, wgu[...]) if k == 1 else mm(act, wdo[:FW])
            total = gn2 if k == 1 else ysum
            if n % 2 == 0:
                for zh in range(2):
                    rows = slice(zh * ROWS, (zh + 1) * ROWS)
                    sib_out[n // 2, k, zh] = wide[rows].astype(BF)
                c = remote(sib_out.at[n // 2, k], sib_got.at[n // 2, k], sb_s.at[n // 2, k], sb_r.at[n // 2, k], sib)
                c.start()
                sib_copies.append(c)
            else:
                theirs = sib_got.at[n // 2, k]
                remote(theirs, theirs, sb_s.at[n // 2, k], sb_r.at[n // 2, k], sib).wait_recv()
                if n == 1:
                    for zh in range(2):
                        rows = slice(zh * ROWS, (zh + 1) * ROWS)
                        red[zh, k] = (wide[rows] + theirs[zh].astype(F32)).astype(BF)
                        z_push(zh, k, me.zhi, 2 * zh + 1 - me.zlo)
                else:
                    mine = me.zhi == 1
                    far = jnp.where(mine, wide[:ROWS], wide[ROWS:])
                    near = jnp.where(mine, wide[ROWS:], wide[:ROWS])
                    red[2, k] = (far + theirs[1 - me.zhi].astype(F32)).astype(BF)
                    z_push(2, k, 2, me.step("z", 2))
                    total[...] = near + theirs[me.zhi].astype(F32)
    for k in range(3):
        v = jnp.where(valid, acc[k], 0.0).astype(BF)
        for i in range(4):
            for t in range(10):
                ft[i * 30 + k * 10 + t] = v[R * i : R * (i + 1), 128 * t : 128 * (t + 1)]
    for t in range(120, 128):
        ft[t] = jnp.zeros((R, 128), BF)
    xy = me.y * 4 + me.x

    def plane(k):
        return me.at(x=lax.rem(k, 4), y=lax.div(k, 4))

    def f_copy(t):
        return remote(ft.at[pl.ds(8 * t, 8)], gf.at[xy], f_s.at[t], f_r.at[xy], plane(t))

    def f_send(k, carry):
        f_copy(lax.rem(xy + k, 16)).start()
        return carry

    lax.fori_loop(1, 16, f_send, 0)
    gf[xy] = ft[pl.ds(8 * xy, 8)]
    wo_load = load(wo_i, wdo.at[:, pl.ds(0, D)], ld.at[9])
    wq_load = load(wq_i, wgu.at[pl.ds(0, D), pl.ds(0, 2048)], ld.at[10])

    def z_take(k, total):
        for slot in range(3):
            ref = got2.at[slot, k]
            remote(ref, ref, rz_s.at[slot, k], rz_r.at[slot, k], sib).wait_recv()
            total[...] += ref[...].astype(F32)

    z_take(1, gn2)
    for c in loads[:4] + small + [wo_load]:
        c.wait()

    def put(tiles, at, v):
        for t in range(v.shape[1] // 128):
            tiles[at + t] = v[:, 128 * t : 128 * (t + 1)].astype(BF)

    gue = gn2[:, D:].astype(BF)
    gn = gn2[:, :D] + mm(gue, a45[...])
    ghv = e[:, :D].astype(F32) + norm_back(hid[...], gain2[...].astype(F32), gn)
    gh[...] = ghv
    ghb = ghv.astype(BF)
    ob = o[...]
    gu3 = nt(ghb, bo[...]).astype(BF)
    go[...] = (nt(ghb, wdo[:, :D]) + mm(gu3, a3[...])).astype(BF)
    u3 = nt(ob, a3[...]).astype(BF)
    s = me.dp

    put(l1, 0, tn(gu3, ob))
    g45b = tn(gue, n2[:, :D]).astype(BF)
    pick_own = jnp.where((iota((R, EXT), 1) == iota((R, EXT), 0) + s * R), 1.0, 0.0).astype(BF)
    pick_up = jnp.where((iota((R, EXT), 1) == iota((R, EXT), 0) + s * R + 64), 1.0, 0.0).astype(BF)
    put(l1, 12, mm(pick_own, g45b))
    put(l1, 24, mm(pick_up, g45b))
    put(l1, 36, tn(u3, ghb))
    for t in range(48, 64):
        l1[t] = jnp.zeros((R, 128), BF)

    def l_copy(tiles, buf, ss, rs, t):
        return remote(tiles.at[pl.ds(2 * t, 2)], buf.at[m], ss.at[t], rs.at[m], (me.dp, t))

    def l_send(tiles, buf, ss, rs):
        def one(k, carry):
            l_copy(tiles, buf, ss, rs, lax.rem(m + k, N_CTX)).start()
            return carry

        lax.fori_loop(1, N_CTX, one, 0)
        buf[m] = tiles[pl.ds(2 * m, 2)]

    def l_sum(buf, ss, rs):
        def one(k, carry):
            t = lax.rem(m + k, N_CTX)
            remote(buf.at[t], buf.at[t], ss.at[t], rs.at[t], (me.dp, t)).wait_recv()
            return carry + buf[t].astype(F32)

        return lax.fori_loop(1, N_CTX, one, buf[m].astype(F32)).astype(BF)

    def l_sent(tiles, buf, ss, rs):
        def one(k, carry):
            l_copy(tiles, buf, ss, rs, lax.rem(m + k, N_CTX)).wait_send()
            return carry

        lax.fori_loop(1, N_CTX, one, 0)

    l_send(l1, gl1, a_s, a_r)

    def covers(t, w, owner, h):
        block = owner if h == 0 else NBLK - 1 - owner
        j = block - ((t if w == 0 else NBLK - 1 - t) - (NWB - 1))
        ok = (j >= 0) & (j < NWB)
        return j, ok if w == 0 else ok & (block > t)

    def kv_copy(w, h, t, j):
        return remote(gwin.at[w, j], got.at[h, w, j], kv_s.at[h, w, t], kv_r.at[h, w, j], (me.dp, t))

    for c in loads[4:7]:
        c.wait()
    for w in (1, 0):
        for a in range(KV_HEADS):
            qs, gv, ov = stack_heads(q, w, a), stack_heads(go, w, a), stack_heads(o, w, a)
            k = win[w, :, :, a * HS : (a + 1) * HS].reshape(KEYS, HS)
            v = win[w, :, :, KW + a * HS : KW + (a + 1) * HS].reshape(KEYS, HS)
            pr = p[2 * w + a]
            delta = jnp.sum(gv.astype(F32) * ov.astype(F32), -1, keepdims=True)
            ds = (pr.astype(F32) * (nt(gv, v) - delta)).astype(BF)
            gqv = mm(ds, k) * SCALE
            for g in range(GROUP):
                cols = slice((a * GROUP + g) * HS, (a * GROUP + g + 1) * HS)
                gq[w * BLK : (w + 1) * BLK, cols] = gqv[g * BLK : (g + 1) * BLK]
            gwin[w, :, :, a * HS : (a + 1) * HS] = (tn(ds, qs) * SCALE).astype(BF).reshape(NWB, BLK, HS)
            gwin[w, :, :, KW + a * HS : KW + (a + 1) * HS] = tn(pr, gv).astype(BF).reshape(NWB, BLK, HS)

        if w == 0:
            def both_windows(j, carry):
                j1 = j + 2 * m - (NBLK - 1)

                @pl.when(j1 >= 0)
                def _():
                    gwin[0, j] = (gwin[0, j].astype(F32) + gwin[1, j1].astype(F32)).astype(BF)

                return carry

            lax.fori_loop(0, NWB, both_windows, 0)

        def kv_send(k, carry):
            t = lax.rem(m + k, N_CTX)
            for h in range(2):
                j, ok = covers(m, w, t, h)

                @pl.when(ok)
                def _():
                    kv_copy(w, h, t, j).start()

            return carry

        lax.fori_loop(1, N_CTX, kv_send, 0)
        for h in range(2):
            j, ok = covers(m, w, m, h)

            @pl.when(ok)
            def _():
                c = pltpu.make_async_copy(gwin.at[w, j], got.at[h, w, j], ls.at[2 * w + h])
                c.start()
                c.wait()


    def f_take(k, carry):
        t = lax.rem(xy + k, 16)
        remote(gf.at[t], gf.at[t], f_s.at[t], f_r.at[t], plane(t)).wait_recv()
        return carry + gf[t].astype(F32)

    red1[:8] = lax.fori_loop(1, 16, f_take, gf[xy].astype(F32)).astype(BF)
    red1[8:] = l_sum(gl1, a_s, a_r)

    def vz(j, h):
        ref = early.at[me.y, me.x, lax.rem(j, 2), me.core, lax.div(j, 2)]
        return ref if h is None else ref.at[pl.ds(5 * h, 5)]

    own_e = pltpu.make_async_copy(red1, vz(me.z, None), ls.at[5])
    own_e.start()
    rz = Ring(me, "z", red1, vz, ring_s.at[0], ring_r.at[0])
    rz.first()
    ta, tb = pl.ds(0, 5), pl.ds(5, 5)

    def x0(j, h):
        return early.at[me.y, j, :, me.core, :, ta] if h is None else early.at[me.y, j, h, me.core, :, ta]

    def y0(j, h):
        return early.at[j, :, :, me.core, :, ta] if h is None else early.at[j, pl.ds(2 * h, 2), :, me.core, :, ta]

    def y1(j, h):
        return early.at[j, me.x, :, me.core, :, tb] if h is None else early.at[j, me.x, h, me.core, :, tb]

    def x1(j, h):
        return early.at[:, j, :, me.core, :, tb] if h is None else early.at[pl.ds(2 * h, 2), j, :, me.core, :, tb]

    gkv[...] = jnp.zeros_like(gkv)

    def take(k, carry):
        t = lax.rem(m + N_CTX - k, N_CTX)
        for w in range(2):
            for h in range(2):
                j, ok = covers(t, w, m, h)

                @pl.when(ok & (k > 0))
                def _():
                    ref = got.at[h, w, j]
                    remote(ref, ref, kv_s.at[h, w, t], kv_r.at[h, w, j], (me.dp, t)).wait_recv()

                @pl.when(ok)
                def _():
                    gkv[h] += got[h, w, j].astype(F32)

        return carry

    lax.fori_loop(0, 20, take, 0)
    rz.second()
    rz.last()
    own_e.wait()
    ra = Ring(me, "x", x0(me.x, None), x0, ring_s.at[1], ring_r.at[1])
    rb = Ring(me, "y", y1(me.y, None), y1, ring_s.at[2], ring_r.at[2])
    ra.first()
    rb.first()

    lax.fori_loop(20, N_CTX, take, 0)

    for c in loads[7:] + [wq_load]:
        c.wait()
    c, sn = cos[...], sin[...]
    for h in range(HEADS):
        cols = slice(h * HS, (h + 1) * HS)
        gj[:, cols] = turn_back(gq[:, cols], c, sn).astype(BF)
    for a in range(KV_HEADS):
        v = jnp.concatenate([gkv[0, :, a * HS : (a + 1) * HS], gkv[1, :, a * HS : (a + 1) * HS]], 0)
        gj[:, QW + a * HS : QW + (a + 1) * HS] = turn_back(v, c, sn).astype(BF)
    gj[:, QW + KW :] = jnp.concatenate([gkv[0, :, KW:], gkv[1, :, KW:]], 0).astype(BF)
    n1b = n1[...]
    more = jnp.zeros((ROWS, D), F32)
    for i, (lo, hi) in enumerate(((0, QW), (QW, QW + KW), (QW + KW, QW + 2 * KW))):
        am = a012[i]
        u = nt(n1b, am).astype(BF)
        gjm = gj[:, lo:hi]
        gum = nt(gjm, bqkv[:, lo:hi]).astype(BF)
        more += mm(gum, am)
        put(l2, 36 + lo // 128, tn(u, gjm))
        put(l2, 12 * i, tn(gum, n1b))
    z_take(0, ysum)
    ud = ysum[:, D:].astype(BF)
    y = hid[...] + ysum[:, :D] + mm(ud, bd[...])
    for h in range(2):
        out_o[:, h, :] = y[h * BLK : (h + 1) * BLK].astype(BF)
    out_load = load(out_o, out_h, ld2.at[8])
    put(l2, 52, mm(pick_own, tn(ud, e[:, :D]).astype(BF)))
    l_send(l2, gl2, b_s, b_r)
    gn = nt(gj[...], wgu[:D, :2048]) + more
    gt = gh[...] + norm_back(x[...].astype(F32), gain1[...].astype(F32), gn)
    for h in range(2):
        gt_o[:, h, :] = gt[h * BLK : (h + 1) * BLK].astype(BF)
    gt_load = load(gt_o, gt_h, ld2.at[9])

    ra.second()
    rb.second()
    red2[...] = l_sum(gl2, b_s, b_r)

    def uz(j):
        return late.at[me.y, me.x, lax.rem(j, 2), me.core, lax.div(j, 2)]

    own_l = pltpu.make_async_copy(red2, uz(me.z), ls.at[6])
    own_l.start()
    own_l.wait()
    def f_sent(k, carry):
        f_copy(lax.rem(xy + k, 16)).wait_send()
        return carry

    def kv_sent(k, carry):
        t = lax.rem(m + k, N_CTX)
        for w in range(2):
            for h in range(2):
                j, ok = covers(m, w, t, h)

                @pl.when(ok)
                def _():
                    kv_copy(w, h, t, j).wait_send()

        return carry

    fz = Fan(me, "z", uz, fan_s.at[0], fan_r.at[0])
    fz.first()
    ra.last()
    rb.last()
    l_sent(l1, gl1, a_s, a_r)
    lax.fori_loop(1, 16, f_sent, 0)
    fz.last()
    t0, t1 = pl.ds(0, 1), pl.ds(1, 1)
    fx = Fan(me, "x", lambda j: late.at[me.y, j, :, me.core, :, t0], fan_s.at[1], fan_r.at[1])
    fy = Fan(me, "y", lambda j: late.at[j, me.x, :, me.core, :, t1], fan_s.at[2], fan_r.at[2])
    fx.first()
    fy.first()
    rc = Ring(me, "y", y0(me.y, None), y0, ring_s.at[3], ring_r.at[3])
    rd = Ring(me, "x", x1(me.x, None), x1, ring_s.at[4], ring_r.at[4])
    rc.first()
    rd.first()
    swaps = []

    def swap(view, j):
        n = len(swaps)
        c = remote(view(j, me.core), view(j, me.core), core_s.at[n], core_r.at[n], sib)
        c.start()
        swaps.append((c, view, j))

    def ey(j, core):
        return early.at[j, :, :, core, :, ta]

    def ex(j, core):
        return early.at[:, j, :, core, :, tb]

    def late_all(j, core):
        return late.at[j, :, :, core]

    swap(ey, me.y)
    swap(ex, me.x)
    lax.fori_loop(1, N_CTX, kv_sent, 0)
    fx.last()
    fy.last()
    fy2 = Fan(me, "y", lambda j: late.at[j, :, :, me.core, :, t0], fan_s.at[3], fan_r.at[3])
    fx2 = Fan(me, "x", lambda j: late.at[:, j, :, me.core, :, t1], fan_s.at[4], fan_r.at[4])
    fy2.first()
    fx2.first()
    rc.second()
    rd.second()
    swap(ey, rc.l)
    swap(ex, rd.l)
    swap(ey, rc.r)
    swap(ex, rd.r)
    l_sent(l2, gl2, b_s, b_r)
    rc.last()
    rd.last()
    swap(ey, rc.o)
    swap(ex, rd.o)
    fy2.last()
    fx2.last()
    for k in range(4):
        swap(late_all, k)

    for c in sib_copies + z_copies:
        c.wait_send()
    out_load.wait()
    gt_load.wait()
    for r in (rz, ra, rb, rc, rd, fz, fx, fy, fx2, fy2):
        r.sent()


    for n, (c, view, j) in enumerate(swaps):
        c.wait_send()
        ref = view(j, 1 - me.core)
        remote(ref, ref, core_s.at[n], core_r.at[n], sib).wait_recv()


def rear(xg, oe, og, wd, ad_all, b_all, e, hid, n2, q, o, p, win, wo, wq, x, n1, *small):
    outs = (
        sds((BLK, 2, D), BF),
        sds((BLK, 2, D), BF),
        sds((4, 4, 2, 2, 2, 10, R, 128), BF),
        sds((4, 4, 2, 2, 2, 2, R, 128), BF),
    )
    block = (ROWS, DX)
    scratch = [pltpu.VMEM(v.shape, v.dtype) for v in small[:8]] + [
        pltpu.VMEM((BLK, 2, D), BF),
        pltpu.VMEM((BLK, 2, D), BF),
        DMA((10,)),
        pltpu.VMEM((DX, 2 * FW), BF),
        pltpu.VMEM((D, DX), BF),
        pltpu.VMEM((ADAPT, R, FW), BF),
        pltpu.VMEM((ADAPT, 2, R, FW), BF),
        pltpu.VMEM((EXT, FW), BF),
        pltpu.VMEM((3, 64, FW), F32),
        pltpu.VMEM((2, 2, 2) + block, BF),
        pltpu.VMEM((2, 2, 2) + block, BF),
        pltpu.VMEM((2, 2, 2) + block, BF),
        pltpu.VMEM((3, 2) + block, BF),
        pltpu.VMEM((3, 2) + block, BF),
        pltpu.VMEM((128, R, 128), BF),
    ]
    scratch += [pltpu.VMEM(v.shape, v.dtype) for v in (e, hid, n2, q, o, p, win, x, n1)]
    scratch += [
        pltpu.VMEM(block, F32),
        pltpu.VMEM(block, F32),
        pltpu.VMEM((ROWS, D), F32),
        pltpu.VMEM((ROWS, D), BF),
        pltpu.VMEM((ROWS, D), F32),
        pltpu.VMEM((2, NWB, BLK, 2 * KW), BF),
        pltpu.VMEM((2, 2, NWB, BLK, 2 * KW), BF),
        pltpu.VMEM((2, BLK, 2 * KW), F32),
        pltpu.VMEM((ROWS, 2048), BF),
        pltpu.VMEM((64, R, 128), BF),
        pltpu.VMEM((64, R, 128), BF),
        pltpu.VMEM((16, 8, R, 128), BF),
        pltpu.VMEM((N_CTX, 2, R, 128), BF),
        pltpu.VMEM((N_CTX, 2, R, 128), BF),
        pltpu.VMEM((10, R, 128), BF),
        pltpu.VMEM((2, R, 128), BF),
        DMA((7,)),
        DMA((2, 2)),
        DMA((11,)),
        DMA((2, 2)),
        DMA((2, 2)),
        DMA((3, 2)),
        DMA((3, 2)),
        DMA((16,)),
        DMA((16,)),
        DMA((N_CTX,)),
        DMA((N_CTX,)),
        DMA((N_CTX,)),
        DMA((N_CTX,)),
        DMA((2, 2, N_CTX)),
        DMA((2, 2, NWB)),
        DMA((7,)),
        DMA((5, 4)),
        DMA((5, 4)),
        DMA((5, 3)),
        DMA((5, 3)),
        DMA((12,)),
        DMA((12,)),
    ]
    return pl.pallas_call(
        rear_kernel,
        out_shape=outs,
        in_specs=[ANY] * 25 + [VM] * 3,
        out_specs=[ANY] * 4,
        scratch_shapes=scratch,
        compiler_params=pltpu.CompilerParams(collective_id=2, has_side_effects=True, vmem_limit_bytes=VMEM_LIMIT),
    )(xg, oe, og, wd, ad_all, b_all, e, hid, n2, q, o, p, win, wo, wq, x, n1, *small)


def spread_kernel(oi, early, late, ain_o, aff_o, bqkv_o, bres_o, bff_o):
    e = pl.program_id(0)
    for ref in (ain_o, aff_o, bqkv_o, bres_o, bff_o):
        ref[...] = jnp.zeros_like(ref)

    def local_tile(ref, at, s, n):
        k, j = n // 2, n % 2
        return ref[k // 8, k % 4, s // 2, s % 2, (k // 4) % 2, at + j].astype(F32)

    def ff_tile(piece, n):
        k, j = n // 8, n % 8
        return early[k // 4, k % 4, piece // 4, (piece // 2) % 2, piece % 2, j].astype(F32)

    for s in range(4):

        @pl.when(oi[s, 0, 0, 0] == e)
        def _():
            for c in range(12):
                cols = slice(128 * c, 128 * (c + 1))
                for m in range(3):
                    ain_o[0, m, :, cols] += local_tile(late, 0, s, 12 * m + c)
                    ain_o[0, 3 + m, :, cols] += local_tile(early, 8, s, 12 * m + c)
                bres_o[0, 0, :, cols] += local_tile(early, 8, s, 36 + c)
                bres_o[0, 1, :, cols] += local_tile(late, 0, s, 52 + c)
            for c in range(16):
                bqkv_o[0, :, 128 * c : 128 * (c + 1)] += local_tile(late, 0, s, 36 + c)
            for piece in range(8):
                tile = 60 if piece == 7 else 35 * piece // 4
                for k in range(3):
                    for c in range(10):
                        cols = slice(128 * (tile + c), 128 * (tile + c + 1))
                        v = ff_tile(piece, s * 30 + k * 10 + c)
                        if k == 0:
                            aff_o[0, :, cols] += v
                        else:
                            bff_o[0, k - 1, :, cols] += v


def spread(oi, early, late):
    outs = (
        sds((ADAPT, 6, R, D), F32),
        sds((ADAPT, R, FF), F32),
        sds((ADAPT, R, 2048), F32),
        sds((ADAPT, 2, R, D), F32),
        sds((ADAPT, 2, R, FF), F32),
    )

    def one(shape):
        return pl.BlockSpec((1,) + shape[1:], lambda i: (i,) + (0,) * (len(shape) - 1))

    return pl.pallas_call(
        spread_kernel,
        out_shape=outs,
        grid=(ADAPT,),
        in_specs=[
            SM,
            pl.BlockSpec(early.shape, lambda i: (0,) * 8),
            pl.BlockSpec(late.shape, lambda i: (0,) * 8),
        ],
        out_specs=[one(o.shape) for o in outs],
        compiler_params=pltpu.CompilerParams(vmem_limit_bytes=VMEM_LIMIT),
    )(oi, early, late)


def local(
    tokens,
    cotangent,
    w_qkv,
    b_qkv,
    w_out,
    w_gu,
    w_down,
    gain_attn,
    gain_mlp,
    adapt_in,
    adapt_in_ff,
    adapt_out_qkv,
    adapt_out_res,
    adapt_out_ff,
    doc_lengths,
    adapter_index,
    window,
):
    member = lax.axis_index("ctx")
    starts = jnp.stack([member * BLK, (NBLK - 1 - member) * BLK])
    pos = (starts[:, None] + jnp.arange(BLK, dtype=jnp.int32)[None]).reshape(ROWS)
    freq = 1000000.0 ** (-(2.0 * jnp.arange(HS // 2, dtype=F32)) / HS)
    ang = pos.astype(F32)[:, None] * freq[None]
    c, sn = jnp.cos(ang), jnp.sin(ang)
    cos = jnp.concatenate([c, c], -1)
    sin = jnp.concatenate([-sn, sn], -1)

    (
        oq, oo, og, down, oe, oi, wins, p, xg, q, o, hid, n2,
        x, n1, eext, a45, bd, a3, bo, a012, bqkv,
    ) = front(
        adapter_index, doc_lengths, window, w_qkv, w_out, w_gu, w_down, tokens[0], cotangent[0],
        adapt_in, adapt_out_qkv, adapt_out_res, gain_attn, b_qkv, cos, sin, gain_mlp,
    )
    oq = oq.reshape(D, 2048)
    oo = oo.reshape(D, D)
    og = og.reshape(4, D, 640)
    out, gt, early, late = rear(
        xg, oe, og, down, adapt_in_ff, adapt_out_ff, eext, hid, n2, q, o, p, wins, oo, oq, x, n1,
        a012, a3, a45, bqkv, bo, bd, cos, sin, oi, gain_attn, gain_mlp,
    )
    return (out[None], gt[None]) + tuple(spread(oi, early, late))


def solution(mesh):
    return jax.shard_map(
        local,
        mesh=mesh,
        in_specs=(
            P("dp", "ctx", None, None),
            P("dp", "ctx", None, None),
            P(("dp", "ctx"), None),
            P(),
            P(("dp", "ctx"), None),
            P(("dp", "ctx"), None, None),
            P(("dp", "ctx"), None),
            P(),
            P(),
            P(),
            P(),
            P(),
            P(),
            P(),
            P("dp", None),
            P("dp"),
            P("dp"),
        ),
        out_specs=(P("dp", "ctx", None, None), P("dp", "ctx", None, None), P(), P(), P(), P(), P()),
        check_vma=False,
    )
```

```python
import functools

import jax
import jax.numpy as jnp
from jax import lax
from jax.experimental import pallas as pl
from jax.experimental.pallas import tpu as pltpu
from jax.sharding import PartitionSpec as P

D = 1536
HEADS = 12
KV_HEADS = 2
HS = 128
GROUP = HEADS // KV_HEADS
FF = 8960
R = 16
ADAPT = 8
BLK = 64
ROWS = 2 * BLK
N_CTX = 32
NBLK = 2 * N_CTX
WIN = 1024
NWB = WIN // BLK + 1
KEYS = NWB * BLK
EXT = 128
DX = D + EXT
FW = 1280
FV = FF // 8
QW = HEADS * HS
KW = KV_HEADS * HS
SCALE = HS**-0.5
EPS = 1e-6

MESH = pl.DeviceIdType.MESH
BF = jnp.bfloat16
F32 = jnp.float32
ANY = pl.BlockSpec(memory_space=pl.ANY)
VM = pl.BlockSpec(memory_space=pltpu.VMEM)
SM = pl.BlockSpec(memory_space=pltpu.SMEM)
DMA = pltpu.SemaphoreType.DMA
VMEM_LIMIT = 60 * 2**20


def sds(shape, dtype):
    return jax.ShapeDtypeStruct(shape, dtype)


def nt(a, b):
    return lax.dot_general(a, b, (((1,), (1,)), ((), ())), preferred_element_type=F32)


def tn(a, b):
    return lax.dot_general(a, b, (((0,), (0,)), ((), ())), preferred_element_type=F32)


def mm(a, b):
    return jnp.dot(a, b, preferred_element_type=F32)


def iota(shape, dim):
    return lax.broadcasted_iota(jnp.int32, shape, dim)


class Place:
    def __init__(self):
        dp, ctx = lax.axis_index("dp"), lax.axis_index("ctx")
        self.dp, self.ctx = dp, ctx
        self.zlo, self.core = lax.div(dp, 2), lax.rem(dp, 2)
        self.y, self.zhi, self.x = lax.div(ctx, 8), lax.rem(lax.div(ctx, 4), 2), lax.rem(ctx, 4)
        self.z = self.zhi * 2 + self.zlo
        self.slice = 2 * dp + self.zhi

    def at(self, x=None, y=None, z=None, core=None):
        x = self.x if x is None else x
        y = self.y if y is None else y
        z = self.z if z is None else z
        core = self.core if core is None else core
        return (lax.rem(z, 2) * 2 + core, y * 8 + lax.div(z, 2) * 4 + x)

    def step(self, axis, by):
        return lax.rem(getattr(self, axis) + by, 4)

    def ring(self, axis):
        return [self.at(**{axis: self.step(axis, k)}) for k in (1, 2, 3)]

    def sibling(self):
        return self.at(core=1 - self.core)


def window_tile(piece):
    return jnp.minimum(lax.div(35 * piece, 4), 60)


def remote(src, dst, send, recv, device):
    return pltpu.make_async_remote_copy(
        src_ref=src, dst_ref=dst, send_sem=send, recv_sem=recv, device_id=device, device_id_type=MESH
    )


def greet(peers):
    sem = pltpu.get_barrier_semaphore()
    for device in peers:
        pl.semaphore_signal(sem, inc=1, device_id=device, device_id_type=MESH)
    pl.semaphore_wait(sem, len(peers))


class Ring:
    def __init__(self, me, axis, own, view, send, recv):
        self.i = getattr(me, axis)
        self.r, self.o, self.l = (me.step(axis, k) for k in (1, 2, 3))
        self.right, self.left = me.at(**{axis: self.r}), me.at(**{axis: self.l})
        self.own, self.view, self.send, self.recv = own, view, send, recv

    def copy(self, k, src, dst, device):
        return remote(src, dst, self.send.at[k], self.recv.at[k], device)

    def first(self):
        place = self.view(self.i, None)
        self.out = [self.copy(0, self.own, place, self.right), self.copy(1, self.own, place, self.left)]
        for c in self.out:
            c.start()

    def second(self):
        v = self.view
        self.copy(0, v(self.l, None), v(self.l, None), self.right).wait_recv()
        c = self.copy(2, v(self.l, 0), v(self.l, 0), self.right)
        c.start()
        self.out.append(c)
        self.copy(1, v(self.r, None), v(self.r, None), self.left).wait_recv()
        c = self.copy(3, v(self.r, 1), v(self.r, 1), self.left)
        c.start()
        self.out.append(c)

    def last(self):
        v = self.view
        self.copy(2, v(self.o, 0), v(self.o, 0), self.right).wait_recv()
        self.copy(3, v(self.o, 1), v(self.o, 1), self.left).wait_recv()

    def sent(self):
        for c in self.out:
            c.wait_send()


class ZGather:
    def __init__(self, me, own, buf, send, recv, core_send, core_recv, half):
        self.me, self.own, self.buf = me, own, buf
        self.cs, self.cr = core_send, core_recv

        def view(j, h, core=me.core):
            ref = buf.at[lax.rem(j, 2), core, lax.div(j, 2)]
            return ref if h is None else ref.at[pl.ds(h * half, half)]

        self.view = view
        self.ring = Ring(me, "z", own, view, send, recv)
        self.out = []

    def swap(self, src, j):
        c = remote(src, self.view(j, None), self.cs.at[len(self.out)], self.cr.at[len(self.out)], self.me.sibling())
        c.start()
        self.out.append((c, j))

    def first(self):
        self.ring.first()
        self.swap(self.own, self.me.z)

    def second(self):
        self.ring.second()
        self.swap(self.view(self.ring.l, None), self.ring.l)
        self.swap(self.view(self.ring.r, None), self.ring.r)

    def last(self):
        self.ring.last()
        self.swap(self.view(self.ring.o, None), self.ring.o)

    def finish(self):
        self.ring.sent()
        for k, (c, j) in enumerate(self.out):
            c.wait_send()
            place = self.view(j, None, 1 - self.me.core)
            remote(place, place, self.cs.at[k], self.cr.at[k], self.me.sibling()).wait_recv()


def rms(z):
    return lax.rsqrt(jnp.mean(z * z, -1, keepdims=True) + EPS)


def turn(v, cos, sin):
    return v * cos + pltpu.roll(v, 64, 1) * sin


def turn_back(v, cos, sin):
    return v * cos - pltpu.roll(v, 64, 1) * sin


def stack_heads(ref, h, a):
    rows = slice(h * BLK, (h + 1) * BLK)
    return jnp.concatenate(
        [ref[rows, (a * GROUP + g) * HS : (a * GROUP + g + 1) * HS] for g in range(GROUP)], 0
    )


def reads(t, block):
    a, b = t - block, NBLK - 1 - t - block
    return ((a >= 0) & (a < NWB)) | ((b >= 0) & (b < NWB))


ZK = [(dz, dc) for dz in range(4) for dc in range(2) if dz or dc]


def front_kernel(
    idx_i, docs, span, wq_i, wo_i, wg_i, wd_i, tok, cot, ain_i, aqkv_i, ares_i, gain1, bias, cos, sin, gain,
    oq_o, oo_o, og, od_o, oe, oi, win_o, p_o, xg, q_h, o_h, hid_h, n2_h,
    x_h, n1_h, e_h, a45_h, bd_h, a3_h, bo_h, a012_h, bqkv_h,
    q, o_o, hid_o, n2, x, n1, eext, a45, bd, a3, bo, a012, bqkv, keep_s,
    ub, idx, wg, ain, aqkv, ares, rq, ro, rg, wdp, rd, cq, co, cg, oq, oo, od, kv_own, kv, p, down, pick70,
    ss, rs, ls, s1, r1, s2, r2, sc, rc, sd, rdn, sk, rk, ez_sems, si, ri, nz_sems,
):
    me = Place()
    sib = me.sibling()
    m = me.ctx
    bar = pltpu.get_barrier_semaphore()

    def hello(t, carry):
        @pl.when(t != m)
        def _():
            pl.semaphore_signal(bar, inc=1, device_id=(me.dp, t), device_id_type=MESH)

        return carry

    lax.fori_loop(0, N_CTX, hello, 0)
    others = [me.at(z=me.step("z", dz), core=lax.rem(me.core + dc, 2)) for dz, dc in ZK if dz % 2 or dc]
    for d in others:
        pl.semaphore_signal(bar, inc=1, device_id=d, device_id_type=MESH)

    adapters = []
    for n, (src, dst) in enumerate(((ain_i, ain), (aqkv_i, aqkv), (ares_i, ares))):
        adapters.append(pltpu.make_async_copy(src, dst, ls.at[21 + n]))
        adapters[-1].start()
    rq[me.x, :12] = wq_i[...]
    rq[me.x, 12:] = jnp.zeros((4, 2048), BF)
    ro[me.x, :12] = wo_i[...]
    ro[me.x, 12:] = jnp.zeros((4, D), BF)
    wdp[:70] = wd_i[...]
    wdp[70:] = jnp.zeros((10, D), BF)
    idx[...] = jnp.full((8, 128), idx_i[0], jnp.int32)

    pl.semaphore_wait(bar, N_CTX - 1 + len(others))

    tiles = [60 if g == 7 else 35 * g // 4 for g in range(8)]

    def panel(g, t):
        col = pl.multiple_of(tiles[g] * 128 + lax.rem(t, 2) * 640, 128)
        return wg.at[lax.div(t, 2), :, pl.ds(col, 640)]

    def strip(t):
        return wdp.at[:, pl.ds(pl.multiple_of(384 * t, 128), 384)]

    def start(c, out):
        c.start()
        out.append(c)

    first = []
    xs = [(k, me.step("x", k), me.at(x=me.step("x", k))) for k in (1, 3, 2)]
    for k, t, d in xs:
        start(remote(rq.at[me.x], rq.at[me.x], s1.at[k - 1, 0], r1.at[k - 1, 0], d), first)
    for k in range(2):
        wg[k, :12] = wg_i[:, k, :]
        wg[k, 12:] = jnp.zeros((4, FF), BF)
    for k, t, d in xs:
        for g in range(8):
            start(remote(panel(g, t), rg.at[me.x, g], s1.at[k - 1, 2 + g], r1.at[k - 1, 2 + g], d), first)
        start(remote(strip(t), rd.at[me.x], s1.at[k - 1, 10], r1.at[k - 1, 10], d), first)
    for k, t, d in xs:
        start(remote(ro.at[me.x], ro.at[me.x], s1.at[k - 1, 1], r1.at[k - 1, 1], d), first)
    mine = []
    for g in range(8):
        start(pltpu.make_async_copy(panel(g, me.x), rg.at[me.x, g], ls.at[2 + g]), mine)
    start(pltpu.make_async_copy(strip(me.x), rd.at[me.x], ls.at[1]), mine)
    side = []
    start(pltpu.make_async_copy(idx, oi.at[me.dp, me.zhi], ls.at[11]), side)
    for n, (dz, dc) in enumerate(ZK):
        d = me.at(z=me.step("z", dz), core=lax.rem(me.core + dc, 2))
        start(remote(idx, oi.at[me.dp, me.zhi], si.at[n], ri.at[n], d), first)

    def from_x(n, ref_of):
        for k in (1, 3, 2):
            f = me.step("x", 4 - k)
            ref = ref_of(f)
            remote(ref, ref, s1.at[k - 1, n], r1.at[k - 1, n], me.at(x=f)).wait_recv()

    row, col = iota((48, 64), 0), iota((48, 64), 1)
    put = jnp.where(
        (lax.rem(col, 16) < 12) & (lax.div(col, 16) * 12 + lax.rem(col, 16) == row), 1.0, 0.0
    ).astype(BF)

    kv[:16] = jnp.zeros((16, BLK, 2 * KW), BF)
    for h in range(2):
        rows = slice(h * BLK, (h + 1) * BLK)
        x[rows] = tok[:, h, :]
        eext[rows, :D] = cot[:, h, :]
    xf = x[...].astype(F32)
    n1[...] = (xf * rms(xf) * gain1[...].astype(F32)).astype(BF)
    row, col = iota((R, 128), 0), iota((R, 128), 1)
    choose = jnp.where((lax.div(col, R) == idx_i[0]) & (lax.rem(col, R) == row), 1.0, 0.0).astype(BF)

    def chosen(ref):
        return mm(choose, ref.reshape(ADAPT * R, ref.shape[-1])).astype(BF)

    for c in adapters:
        c.wait()
    for k in range(3):
        a012[k] = chosen(ain[:, k])
    a3[...] = chosen(ain[:, 3])
    at = pl.multiple_of(me.dp * R, R)
    a45[...] = jnp.zeros_like(a45)
    a45[pl.ds(at, R), :] = chosen(ain[:, 4])
    a45[pl.ds(at + 64, R), :] = chosen(ain[:, 5])
    bqkv[...] = chosen(aqkv[...])
    bo[...] = chosen(ares[:, 0])
    bd[...] = jnp.zeros_like(bd)
    bd[pl.ds(at, R), :] = chosen(ares[:, 1])
    for k, (c0, c1) in enumerate(((0, QW), (QW, QW + KW), (QW + KW, QW + 2 * KW))):
        u = nt(n1[...], a012[k]).astype(BF)
        ub[:, c0:c1] = mm(u, bqkv[:, c0:c1]) + bias[c0:c1].astype(F32)
    eext[:, D:] = nt(eext[:, :D], bd[...]).astype(BF)
    start(pltpu.make_async_copy(eext, oe.at[me.zlo, me.core, me.zhi], ls.at[10]), side)
    kept = []

    def keep_all(*pairs):
        for ref, place in pairs:
            start(pltpu.make_async_copy(ref, place, keep_s.at[len(kept)]), kept)

    keep_all(
        (x, x_h), (n1, n1_h), (eext, e_h), (a45, a45_h), (bd, bd_h), (a3, a3_h), (bo, bo_h), (a012, a012_h), (bqkv, bqkv_h)
    )
    from_x(0, lambda f: rq.at[f])
    cq[...] = mm(put, rq[...].reshape(64, 2048)).astype(BF)
    lo, hi = pl.ds(0, 1024), pl.ds(1024, 1024)

    def qy0(j, h):
        return oq.at[me.zlo, me.core, j, me.zhi, :, lo if h is None else pl.ds(512 * h, 512)]

    def qz0(j, h, core=me.core):
        zl, zh = lax.rem(j, 2), lax.div(j, 2)
        return oq.at[zl, core, :, zh, :, lo] if h is None else oq.at[zl, core, pl.ds(2 * h, 2), zh, :, lo]

    def qz1(j, h):
        cols = hi if h is None else pl.ds(1024 + 512 * h, 512)
        return oq.at[lax.rem(j, 2), me.core, me.y, lax.div(j, 2), :, cols]

    def qy1(j, h, core=me.core):
        return oq.at[:, core, j, :, :, hi] if h is None else oq.at[h, core, j, :, :, hi]

    qa = Ring(me, "y", cq.at[:, lo], qy0, ss.at[0], rs.at[0])
    qb = Ring(me, "z", cq.at[:, hi], qz1, ss.at[1], rs.at[1])
    qa.first()
    qb.first()
    oq[me.zlo, me.core, me.y, me.zhi] = cq[...]
    qa.second()
    qb.second()
    for n in range(8):
        from_x(2 + n, lambda f: rg.at[f, n])
    from_x(10, lambda f: rd.at[f])
    for c in mine:
        c.wait()
    for g in range(8):
        cg[g] = mm(put, rg[:, g].reshape(64, 640)).astype(BF)

    own_g = pltpu.make_async_copy(cg.at[me.slice], og.at[me.x, me.zlo, me.core, me.y, me.zhi], ls.at[14])
    own_g.start()
    zc = []
    for n, (dz, dc) in enumerate(ZK):
        z, core = me.step("z", dz), lax.rem(me.core + dc, 2)
        piece = 2 * (2 * lax.rem(z, 2) + core) + lax.div(z, 2)
        d = me.at(z=z, core=core)
        start(remote(cg.at[piece], og.at[me.x, me.zlo, me.core, me.y, me.zhi], s2.at[n], r2.at[n], d), zc)
    keeper = lax.div(me.y, 2) == me.zhi
    rows4 = pl.ds(lax.rem(me.y, 2) * 8 + me.zhi * 4, 4)
    across = me.at(z=me.step("z", 2))
    d_local = pltpu.make_async_copy(rd, od.at[me.x, rows4], ls.at[15])
    d_cross = remote(rd, od.at[me.x, rows4], sd.at[0], rdn.at[0], across)

    @pl.when(keeper)
    def _():
        d_local.start()

    @pl.when(jnp.logical_not(keeper))
    def _():
        d_cross.start()

    qa.last()
    qb.last()
    qa2 = Ring(me, "z", qz0(me.z, None), qz0, ss.at[2], rs.at[2])
    qb2 = Ring(me, "y", qy1(me.y, None), qy1, ss.at[3], rs.at[3])
    qa2.first()
    qb2.first()
    swaps = []

    def swap(view, j):
        n = len(swaps)
        c = remote(view(j, None), view(j, None), sc.at[n], rc.at[n], sib)
        c.start()
        swaps.append((c, view, j))

    def swapped(n):
        c, view, j = swaps[n]
        c.wait_send()
        ref = view(j, None, 1 - me.core)
        remote(ref, ref, sc.at[n], rc.at[n], sib).wait_recv()

    swap(qz0, me.z)
    swap(qy1, me.y)
    from_x(1, lambda f: ro.at[f])
    co[...] = mm(put, ro[...].reshape(64, D)).astype(BF)
    own_g.wait()
    for n, (dz, dc) in enumerate(ZK):
        z, core = me.step("z", 4 - dz if dz else 0), lax.rem(me.core + dc, 2)
        ref = og.at[me.x, lax.rem(z, 2), core, me.y, lax.div(z, 2)]
        remote(ref, ref, s2.at[n], r2.at[n], me.at(z=z, core=core)).wait_recv()

    def g0a(j, h):
        return og.at[me.x, 0, :, j] if h is None else og.at[me.x, 0, h, j]

    def g0b(j, h):
        return og.at[j, 0] if h is None else og.at[j, 0, h]

    def g1a(j, h):
        return og.at[j, 1, :, me.y] if h is None else og.at[j, 1, h, me.y]

    def g1b(j, h):
        return og.at[:, 1, :, j] if h is None else og.at[:, 1, h, j]

    ga = Ring(me, "y", g0a(me.y, None), g0a, ss.at[4], rs.at[4])
    gb = Ring(me, "x", g1a(me.x, None), g1a, ss.at[5], rs.at[5])
    ga.first()
    gb.first()
    def oy(j, h):
        ref = oo.at[me.zlo, me.core, j, me.zhi]
        return ref if h is None else ref.at[:, pl.ds(768 * h, 768)]

    def oz(j, h, core=me.core):
        zl, zh = lax.rem(j, 2), lax.div(j, 2)
        return oo.at[zl, core, :, zh] if h is None else oo.at[zl, core, pl.ds(2 * h, 2), zh]

    wa = Ring(me, "y", co, oy, ss.at[8], rs.at[8])
    qa2.second()
    qb2.second()
    swap(qz0, qa2.l)
    swap(qy1, qb2.l)
    swap(qz0, qa2.r)
    swap(qy1, qb2.r)
    oo[me.zlo, me.core, me.y, me.zhi] = co[...]

    ga.second()
    gb.second()
    wa.first()
    ga.last()
    gb.last()
    ga2 = Ring(me, "x", g0b(me.x, None), g0b, ss.at[6], rs.at[6])
    gb2 = Ring(me, "y", g1b(me.y, None), g1b, ss.at[7], rs.at[7])

    ga2.first()
    qa2.last()
    qb2.last()
    swap(qz0, qa2.o)
    swap(qy1, qb2.o)

    wa.second()
    rows4b = pl.ds(lax.rem(me.y, 2) * 8 + (1 - me.zhi) * 4, 4)
    rows8 = pl.ds(lax.rem(me.y, 2) * 8, 8)
    ys = [(k, me.step("y", k)) for k in (1, 3, 2)]

    @pl.when(keeper)
    def _():
        d_local.wait()
        ref = od.at[me.x, rows4b]
        remote(rd, ref, sd.at[0], rdn.at[0], across).wait_recv()
        for k, t in ys:
            remote(od.at[me.x, rows8], od.at[me.x, rows8], sd.at[k], rdn.at[k], me.at(y=t)).start()

    for n in range(8):
        swapped(n)
    keep_q = pltpu.make_async_copy(oq, oq_o, ls.at[12])
    keep_q.start()

    c, s = cos[...], sin[...]
    n1v = n1[...]
    for h in (12, 14, 0, 2, 4, 6, 8, 10):
        pair = slice(h * HS, (h + 2) * HS)
        j = mm(n1v, oq[:, :, :, :, :, pair].reshape(D, 2 * HS)) + ub[:, pair]
        for i in range(2):
            v = j[:, i * HS : (i + 1) * HS]
            if h + i < HEADS + KV_HEADS:
                v = turn(v, c, s)
            v = v.astype(BF)
            if h + i < HEADS:
                q[:, (h + i) * HS : (h + i + 1) * HS] = v
            else:
                at = slice((h + i - HEADS) * HS, (h + i - HEADS + 1) * HS)
                kv_own[0, :, at] = v[:BLK]
                kv_own[1, :, at] = v[BLK:]
        if h == 14:
            def send(k, carry):
                t = lax.rem(m + k, N_CTX)
                for half in range(2):
                    block = m if half == 0 else NBLK - 1 - m

                    @pl.when(reads(t, block))
                    def _():
                        src, dst = kv_own.at[half], kv.at[16 + block]
                        remote(src, dst, sk.at[half, k], rk.at[block], (me.dp, t)).start()

                return carry

            lax.fori_loop(1, N_CTX, send, 0)
            kv[16 + m] = kv_own[0]
            kv[16 + NBLK - 1 - m] = kv_own[1]

    gb2.first()
    wa.last()
    wb = Ring(me, "z", oz(me.z, None), oz, ss.at[9], rs.at[9])
    wb.first()
    swap(oz, me.z)
    ez = ZGather(me, eext, oe, *ez_sems, BLK)
    ez.first()
    def dx(j, h):
        return od.at[j] if h is None else od.at[j, pl.ds(8 * h, 8)]

    def arrived(block):
        src = jnp.where(block < N_CTX, block, NBLK - 1 - block)
        remote(kv_own.at[0], kv.at[16 + block], sk.at[0, 0], rk.at[block], (me.dp, src)).wait_recv()

    def near0(j, carry):
        block = m - (NWB - 1) + j

        @pl.when(block >= 0)
        def _():
            arrived(block)

        return carry

    def near1(j, carry):
        block = NBLK - 1 - m - (NWB - 1) + j

        @pl.when(block > m)
        def _():
            arrived(block)

        return carry

    wins = []
    keep_p = []
    for h in range(2):
        lax.fori_loop(0, NWB - 1, near0 if h == 0 else near1, 0)
        win = kv.at[pl.ds(m if h == 0 else NBLK - 1 - m, NWB)]
        start(pltpu.make_async_copy(win, win_o.at[h], ls.at[16 + h]), wins)
        base = (m if h == 0 else NBLK - 1 - m) * BLK
        kpos = base - WIN + iota((BLK, KEYS), 1)
        qpos = base + iota((BLK, KEYS), 0)
        pos = base + iota((BLK, 1), 0)
        begin, end = jnp.zeros((BLK, 1), jnp.int32), 0
        for i in range(8):
            end = end + docs[0, i]
            begin = jnp.where(end <= pos, end, begin)
        low = jnp.maximum(begin, pos - span[0] + 1)
        keep = (kpos <= qpos) & (kpos >= low)
        for a in range(KV_HEADS):
            qs = stack_heads(q, h, a)
            k = win[:, :, a * HS : (a + 1) * HS].reshape(KEYS, HS)
            v = win[:, :, KW + a * HS : KW + (a + 1) * HS].reshape(KEYS, HS)
            sco = nt(qs, k) * SCALE
            sco = jnp.where(keep[None], sco.reshape(GROUP, BLK, KEYS), -1e30)
            e = jnp.exp(sco - jnp.max(sco, -1, keepdims=True))
            pr = (e / jnp.sum(e, -1, keepdims=True)).astype(BF).reshape(GROUP * BLK, KEYS)
            p[2 * h + a] = pr
            o = mm(pr, v).astype(BF)
            for g in range(GROUP):
                o_o[h * BLK : (h + 1) * BLK, (a * GROUP + g) * HS : (a * GROUP + g + 1) * HS] = o[
                    g * BLK : (g + 1) * BLK
                ]
        if h == 0:
            for k, t in ys:
                f = me.step("y", 4 - k)

                @pl.when(lax.div(f, 2) == me.zhi)
                def _():
                    ref = od.at[me.x, pl.ds(lax.rem(f, 2) * 8, 8)]
                    remote(ref, ref, sd.at[k], rdn.at[k], me.at(y=f)).wait_recv()

            da = Ring(me, "x", od.at[me.x], dx, ss.at[10], rs.at[10])
            da.first()
            wb.second()
            swap(oz, wb.l)
            swap(oz, wb.r)
            ga2.second()

    start(pltpu.make_async_copy(p, p_o, ls.at[18]), keep_p)
    ez.second()
    wb.last()
    swap(oz, wb.o)
    for n in range(8, 12):
        swapped(n)
    keep_o = pltpu.make_async_copy(oo, oo_o, ls.at[13])
    keep_o.start()

    ob = o_o[...]
    u3 = nt(ob, a3[...]).astype(BF)
    hid = x[...].astype(F32) + mm(ob, oo[...].reshape(D, D)) + mm(u3, bo[...])
    hid_o[...] = hid
    nv = (hid * rms(hid) * gain[...].astype(F32)).astype(BF)
    n2[:, :D] = nv
    n2[:, D:] = nt(nv, a45[...]).astype(BF)
    nz = ZGather(me, n2, xg, *nz_sems, BLK)
    nz.first()
    keep_all((q, q_h), (o_o, o_h), (hid_o, hid_h), (n2, n2_h))
    start(pltpu.make_async_copy(n2, xg.at[me.zlo, me.core, me.zhi], ls.at[19]), side)
    gb2.second()
    nz.second()
    da.second()
    off = FV * me.slice - 128 * window_tile(me.slice)

    def pack(r, strips, fresh):
        base = 256 * r - off
        i0 = jnp.minimum(lax.div(jnp.maximum(base, 0), 70), 11)
        if fresh:
            rw, cl = iota((256, 400), 0) + base, iota((256, 400), 1)
            i, k = i0 + lax.div(cl, 80), lax.rem(cl, 80)
            pick70[r] = jnp.where((k < 70) & (i * 70 + k == rw), 1.0, 0.0).astype(BF)
        for j in strips:
            src = od[j, pl.ds(i0, 5)].reshape(400, 384)
            at = pl.ds(pl.multiple_of(384 * j, 128), 384)
            down[256 * r : 256 * (r + 1), at] = mm(pick70[r], src).astype(BF)

    for r in range(5):
        pack(r, (da.i, da.l, da.r), True)
    nz.last()
    ez.last()
    da.last()
    for r in range(5):
        pack(r, (da.o,), False)
    keep_d = pltpu.make_async_copy(down, od_o, ls.at[20])
    keep_d.start()
    ga2.last()
    gb2.last()

    for r in (qa, qb, qa2, qb2, wa, wb, ga, gb, ga2, gb2, da):
        r.sent()
    for c in first + zc:
        c.wait_send()

    @pl.when(jnp.logical_not(keeper))
    def _():
        d_cross.wait_send()

    @pl.when(keeper)
    def _():
        for k, t in ys:
            remote(od.at[me.x, rows8], od.at[me.x, rows8], sd.at[k], rdn.at[k], me.at(y=t)).wait_send()

    def sent(k, carry):
        t = lax.rem(m + k, N_CTX)
        for half in range(2):
            block = m if half == 0 else NBLK - 1 - m

            @pl.when(reads(t, block))
            def _():
                src, dst = kv_own.at[half], kv.at[16 + block]
                remote(src, dst, sk.at[half, k], rk.at[block], (me.dp, t)).wait_send()

        return carry

    lax.fori_loop(1, N_CTX, sent, 0)
    for n, (dz, dc) in enumerate(ZK):
        z, core = me.step("z", 4 - dz if dz else 0), lax.rem(me.core + dc, 2)
        ref = oi.at[2 * lax.rem(z, 2) + core, lax.div(z, 2)]
        remote(ref, ref, si.at[n], ri.at[n], me.at(z=z, core=core)).wait_recv()
    ez.finish()
    nz.finish()
    for c in side + wins + keep_p + kept + [keep_q, keep_o, keep_d]:
        c.wait()


def front(*args):
    outs = (
        sds((2, 2, 4, 2, 48, 2048), BF),
        sds((2, 2, 4, 2, 48, D), BF),
        sds((4, 2, 2, 4, 2, 48, 640), BF),
        sds((FW, D), BF),
        sds((2, 2, 2, ROWS, DX), BF),
        sds((4, 2, 8, 128), jnp.int32),
        sds((2, NWB, BLK, 2 * KW), BF),
        sds((4, GROUP * BLK, KEYS), BF),
        sds((2, 2, 2, ROWS, DX), BF),
        sds((ROWS, D), BF),
        sds((ROWS, D), BF),
        sds((ROWS, D), F32),
        sds((ROWS, DX), BF),
        sds((ROWS, D), BF),
        sds((ROWS, D), BF),
        sds((ROWS, DX), BF),
        sds((EXT, D), BF),
        sds((EXT, D), BF),
        sds((R, D), BF),
        sds((R, D), BF),
        sds((3, R, D), BF),
        sds((R, 2048), BF),
    )
    four = (DMA((4,)),) * 4
    scratch = [pltpu.VMEM(v.shape, v.dtype) for v in outs[9:]] + [
        DMA((13,)),
        pltpu.VMEM((ROWS, 2048), F32),
        pltpu.VMEM((8, 128), jnp.int32),
        pltpu.VMEM((2, 16, FF), BF),
        pltpu.VMEM((ADAPT, 6, R, D), BF),
        pltpu.VMEM((ADAPT, R, 2048), BF),
        pltpu.VMEM((ADAPT, 2, R, D), BF),
        pltpu.VMEM((4, 16, 2048), BF),
        pltpu.VMEM((4, 16, D), BF),
        pltpu.VMEM((4, 8, 16, 640), BF),
        pltpu.VMEM((80, D), BF),
        pltpu.VMEM((4, 80, 384), BF),
        pltpu.VMEM((48, 2048), BF),
        pltpu.VMEM((48, D), BF),
        pltpu.VMEM((8, 48, 640), BF),
        pltpu.VMEM((2, 2, 4, 2, 48, 2048), BF),
        pltpu.VMEM((2, 2, 4, 2, 48, D), BF),
        pltpu.VMEM((4, 16, 80, 384), BF),
        pltpu.VMEM((2, BLK, 2 * KW), BF),
        pltpu.VMEM((16 + NBLK, BLK, 2 * KW), BF),
        pltpu.VMEM((4, GROUP * BLK, KEYS), BF),
        pltpu.VMEM((FW, D), BF),
        pltpu.VMEM((5, 256, 400), BF),
        DMA((11, 4)),
        DMA((11, 4)),
        DMA((24,)),
        DMA((3, 11)),
        DMA((3, 11)),
        DMA((7,)),
        DMA((7,)),
        DMA((12,)),
        DMA((12,)),
        DMA((4,)),
        DMA((4,)),
        DMA((2, N_CTX)),
        DMA((NBLK,)),
        four,
        DMA((7,)),
        DMA((7,)),
        four,
    ]
    return pl.pallas_call(
        front_kernel,
        out_shape=outs,
        in_specs=[SM] * 3 + [VM] * 6 + [ANY] * 3 + [VM] * 5,
        out_specs=[ANY] * 22,
        scratch_shapes=scratch,
        compiler_params=pltpu.CompilerParams(collective_id=1, has_side_effects=True, vmem_limit_bytes=VMEM_LIMIT),
    )(*args)


class Fan:
    def __init__(self, me, axis, view, send, recv):
        self.me, self.axis, self.view, self.send, self.recv = me, axis, view, send, recv
        self.i = getattr(me, axis)

    def copy(self, k, j, to):
        ref = self.view(j)
        return remote(ref, ref, self.send.at[k - 1], self.recv.at[k - 1], self.me.at(**{self.axis: to}))

    def first(self):
        self.out = []
        for k in (1, 3, 2):
            c = self.copy(k, self.i, self.me.step(self.axis, k))
            c.start()
            self.out.append(c)

    def last(self):
        for k in (1, 3, 2):
            f = self.me.step(self.axis, 4 - k)
            self.copy(k, f, f).wait_recv()

    def sent(self):
        for c in self.out:
            c.wait_send()


def norm_back(z, gain, grad):
    r = rms(z)
    t = gain * grad
    return r * t - z * (r * r * r) * jnp.mean(t * z, -1, keepdims=True)


def rear_kernel(
    xg, oe, og, wd_i, ad_all, b_all, e_i, hid_i, n2_i, q_i, o_i, p_i, win_i, wo_i, wq_i, x_i, n1_i,
    a012_i, a3_i, a45_i, bqkv_i, bo_i, bd_i, cos_i, sin_i, oi, gain1, gain2,
    out_h, gt_h, early, late,
    a012, a3, a45, bqkv, bo, bd, cos, sin, out_o, gt_o, ld2,
    wgu, wdo, ad_in, b_in, ad, acc, xb, sib_out, sib_got, red, got2, ft,
    e, hid, n2, q, o, p, win, x, n1,
    gn2, ysum, gh, go, gq, gwin, got, gkv, gj, l1, l2, gf, gl1, gl2, red1, red2,
    wl, xl, ld, sb_s, sb_r, rz_s, rz_r, f_s, f_r, a_s, a_r, b_s, b_r, kv_s, kv_r, ls,
    ring_s, ring_r, fan_s, fan_r, core_s, core_r,
):
    me = Place()
    sib = me.sibling()
    m = me.ctx
    tile = window_tile(me.slice)
    off = FV * me.slice - 128 * tile
    bar = pltpu.get_barrier_semaphore()

    def hello(t, carry):
        @pl.when(t != m)
        def _():
            pl.semaphore_signal(bar, inc=1, device_id=(me.dp, t), device_id_type=MESH)

        return carry

    def load(src, dst, sem):
        c = pltpu.make_async_copy(src, dst, sem)
        c.start()
        return c

    cols = pl.ds(pl.multiple_of(tile * 128, 128), FW)
    wloads = [
        load(ad_all.at[:, :, cols], ad_in, wl.at[0]),
        load(b_all.at[:, :, :, cols], b_in, wl.at[1]),
    ]
    for k in range(4):
        wloads.append(load(og.at[k], wgu.at[pl.ds(0, D), pl.ds(640 * k, 640)], wl.at[2 + k]))
    wloads.append(load(wd_i, wdo.at[pl.ds(0, FW), pl.ds(0, D)], wl.at[6]))
    steps = [(1 - me.zlo, 1 - me.core), (1 - me.zlo, me.core), (me.zlo, 1 - me.core), (me.zlo, me.core)]

    def rows_in(n):
        zl, core = steps[n]
        return [load(src.at[zl, core], xb.at[n % 2, k], xl.at[n % 2, k]) for k, src in enumerate((xg, oe))]

    coming = [rows_in(0), rows_in(1)]
    lax.fori_loop(0, N_CTX, hello, 0)
    others = [me.at(z=me.step("z", 1)), me.at(z=me.step("z", 3)), sib]
    for d in others:
        pl.semaphore_signal(bar, inc=1, device_id=d, device_id_type=MESH)
    loads = [
        load(src, dst, ld.at[n])
        for n, (src, dst) in enumerate(
            (
                (e_i, e), (hid_i, hid), (n2_i, n2), (o_i, o), (q_i, q),
                (win_i, win), (p_i, p), (n1_i, n1), (x_i, x),
            )
        )
    ]
    small = [
        load(src, dst, ld2.at[n])
        for n, (src, dst) in enumerate(
            (
                (a45_i, a45), (bo_i, bo), (a3_i, a3), (a012_i, a012), (bqkv_i, bqkv), (bd_i, bd), (cos_i, cos), (sin_i, sin),
            )
        )
    ]
    for c in wloads[:2]:
        c.wait()
    row, col = iota((64, 128), 0), iota((64, 128), 1)
    choose = jnp.zeros((64, 128), F32)
    for k in range(4):
        hit = (lax.div(row, R) == k) & (lax.rem(row, R) == lax.rem(col, R)) & (lax.div(col, R) == oi[k, 0, :1, :1])
        choose += jnp.where(hit, 1.0, 0.0)
    choose = choose.astype(BF)
    fcol = iota((64, FW), 1)
    valid = (fcol >= off) & (fcol < off + FV)
    ad[:64] = jnp.where(valid, mm(choose, ad_in[...].reshape(128, FW)), 0.0).astype(BF)
    ad[64:] = jnp.zeros((64, FW), BF)
    eye = jnp.where(iota((EXT, EXT), 0) == iota((EXT, EXT), 1), 1.0, 0.0).astype(BF)
    wdo[:FW, D:] = tn(ad[...], eye).astype(BF)
    none = jnp.zeros((64, FW), BF)
    wgu[D : D + 64, :FW] = mm(choose, b_in[:, 0].reshape(128, FW)).astype(BF)
    wgu[D + 64 :, :FW] = none
    wgu[D : D + 64, FW:] = none
    wgu[D + 64 :, FW:] = mm(choose, b_in[:, 1].reshape(128, FW)).astype(BF)
    acc[...] = jnp.zeros_like(acc)
    for c in wloads[2:6]:
        c.wait()
    sib_copies, z_copies = [], []

    def z_push(j, k, slot, z):
        c = remote(red.at[j, k], got2.at[slot, k], rz_s.at[j, k], rz_r.at[slot, k], me.at(z=z))
        c.start()
        z_copies.append(c)

    for n in range(4):
        for c in coming[n]:
            c.wait()
        xv = xb[n % 2, 0].reshape(2 * ROWS, DX)
        ev = xb[n % 2, 1].reshape(2 * ROWS, DX)
        both = mm(xv, wgu[...])
        gate, up = both[:, :FW], both[:, FW:]
        if n == 0:
            wloads[6].wait()
        gm = nt(ev, wdo[:FW])
        sig = 1.0 / (1.0 + jnp.exp(-gate))
        sl = gate * sig
        act = (sl * up).astype(BF)
        gg = (gm * up * (sig * (1.0 + gate * (1.0 - sig)))).astype(BF)
        gu = (gm * sl).astype(BF)
        grads = jnp.concatenate([gg, gu], 1)
        acc[0] += tn(ev[:, D:], act)[:64]
        by_u = tn(xv[:, D:], grads)
        acc[1] += by_u[:64, :FW]
        acc[2] += by_u[64:, FW:]
        if n < 2:
            coming.append(rows_in(n + 2))
        if n == 0:
            pl.semaphore_wait(bar, N_CTX - 1 + len(others))
        for k in (1, 0):
            wide = nt(grads, wgu[...]) if k == 1 else mm(act, wdo[:FW])
            total = gn2 if k == 1 else ysum
            if n % 2 == 0:
                for zh in range(2):
                    rows = slice(zh * ROWS, (zh + 1) * ROWS)
                    sib_out[n // 2, k, zh] = wide[rows].astype(BF)
                c = remote(sib_out.at[n // 2, k], sib_got.at[n // 2, k], sb_s.at[n // 2, k], sb_r.at[n // 2, k], sib)
                c.start()
                sib_copies.append(c)
            else:
                theirs = sib_got.at[n // 2, k]
                remote(theirs, theirs, sb_s.at[n // 2, k], sb_r.at[n // 2, k], sib).wait_recv()
                if n == 1:
                    for zh in range(2):
                        rows = slice(zh * ROWS, (zh + 1) * ROWS)
                        red[zh, k] = (wide[rows] + theirs[zh].astype(F32)).astype(BF)
                        z_push(zh, k, me.zhi, 2 * zh + 1 - me.zlo)
                else:
                    mine = me.zhi == 1
                    far = jnp.where(mine, wide[:ROWS], wide[ROWS:])
                    near = jnp.where(mine, wide[ROWS:], wide[:ROWS])
                    red[2, k] = (far + theirs[1 - me.zhi].astype(F32)).astype(BF)
                    z_push(2, k, 2, me.step("z", 2))
                    total[...] = near + theirs[me.zhi].astype(F32)
    for k in range(3):
        v = jnp.where(valid, acc[k], 0.0).astype(BF)
        for i in range(4):
            for t in range(10):
                ft[i * 30 + k * 10 + t] = v[R * i : R * (i + 1), 128 * t : 128 * (t + 1)]
    for t in range(120, 128):
        ft[t] = jnp.zeros((R, 128), BF)
    xy = me.y * 4 + me.x

    def plane(k):
        return me.at(x=lax.rem(k, 4), y=lax.div(k, 4))

    def f_copy(t):
        return remote(ft.at[pl.ds(8 * t, 8)], gf.at[xy], f_s.at[t], f_r.at[xy], plane(t))

    def f_send(k, carry):
        f_copy(lax.rem(xy + k, 16)).start()
        return carry

    lax.fori_loop(1, 16, f_send, 0)
    gf[xy] = ft[pl.ds(8 * xy, 8)]
    wo_load = load(wo_i, wdo.at[:, pl.ds(0, D)], ld.at[9])
    wq_load = load(wq_i, wgu.at[pl.ds(0, D), pl.ds(0, 2048)], ld.at[10])

    def z_take(k, total):
        for slot in range(3):
            ref = got2.at[slot, k]
            remote(ref, ref, rz_s.at[slot, k], rz_r.at[slot, k], sib).wait_recv()
            total[...] += ref[...].astype(F32)

    z_take(1, gn2)
    for c in loads[:4] + small + [wo_load]:
        c.wait()

    def put(tiles, at, v):
        for t in range(v.shape[1] // 128):
            tiles[at + t] = v[:, 128 * t : 128 * (t + 1)].astype(BF)

    gue = gn2[:, D:].astype(BF)
    gn = gn2[:, :D] + mm(gue, a45[...])
    ghv = e[:, :D].astype(F32) + norm_back(hid[...], gain2[...].astype(F32), gn)
    gh[...] = ghv
    ghb = ghv.astype(BF)
    ob = o[...]
    gu3 = nt(ghb, bo[...]).astype(BF)
    go[...] = (nt(ghb, wdo[:, :D]) + mm(gu3, a3[...])).astype(BF)
    u3 = nt(ob, a3[...]).astype(BF)
    s = me.dp

    put(l1, 0, tn(gu3, ob))
    g45b = tn(gue, n2[:, :D]).astype(BF)
    pick_own = jnp.where((iota((R, EXT), 1) == iota((R, EXT), 0) + s * R), 1.0, 0.0).astype(BF)
    pick_up = jnp.where((iota((R, EXT), 1) == iota((R, EXT), 0) + s * R + 64), 1.0, 0.0).astype(BF)
    put(l1, 12, mm(pick_own, g45b))
    put(l1, 24, mm(pick_up, g45b))
    put(l1, 36, tn(u3, ghb))
    for t in range(48, 64):
        l1[t] = jnp.zeros((R, 128), BF)

    def l_copy(tiles, buf, ss, rs, t):
        return remote(tiles.at[pl.ds(2 * t, 2)], buf.at[m], ss.at[t], rs.at[m], (me.dp, t))

    def l_send(tiles, buf, ss, rs):
        def one(k, carry):
            l_copy(tiles, buf, ss, rs, lax.rem(m + k, N_CTX)).start()
            return carry

        lax.fori_loop(1, N_CTX, one, 0)
        buf[m] = tiles[pl.ds(2 * m, 2)]

    def l_sum(buf, ss, rs):
        def one(k, carry):
            t = lax.rem(m + k, N_CTX)
            remote(buf.at[t], buf.at[t], ss.at[t], rs.at[t], (me.dp, t)).wait_recv()
            return carry + buf[t].astype(F32)

        return lax.fori_loop(1, N_CTX, one, buf[m].astype(F32)).astype(BF)

    def l_sent(tiles, buf, ss, rs):
        def one(k, carry):
            l_copy(tiles, buf, ss, rs, lax.rem(m + k, N_CTX)).wait_send()
            return carry

        lax.fori_loop(1, N_CTX, one, 0)

    l_send(l1, gl1, a_s, a_r)

    def covers(t, w, owner, h):
        block = owner if h == 0 else NBLK - 1 - owner
        j = block - ((t if w == 0 else NBLK - 1 - t) - (NWB - 1))
        ok = (j >= 0) & (j < NWB)
        return j, ok if w == 0 else ok & (block > t)

    def kv_copy(w, h, t, j):
        return remote(gwin.at[w, j], got.at[h, w, j], kv_s.at[h, w, t], kv_r.at[h, w, j], (me.dp, t))

    for c in loads[4:7]:
        c.wait()
    for w in (1, 0):
        for a in range(KV_HEADS):
            qs, gv, ov = stack_heads(q, w, a), stack_heads(go, w, a), stack_heads(o, w, a)
            k = win[w, :, :, a * HS : (a + 1) * HS].reshape(KEYS, HS)
            v = win[w, :, :, KW + a * HS : KW + (a + 1) * HS].reshape(KEYS, HS)
            pr = p[2 * w + a]
            delta = jnp.sum(gv.astype(F32) * ov.astype(F32), -1, keepdims=True)
            ds = (pr.astype(F32) * (nt(gv, v) - delta)).astype(BF)
            gqv = mm(ds, k) * SCALE
            for g in range(GROUP):
                cols = slice((a * GROUP + g) * HS, (a * GROUP + g + 1) * HS)
                gq[w * BLK : (w + 1) * BLK, cols] = gqv[g * BLK : (g + 1) * BLK]
            gwin[w, :, :, a * HS : (a + 1) * HS] = (tn(ds, qs) * SCALE).astype(BF).reshape(NWB, BLK, HS)
            gwin[w, :, :, KW + a * HS : KW + (a + 1) * HS] = tn(pr, gv).astype(BF).reshape(NWB, BLK, HS)

        if w == 0:
            def both_windows(j, carry):
                j1 = j + 2 * m - (NBLK - 1)

                @pl.when(j1 >= 0)
                def _():
                    gwin[0, j] = (gwin[0, j].astype(F32) + gwin[1, j1].astype(F32)).astype(BF)

                return carry

            lax.fori_loop(0, NWB, both_windows, 0)

        def kv_send(k, carry):
            t = lax.rem(m + k, N_CTX)
            for h in range(2):
                j, ok = covers(m, w, t, h)

                @pl.when(ok)
                def _():
                    kv_copy(w, h, t, j).start()

            return carry

        lax.fori_loop(1, N_CTX, kv_send, 0)
        for h in range(2):
            j, ok = covers(m, w, m, h)

            @pl.when(ok)
            def _():
                c = pltpu.make_async_copy(gwin.at[w, j], got.at[h, w, j], ls.at[2 * w + h])
                c.start()
                c.wait()


    def f_take(k, carry):
        t = lax.rem(xy + k, 16)
        remote(gf.at[t], gf.at[t], f_s.at[t], f_r.at[t], plane(t)).wait_recv()
        return carry + gf[t].astype(F32)

    red1[:8] = lax.fori_loop(1, 16, f_take, gf[xy].astype(F32)).astype(BF)
    red1[8:] = l_sum(gl1, a_s, a_r)

    def vz(j, h):
        ref = early.at[me.y, me.x, lax.rem(j, 2), me.core, lax.div(j, 2)]
        return ref if h is None else ref.at[pl.ds(5 * h, 5)]

    own_e = pltpu.make_async_copy(red1, vz(me.z, None), ls.at[5])
    own_e.start()
    rz = Ring(me, "z", red1, vz, ring_s.at[0], ring_r.at[0])
    rz.first()
    ta, tb = pl.ds(0, 5), pl.ds(5, 5)

    def x0(j, h):
        return early.at[me.y, j, :, me.core, :, ta] if h is None else early.at[me.y, j, h, me.core, :, ta]

    def y0(j, h):
        return early.at[j, :, :, me.core, :, ta] if h is None else early.at[j, pl.ds(2 * h, 2), :, me.core, :, ta]

    def y1(j, h):
        return early.at[j, me.x, :, me.core, :, tb] if h is None else early.at[j, me.x, h, me.core, :, tb]

    def x1(j, h):
        return early.at[:, j, :, me.core, :, tb] if h is None else early.at[pl.ds(2 * h, 2), j, :, me.core, :, tb]

    gkv[...] = jnp.zeros_like(gkv)

    def take(k, carry):
        t = lax.rem(m + N_CTX - k, N_CTX)
        for w in range(2):
            for h in range(2):
                j, ok = covers(t, w, m, h)

                @pl.when(ok & (k > 0))
                def _():
                    ref = got.at[h, w, j]
                    remote(ref, ref, kv_s.at[h, w, t], kv_r.at[h, w, j], (me.dp, t)).wait_recv()

                @pl.when(ok)
                def _():
                    gkv[h] += got[h, w, j].astype(F32)

        return carry

    lax.fori_loop(0, 20, take, 0)
    rz.second()
    rz.last()
    own_e.wait()
    ra = Ring(me, "x", x0(me.x, None), x0, ring_s.at[1], ring_r.at[1])
    rb = Ring(me, "y", y1(me.y, None), y1, ring_s.at[2], ring_r.at[2])
    ra.first()
    rb.first()

    lax.fori_loop(20, N_CTX, take, 0)

    for c in loads[7:] + [wq_load]:
        c.wait()
    c, sn = cos[...], sin[...]
    for h in range(HEADS):
        cols = slice(h * HS, (h + 1) * HS)
        gj[:, cols] = turn_back(gq[:, cols], c, sn).astype(BF)
    for a in range(KV_HEADS):
        v = jnp.concatenate([gkv[0, :, a * HS : (a + 1) * HS], gkv[1, :, a * HS : (a + 1) * HS]], 0)
        gj[:, QW + a * HS : QW + (a + 1) * HS] = turn_back(v, c, sn).astype(BF)
    gj[:, QW + KW :] = jnp.concatenate([gkv[0, :, KW:], gkv[1, :, KW:]], 0).astype(BF)
    n1b = n1[...]
    more = jnp.zeros((ROWS, D), F32)
    for i, (lo, hi) in enumerate(((0, QW), (QW, QW + KW), (QW + KW, QW + 2 * KW))):
        am = a012[i]
        u = nt(n1b, am).astype(BF)
        gjm = gj[:, lo:hi]
        gum = nt(gjm, bqkv[:, lo:hi]).astype(BF)
        more += mm(gum, am)
        put(l2, 36 + lo // 128, tn(u, gjm))
        put(l2, 12 * i, tn(gum, n1b))
    z_take(0, ysum)
    ud = ysum[:, D:].astype(BF)
    y = hid[...] + ysum[:, :D] + mm(ud, bd[...])
    for h in range(2):
        out_o[:, h, :] = y[h * BLK : (h + 1) * BLK].astype(BF)
    out_load = load(out_o, out_h, ld2.at[8])
    put(l2, 52, mm(pick_own, tn(ud, e[:, :D]).astype(BF)))
    l_send(l2, gl2, b_s, b_r)
    gn = nt(gj[...], wgu[:D, :2048]) + more
    gt = gh[...] + norm_back(x[...].astype(F32), gain1[...].astype(F32), gn)
    for h in range(2):
        gt_o[:, h, :] = gt[h * BLK : (h + 1) * BLK].astype(BF)
    gt_load = load(gt_o, gt_h, ld2.at[9])

    ra.second()
    rb.second()
    red2[...] = l_sum(gl2, b_s, b_r)

    def uz(j):
        return late.at[me.y, me.x, lax.rem(j, 2), me.core, lax.div(j, 2)]

    own_l = pltpu.make_async_copy(red2, uz(me.z), ls.at[6])
    own_l.start()
    own_l.wait()
    def f_sent(k, carry):
        f_copy(lax.rem(xy + k, 16)).wait_send()
        return carry

    def kv_sent(k, carry):
        t = lax.rem(m + k, N_CTX)
        for w in range(2):
            for h in range(2):
                j, ok = covers(m, w, t, h)

                @pl.when(ok)
                def _():
                    kv_copy(w, h, t, j).wait_send()

        return carry

    fz = Fan(me, "z", uz, fan_s.at[0], fan_r.at[0])
    fz.first()
    ra.last()
    rb.last()
    l_sent(l1, gl1, a_s, a_r)
    lax.fori_loop(1, 16, f_sent, 0)
    fz.last()
    t0, t1 = pl.ds(0, 1), pl.ds(1, 1)
    fx = Fan(me, "x", lambda j: late.at[me.y, j, :, me.core, :, t0], fan_s.at[1], fan_r.at[1])
    fy = Fan(me, "y", lambda j: late.at[j, me.x, :, me.core, :, t1], fan_s.at[2], fan_r.at[2])
    fx.first()
    fy.first()
    rc = Ring(me, "y", y0(me.y, None), y0, ring_s.at[3], ring_r.at[3])
    rd = Ring(me, "x", x1(me.x, None), x1, ring_s.at[4], ring_r.at[4])
    rc.first()
    rd.first()
    swaps = []

    def swap(view, j):
        n = len(swaps)
        c = remote(view(j, me.core), view(j, me.core), core_s.at[n], core_r.at[n], sib)
        c.start()
        swaps.append((c, view, j))

    def ey(j, core):
        return early.at[j, :, :, core, :, ta]

    def ex(j, core):
        return early.at[:, j, :, core, :, tb]

    def late_all(j, core):
        return late.at[j, :, :, core]

    swap(ey, me.y)
    swap(ex, me.x)
    lax.fori_loop(1, N_CTX, kv_sent, 0)
    fx.last()
    fy.last()
    fy2 = Fan(me, "y", lambda j: late.at[j, :, :, me.core, :, t0], fan_s.at[3], fan_r.at[3])
    fx2 = Fan(me, "x", lambda j: late.at[:, j, :, me.core, :, t1], fan_s.at[4], fan_r.at[4])
    fy2.first()
    fx2.first()
    rc.second()
    rd.second()
    swap(ey, rc.l)
    swap(ex, rd.l)
    swap(ey, rc.r)
    swap(ex, rd.r)
    l_sent(l2, gl2, b_s, b_r)
    rc.last()
    rd.last()
    swap(ey, rc.o)
    swap(ex, rd.o)
    fy2.last()
    fx2.last()
    for k in range(4):
        swap(late_all, k)

    for c in sib_copies + z_copies:
        c.wait_send()
    out_load.wait()
    gt_load.wait()
    for r in (rz, ra, rb, rc, rd, fz, fx, fy, fx2, fy2):
        r.sent()


    for n, (c, view, j) in enumerate(swaps):
        c.wait_send()
        ref = view(j, 1 - me.core)
        remote(ref, ref, core_s.at[n], core_r.at[n], sib).wait_recv()


def rear(xg, oe, og, wd, ad_all, b_all, e, hid, n2, q, o, p, win, wo, wq, x, n1, *small):
    outs = (
        sds((BLK, 2, D), BF),
        sds((BLK, 2, D), BF),
        sds((4, 4, 2, 2, 2, 10, R, 128), BF),
        sds((4, 4, 2, 2, 2, 2, R, 128), BF),
    )
    block = (ROWS, DX)
    scratch = [pltpu.VMEM(v.shape, v.dtype) for v in small[:8]] + [
        pltpu.VMEM((BLK, 2, D), BF),
        pltpu.VMEM((BLK, 2, D), BF),
        DMA((10,)),
        pltpu.VMEM((DX, 2 * FW), BF),
        pltpu.VMEM((D, DX), BF),
        pltpu.VMEM((ADAPT, R, FW), BF),
        pltpu.VMEM((ADAPT, 2, R, FW), BF),
        pltpu.VMEM((EXT, FW), BF),
        pltpu.VMEM((3, 64, FW), F32),
        pltpu.VMEM((2, 2, 2) + block, BF),
        pltpu.VMEM((2, 2, 2) + block, BF),
        pltpu.VMEM((2, 2, 2) + block, BF),
        pltpu.VMEM((3, 2) + block, BF),
        pltpu.VMEM((3, 2) + block, BF),
        pltpu.VMEM((128, R, 128), BF),
    ]
    scratch += [pltpu.VMEM(v.shape, v.dtype) for v in (e, hid, n2, q, o, p, win, x, n1)]
    scratch += [
        pltpu.VMEM(block, F32),
        pltpu.VMEM(block, F32),
        pltpu.VMEM((ROWS, D), F32),
        pltpu.VMEM((ROWS, D), BF),
        pltpu.VMEM((ROWS, D), F32),
        pltpu.VMEM((2, NWB, BLK, 2 * KW), BF),
        pltpu.VMEM((2, 2, NWB, BLK, 2 * KW), BF),
        pltpu.VMEM((2, BLK, 2 * KW), F32),
        pltpu.VMEM((ROWS, 2048), BF),
        pltpu.VMEM((64, R, 128), BF),
        pltpu.VMEM((64, R, 128), BF),
        pltpu.VMEM((16, 8, R, 128), BF),
        pltpu.VMEM((N_CTX, 2, R, 128), BF),
        pltpu.VMEM((N_CTX, 2, R, 128), BF),
        pltpu.VMEM((10, R, 128), BF),
        pltpu.VMEM((2, R, 128), BF),
        DMA((7,)),
        DMA((2, 2)),
        DMA((11,)),
        DMA((2, 2)),
        DMA((2, 2)),
        DMA((3, 2)),
        DMA((3, 2)),
        DMA((16,)),
        DMA((16,)),
        DMA((N_CTX,)),
        DMA((N_CTX,)),
        DMA((N_CTX,)),
        DMA((N_CTX,)),
        DMA((2, 2, N_CTX)),
        DMA((2, 2, NWB)),
        DMA((7,)),
        DMA((5, 4)),
        DMA((5, 4)),
        DMA((5, 3)),
        DMA((5, 3)),
        DMA((12,)),
        DMA((12,)),
    ]
    return pl.pallas_call(
        rear_kernel,
        out_shape=outs,
        in_specs=[ANY] * 25 + [VM] * 3,
        out_specs=[ANY] * 4,
        scratch_shapes=scratch,
        compiler_params=pltpu.CompilerParams(collective_id=2, has_side_effects=True, vmem_limit_bytes=VMEM_LIMIT),
    )(xg, oe, og, wd, ad_all, b_all, e, hid, n2, q, o, p, win, wo, wq, x, n1, *small)


def spread_kernel(oi, early_i, late_i, ain_o, aff_o, bqkv_o, bres_o, bff_o, early, late, loaded, sem):
    step = pl.program_id(0)
    e = lax.rem(step + 1, ADAPT)
    copies = [pltpu.make_async_copy(early_i, early, sem.at[0]), pltpu.make_async_copy(late_i, late, sem.at[1])]

    @pl.when(step == 0)
    def _():
        loaded[0] = 0
        for c in copies:
            c.start()

    for ref in (ain_o, aff_o, bqkv_o, bres_o, bff_o):
        ref[...] = jnp.zeros_like(ref)

    def local_tile(ref, at, s, n):
        k, j = n // 2, n % 2
        return ref[k // 8, k % 4, s // 2, s % 2, (k // 4) % 2, at + j].astype(F32)

    def ff_tile(piece, n):
        k, j = n // 8, n % 8
        return early[k // 4, k % 4, piece // 4, (piece // 2) % 2, piece % 2, j].astype(F32)

    used = step == ADAPT - 1
    for s in range(4):
        used = used | (oi[s, 0, 0, 0] == e)

    @pl.when(used & (loaded[0] == 0))
    def _():
        loaded[0] = 1
        for c in copies:
            c.wait()

    for s in range(4):

        @pl.when(oi[s, 0, 0, 0] == e)
        def _():
            for c in range(12):
                cols = slice(128 * c, 128 * (c + 1))
                for m in range(3):
                    ain_o[0, m, :, cols] += local_tile(late, 0, s, 12 * m + c)
                    ain_o[0, 3 + m, :, cols] += local_tile(early, 8, s, 12 * m + c)
                bres_o[0, 0, :, cols] += local_tile(early, 8, s, 36 + c)
                bres_o[0, 1, :, cols] += local_tile(late, 0, s, 52 + c)
            for c in range(16):
                bqkv_o[0, :, 128 * c : 128 * (c + 1)] += local_tile(late, 0, s, 36 + c)
            for piece in range(8):
                tile = 60 if piece == 7 else 35 * piece // 4
                for k in range(3):
                    for c in range(10):
                        cols = slice(128 * (tile + c), 128 * (tile + c + 1))
                        v = ff_tile(piece, s * 30 + k * 10 + c)
                        if k == 0:
                            aff_o[0, :, cols] += v
                        else:
                            bff_o[0, k - 1, :, cols] += v


def spread(oi, early, late):
    outs = (
        sds((ADAPT, 6, R, D), F32),
        sds((ADAPT, R, FF), F32),
        sds((ADAPT, R, 2048), F32),
        sds((ADAPT, 2, R, D), F32),
        sds((ADAPT, 2, R, FF), F32),
    )

    def one(shape):
        return pl.BlockSpec((1,) + shape[1:], lambda i: (lax.rem(i + 1, ADAPT),) + (0,) * (len(shape) - 1))

    return pl.pallas_call(
        spread_kernel,
        out_shape=outs,
        grid=(ADAPT,),
        in_specs=[SM, ANY, ANY],
        out_specs=[one(o.shape) for o in outs],
        scratch_shapes=[
            pltpu.VMEM(early.shape, BF),
            pltpu.VMEM(late.shape, BF),
            pltpu.SMEM((1,), jnp.int32),
            DMA((2,)),
        ],
        compiler_params=pltpu.CompilerParams(vmem_limit_bytes=VMEM_LIMIT),
    )(oi, early, late)


def local(
    tokens,
    cotangent,
    w_qkv,
    b_qkv,
    w_out,
    w_gu,
    w_down,
    gain_attn,
    gain_mlp,
    adapt_in,
    adapt_in_ff,
    adapt_out_qkv,
    adapt_out_res,
    adapt_out_ff,
    doc_lengths,
    adapter_index,
    window,
):
    member = lax.axis_index("ctx")
    starts = jnp.stack([member * BLK, (NBLK - 1 - member) * BLK])
    pos = (starts[:, None] + jnp.arange(BLK, dtype=jnp.int32)[None]).reshape(ROWS)
    freq = 1000000.0 ** (-(2.0 * jnp.arange(HS // 2, dtype=F32)) / HS)
    ang = pos.astype(F32)[:, None] * freq[None]
    c, sn = jnp.cos(ang), jnp.sin(ang)
    cos = jnp.concatenate([c, c], -1)
    sin = jnp.concatenate([-sn, sn], -1)

    (
        oq, oo, og, down, oe, oi, wins, p, xg, q, o, hid, n2,
        x, n1, eext, a45, bd, a3, bo, a012, bqkv,
    ) = front(
        adapter_index, doc_lengths, window, w_qkv, w_out, w_gu, w_down, tokens[0], cotangent[0],
        adapt_in, adapt_out_qkv, adapt_out_res, gain_attn, b_qkv, cos, sin, gain_mlp,
    )
    oq = oq.reshape(D, 2048)
    oo = oo.reshape(D, D)
    og = og.reshape(4, D, 640)
    out, gt, early, late = rear(
        xg, oe, og, down, adapt_in_ff, adapt_out_ff, eext, hid, n2, q, o, p, wins, oo, oq, x, n1,
        a012, a3, a45, bqkv, bo, bd, cos, sin, oi, gain_attn, gain_mlp,
    )
    return (out[None], gt[None]) + tuple(spread(oi, early, late))


def solution(mesh):
    return jax.shard_map(
        local,
        mesh=mesh,
        in_specs=(
            P("dp", "ctx", None, None),
            P("dp", "ctx", None, None),
            P(("dp", "ctx"), None),
            P(),
            P(("dp", "ctx"), None),
            P(("dp", "ctx"), None, None),
            P(("dp", "ctx"), None),
            P(),
            P(),
            P(),
            P(),
            P(),
            P(),
            P(),
            P("dp", None),
            P("dp"),
            P("dp"),
        ),
        out_specs=(P("dp", "ctx", None, None), P("dp", "ctx", None, None), P(), P(), P(), P(), P()),
        check_vma=False,
    )
```
